256 devices in a mesh: inst: 8 (over y_lo, x), space: 32 (over z, y_hi, core).
Axes of the slice: x: 4, y: 4 (y_hi: 2, y_lo: 2; y = y_hi * 2 + y_lo), z: 8, core: 2. Of those that a mesh axis runs over, the one named last changes fastest.
Arguments:
- fluid_init: float32 [48, 5, 256, 1024], P('inst', None, 'space'), may hold values from -6 to 6
- source_term: float32 [48, 5, 256, 1024], P('inst', None, 'space'), may hold values from -6 to 6
- pseudo_step: float32 [256, 1024], P('space'), may hold values from 0.05 to 0.15
- jacobian_x: float32 [5, 5], replicated, may hold values from -2.5 to 2.5
- jacobian_z: float32 [5, 5], replicated, may hold values from -2.5 to 2.5
- metal_init: float32 [2, 4, 256, 512], P(None, None, 'space'), may hold values from -6 to 6
- conductivity: float32 [256, 512], P('space'), may hold values from 0.2 to 1
- face_coeff: float32 [16384], P('space'), may hold values from 0.5 to 2
- fluid_face: int32 [16384], P('space'), may hold values from 0 to 8191
- metal_face: int32 [16384], P('space'), may hold values from 0 to 4095
Outputs:
- fluid_out: float32 [48, 5, 256, 1024], P('inst', None, 'space')
- metal_out: float32 [2, 4, 256, 512], P(None, None, 'space')
The draws below stay inside these ranges and needn't reach their ends.
All inputs are finite; a program needn't handle non-finite values.
Results may differ from the reference program's by a relative error of at most 0.0001.
Values sent between devices are 32-bit elements; how exact they have to be, the bound alone decides.
No kernel may reach another device: no remote copies, remote signals or barrier semaphores. Data moves between devices by JAX's collectives and lax.ppermute only.
A program may use at most 128 MiB of HBM per device.

```python
import math
import jax
import jax.numpy as jnp
from jax import lax

NT = 48
NV = 5
NH = 4
CX = 8
CZ = 1024
MZ = 512
NFACE = 512
SWEEPS = 2
NX = 256
FACES = 16384
N_SPACE = 32


def touch_ends(result, stream_key, least, largest):
    shape = result.shape
    index_at = [jax.random.randint(jax.random.fold_in(stream_key, axis), (), 0, shape[axis]) for axis in range(len(shape))]
    result = result.at[tuple(index_at)].set(least)
    longest = shape.index(max(shape))
    index_at[longest] = (index_at[longest] + 1) % shape[longest]
    return result.at[tuple(index_at)].set(largest)


def block_levels(rng, shape, pieces, smallest, top_value):
    def one(dim, blocks):
        heights = jax.random.uniform(jax.random.fold_in(jax.random.fold_in(rng, 6), dim), (blocks,), jnp.float32, smallest / len(pieces), top_value / len(pieces))
        return jnp.repeat(jnp.exp(heights), shape[dim] // blocks).reshape((-1,) + (1,) * (len(shape) - dim - 1))

    loudness = one(*pieces[0])
    for cut in pieces[1:]:
        loudness = loudness * one(*cut)
    return loudness


def scatter_about(stream_key, extent, spread, most, shards=(), kind=jnp.bfloat16):
    values = spread * jax.random.normal(stream_key, extent, jnp.float32)
    if shards:
        values = values * block_levels(stream_key, extent, shards, -0.22, 0.18)
    return jnp.clip(values, -most, most).astype(kind)


def setup_inputs(seed: int = 0) -> dict:
    key_list = jax.random.split(jax.random.key(seed), 11)
    fluid_init = scatter_about(key_list[0], (NT, NV, NX, CZ), 1.0, 6.0, ((0, 8), (2, 32)), jnp.float32)
    source_term = scatter_about(key_list[1], (NT, NV, NX, CZ), 1.0, 6.0, ((0, 8), (2, 32)), jnp.float32)
    pseudo_step = jnp.clip(jnp.exp(math.log(0.15) - 1.0986123 * jax.random.uniform(key_list[2], (NX, CZ), jnp.float32) ** block_levels(key_list[2], (NX, CZ), ((0, 32),), -0.2, 0.2)), 0.05, 0.15)
    jacobian_x = scatter_about(key_list[3], (NV, NV), NV ** -0.5, 2.5, (), jnp.float32)
    jacobian_z = scatter_about(key_list[4], (NV, NV), NV ** -0.5, 2.5, (), jnp.float32)
    metal_init = scatter_about(key_list[5], (2, NH, NX, MZ), 1.0, 6.0, ((2, 32),), jnp.float32)
    conductivity = jnp.clip(jnp.exp(math.log(1.0) - 1.609438 * jax.random.uniform(key_list[6], (NX, MZ), jnp.float32) ** block_levels(key_list[6], (NX, MZ), ((0, 32),), -0.2, 0.2)), 0.2, 1.0)
    face_coeff = jnp.clip(0.5 + 1.5 * jax.random.uniform(key_list[7], (FACES,), jnp.float32) ** block_levels(key_list[7], (FACES,), ((0, 32),), -0.2, 0.2), 0.5, 2.0)
    fluid_face = touch_ends(jax.random.randint(key_list[8], (FACES,), 0, CX * CZ), jax.random.fold_in(key_list[8], 1), 0, (CX * CZ) - 1).astype(jnp.int32)
    metal_face = touch_ends(jax.random.randint(key_list[9], (FACES,), 0, CX * MZ), jax.random.fold_in(key_list[9], 1), 0, (CX * MZ) - 1).astype(jnp.int32)
    return dict(fluid_init=fluid_init, source_term=source_term, pseudo_step=pseudo_step, jacobian_x=jacobian_x, jacobian_z=jacobian_z, metal_init=metal_init, conductivity=conductivity, face_coeff=face_coeff, fluid_face=fluid_face, metal_face=metal_face)


damping_fourth = 1.0 / 32.0
viscous_coef = 0.1
omega_base = 1.0
sigma_fluid = 0.5
metal_step = 0.2
sigma_metal = 0.5
heat_capacity = 0.5
flux_scale = 4.0
highest = lax.Precision.HIGHEST


def spectral_matrix(instances):
    position = jnp.arange(instances, dtype=jnp.int32)
    offset = position[:, None] - position[None, :]
    parity = 1.0 - 2.0 * (offset % 2).astype(jnp.float32)
    angle_value = math.pi * offset.astype(jnp.float32) / instances
    safe_angle = jnp.where(offset == 0, 0.5, angle_value)
    entries = 0.5 * parity * jnp.cos(safe_angle) / jnp.sin(safe_angle)
    return jnp.where(offset == 0, 0.0, entries).astype(jnp.float32)


def harmonic_tables(instance_ids, instances):
    harmonic = jnp.arange(NH, dtype=jnp.int32)
    phase_angle = 2.0 * math.pi * ((harmonic[:, None] * instance_ids[None, :]) % instances).astype(jnp.float32) / instances
    return jnp.cos(phase_angle), jnp.sin(phase_angle)


def fluid_update(adjoint, east_one, west_one, east_two, west_two, derivative, source_term, pseudo_step, jacobian_x, jacobian_z, energy):
    north_side = jnp.pad(adjoint[..., 1:], ((0, 0), (0, 0), (0, 0), (0, 1)))
    south_side = jnp.pad(adjoint[..., :-1], ((0, 0), (0, 0), (0, 0), (1, 0)))
    central_x = 0.5 * (east_one - west_one)
    fourth = east_two - 4.0 * east_one + 6.0 * adjoint - 4.0 * west_one + west_two
    central_z = 0.5 * (north_side - south_side)
    second_z = north_side - 2.0 * adjoint + south_side
    convect = jnp.einsum('uv,tvxz->tuxz', jacobian_x, central_x, precision=highest)
    convect = convect + jnp.einsum('uv,tvxz->tuxz', jacobian_z, central_z, precision=highest)
    residual = source_term - convect - damping_fourth * fourth + viscous_coef * second_z - omega_base * derivative - sigma_fluid * adjoint
    residual = residual.at[:, adjoint.shape[1] - 1].add(energy)
    return adjoint + pseudo_step[None, None] * residual


def metal_update(metal_state, east_side, west_side, conductivity, heat_source):
    north_side = jnp.pad(metal_state[..., 1:], ((0, 0), (0, 0), (0, 0), (0, 1)))
    south_side = jnp.pad(metal_state[..., :-1], ((0, 0), (0, 0), (0, 0), (1, 0)))
    laplace = east_side + west_side + north_side + south_side - 4.0 * metal_state
    harmonic = jnp.arange(metal_state.shape[1], dtype=jnp.float32)[:, None, None]
    rotate = jnp.stack([-heat_capacity * harmonic * metal_state[1], heat_capacity * harmonic * metal_state[0]])
    change = heat_source + conductivity[None, None] * laplace - sigma_metal * metal_state - rotate
    return metal_state + metal_step * change


def reference(fluid_init, source_term, pseudo_step, jacobian_x, jacobian_z, metal_init, conductivity, face_coeff, fluid_face, metal_face):
    rows_all = CX * N_SPACE
    block_row = ((jnp.arange(N_SPACE * NFACE, dtype=jnp.int32) // NFACE) * CX).astype(jnp.int32)
    fluid_global = ((block_row + fluid_face // CZ) * CZ + fluid_face % CZ).astype(jnp.int32)
    metal_global = ((block_row + metal_face // MZ) * MZ + metal_face % MZ).astype(jnp.int32)
    spectral = spectral_matrix(NT)
    cosine_table, sine_table = harmonic_tables(jnp.arange(NT, dtype=jnp.int32), NT)
    adjoint = fluid_init
    metal_state = metal_init
    for sweep_index in range(SWEEPS):
        at_faces = metal_state.reshape(2, NH, rows_all * MZ)[:, :, metal_global]
        synthesis = jnp.dot(cosine_table.T, at_faces[0], precision=highest) - jnp.dot(sine_table.T, at_faces[1], precision=highest)
        synthesis = synthesis * face_coeff[None]
        energy = jnp.zeros((NT, rows_all * CZ), jnp.float32).at[:, fluid_global].add(synthesis).reshape(NT, rows_all, CZ)
        derivative = jnp.einsum('ts,svxz->tvxz', spectral, adjoint, precision=highest)
        adjoint = fluid_update(adjoint, jnp.roll(adjoint, -1, 2), jnp.roll(adjoint, 1, 2), jnp.roll(adjoint, -2, 2), jnp.roll(adjoint, 2, 2), derivative, source_term, pseudo_step, jacobian_x, jacobian_z, energy)
        face_flux = adjoint[:, NV - 1].reshape(NT, rows_all * CZ)[:, fluid_global] * face_coeff[None]
        heat_terms = jnp.stack([jnp.dot(cosine_table, face_flux, precision=highest), -jnp.dot(sine_table, face_flux, precision=highest)]) * (flux_scale / NT)
        heat_source = jnp.zeros((2, NH, rows_all * MZ), jnp.float32).at[:, :, metal_global].add(heat_terms).reshape(2, NH, rows_all, MZ)
        metal_state = metal_update(metal_state, jnp.roll(metal_state, -1, 2), jnp.roll(metal_state, 1, 2), conductivity, heat_source)
    return adjoint, metal_state
```

```python
import functools
import math

import jax
import jax.numpy as jnp
import ml_dtypes
import numpy as np
from jax import lax
from jax.experimental import pallas as pl
from jax.experimental.pallas import tpu as pltpu
from jax.sharding import PartitionSpec as P

NT, NV, NH = 48, 5, 4
ROWS, SPAN, MSPAN, NF = 8, 1024, 512, 512
CHUNK = 128
CH = 2 * NH
F32, BF16 = jnp.float32, jnp.bfloat16
VMEM = pl.BlockSpec(memory_space=pltpu.VMEM)
SMEM = pl.BlockSpec(memory_space=pltpu.SMEM)

damping_fourth = 1.0 / 32.0
viscous_coef = 0.1
sigma_fluid = 0.5
metal_step = 0.2
sigma_metal = 0.5
heat_capacity = 0.5
flux_scale = 4.0


def tables():
    t = np.arange(NT)
    offset = t[:, None] - t[None, :]
    angle = np.where(offset == 0, 0.5, math.pi * offset / NT)
    spectral = np.where(
        offset == 0, 0.0, 0.5 * (1.0 - 2.0 * (offset % 2)) * np.cos(angle) / np.sin(angle)
    )
    phase = 2.0 * math.pi * ((np.arange(NH)[:, None] * t[None, :]) % NT) / NT
    synth = np.concatenate([np.cos(phase), -np.sin(phase)])
    w0 = synth * (flux_scale / NT)
    w1 = w0 @ spectral
    w2 = w1 @ spectral
    high = spectral.astype(np.float32).astype(ml_dtypes.bfloat16)
    low = (spectral - high.astype(np.float64)).astype(np.float32).astype(ml_dtypes.bfloat16)
    eye = np.eye(ROWS, dtype=np.float32)
    kron_high = np.kron(high.astype(np.float32), eye)
    kron_low = np.kron(low.astype(np.float32), eye)
    kron = np.concatenate([kron_high, kron_high, kron_low], axis=1).astype(ml_dtypes.bfloat16)
    flat = np.concatenate([m.T.reshape(-1) for m in (synth, w0, w1, w2)]).astype(np.float32)
    return kron, flat


KRON, FLAT = tables()
SYNTH, W0, W1, W2 = (i * NT * CH for i in range(4))


def call(body, outs, n_in, smem=(), scratch=(), flops=1 << 20, moved=1 << 21):
    return pl.pallas_call(
        body,
        out_shape=outs,
        in_specs=[SMEM if i in smem else VMEM for i in range(n_in)],
        out_specs=[VMEM] * len(outs),
        scratch_shapes=list(scratch),
        compiler_params=pltpu.CompilerParams(vmem_limit_bytes=24 << 20),
        cost_estimate=pl.CostEstimate(flops=flops, bytes_accessed=moved, transcendentals=0),
    )


def shape(*dims):
    return jax.ShapeDtypeStruct(dims, F32)


def row_index(n=SPAN):
    return lax.broadcasted_iota(jnp.int32, (ROWS, n), 0)


def split(x):
    high = x.astype(BF16)
    return high, (x - high.astype(F32)).astype(BF16)


def one_hot(index, n):
    cell = lax.broadcasted_iota(jnp.int32, (n, NF), 0)
    return jnp.where(cell == index, 1.0, 0.0).astype(BF16)


def at_faces(field, span_hot, row_hot):
    n = field.shape[-1]
    both = jnp.concatenate(split(field.reshape(CH * ROWS, n)), axis=0)
    picked = jnp.dot(both, span_hot, preferred_element_type=F32)
    picked = (picked[: CH * ROWS] + picked[CH * ROWS :]).reshape(CH, ROWS, NF)
    return jnp.sum(picked * row_hot[None], axis=1)


def onto_cells(values, span_hot, row_hot):
    spread = (values[:, None, :] * row_hot[None]).reshape(CH * ROWS, NF)
    both = jnp.concatenate(split(spread), axis=0)
    out = lax.dot_general(both, span_hot, (((1,), (1,)), ((), ())), preferred_element_type=F32)
    return (out[: CH * ROWS] + out[CH * ROWS :]).reshape(CH, ROWS, span_hot.shape[0])


def fluid_hots(ff_ref):
    cell = ff_ref[...]
    span = one_hot(cell & (SPAN - 1), SPAN)
    rows = jnp.where(row_index(NF) == (cell >> 10), 1.0, 0.0)
    return span, rows


def metal_hots(mf_ref):
    cell = mf_ref[...]
    span = one_hot(cell & (MSPAN - 1), MSPAN)
    rows = jnp.where(row_index(NF) == (cell >> 9), 1.0, 0.0)
    return span, rows


def span_sides(a):
    n = a.shape[-1]
    lane = lax.broadcasted_iota(jnp.int32, a.shape, a.ndim - 1)
    north = jnp.where(lane == n - 1, 0.0, pltpu.roll(a, n - 1, a.ndim - 1))
    south = jnp.where(lane == 0, 0.0, pltpu.roll(a, 1, a.ndim - 1))
    return north, south


def stencil_parts(a, before, after):
    row = row_index(a.shape[-1])
    east_one = pltpu.roll(jnp.where(row == 0, after, a), 7, 0)
    east_two = pltpu.roll(jnp.where(row < 2, after, a), 6, 0)
    west_one = pltpu.roll(jnp.where(row == 7, before, a), 1, 0)
    west_two = pltpu.roll(jnp.where(row >= 6, before, a), 2, 0)
    north, south = span_sides(a)
    rest = (
        (4.0 * damping_fourth) * (east_one + west_one)
        - damping_fourth * (east_two + west_two)
        + viscous_coef * (north + south)
        - (6.0 * damping_fourth + 2.0 * viscous_coef + sigma_fluid) * a
    )
    return east_one - west_one, north - south, rest


def halo_pair(up_ref, down_ref, t, v):
    if v < 4:
        tile, slot = t, v
        before = pltpu.roll(up_ref[tile], (6 - 2 * slot) % 8, 0)
        after = pltpu.roll(down_ref[tile], (8 - 2 * slot) % 8, 0)
        return before, after
    tile, slot = 6 + t // 4, t % 4
    before = pltpu.roll(up_ref[tile], (6 - 2 * slot) % 8, 0)
    after = pltpu.roll(down_ref[tile], (8 - 2 * slot) % 8, 0)
    return before, after


def pack_edges(get, up_ref, down_ref, extra):
    row = row_index()
    groups = [[get(t, v) for v in range(4)] for t in range(6)]
    groups += [[get(t, 4) for t in range(4)], [get(4, 4), get(5, 4), extra, extra]]
    for tile, blocks in enumerate(groups):
        up = down = None
        for slot, a in enumerate(blocks):
            u = pltpu.roll(a, (2 * slot + 2) % 8, 0) if (2 * slot + 2) % 8 else a
            d = pltpu.roll(a, 2 * slot, 0) if slot else a
            mine = (row >> 1) == slot
            up = u if up is None else jnp.where(mine, u, up)
            down = d if down is None else jnp.where(mine, d, down)
        up_ref[tile] = up
        down_ref[tile] = down


def edges_kernel(a_ref, ps_ref, up_ref, down_ref):
    pack_edges(lambda t, v: a_ref[t, v], up_ref, down_ref, ps_ref[...])


def blocks_kernel(a_ref, out_ref):
    for i in range(8):
        for t in range(6):
            for v in range(NV):
                out_ref[i, t * NV + v] = a_ref[t, v, :, i * CHUNK : (i + 1) * CHUNK]


def energy_kernel(tab_ref, m_ref, fc_ref, ff_ref, mf_ref, e_ref):
    first = lax.axis_index("inst") * 6
    m_hot, m_row = metal_hots(mf_ref)
    f_hot, f_row = fluid_hots(ff_ref)
    values = at_faces(m_ref[...], m_hot, m_row) * fc_ref[...]
    cells = onto_cells(values, f_hot, f_row)
    for t in range(6):
        e_ref[t] = combine(tab_ref, SYNTH, first + t, cells)


def combine(tab_ref, base, t, fields):
    total = tab_ref[base + t * CH] * fields[0]
    for ch in range(1, CH):
        if ch != NH:
            total += tab_ref[base + t * CH + ch] * fields[ch]
    return total


def convect(jx_ref, jz_ref, dx, dz, rest, u):
    out = rest
    for v in range(NV):
        out = out - (0.5 * jx_ref[u, v]) * dx[v] - (0.5 * jz_ref[u, v]) * dz[v]
    return out


def first_kernel(
    tab_ref, jx_ref, jz_ref, a_ref, s_ref, ps_ref, up_ref, down_ref, e_ref, fc_ref, ff_ref,
    q_ref, b_ref, bup_ref, bdown_ref, hq_ref,
    parts,
):
    first = lax.axis_index("inst") * 6
    step = ps_ref[...]
    step_before = pltpu.roll(up_ref[7], 2, 0)
    step_after = pltpu.roll(down_ref[7], 4, 0)
    for t in range(6):
        for v in range(NV):
            a = a_ref[t, v]
            before, after = halo_pair(up_ref, down_ref, t, v)
            dx, dz, rest = stencil_parts(a, before, after)
            parts[0, v], parts[1, v], parts[2, v] = dx, dz, rest
            dx, dz, rest = stencil_parts(step * a, step_before * before, step_after * after)
            parts[3, v], parts[4, v], parts[5, v] = dx, dz, rest
        for i in range(8):
            cut = pl.ds(i * CHUNK, CHUNK)
            dx = [parts[0, v, :, cut] for v in range(NV)]
            dz = [parts[1, v, :, cut] for v in range(NV)]
            px = [parts[3, v, :, cut] for v in range(NV)]
            pz = [parts[4, v, :, cut] for v in range(NV)]
            for u in range(NV):
                a = a_ref[t, u, :, cut]
                space = convect(jx_ref, jz_ref, dx, dz, parts[2, u, :, cut], u)
                source = s_ref[t, u, :, cut] + space
                if u == NV - 1:
                    source = source + e_ref[t, :, cut]
                b = a + ps_ref[:, cut] * source
                b_ref[t, u, :, cut] = b
                q_ref[i, t * NV + u] = a + b + convect(jx_ref, jz_ref, px, pz, parts[5, u, :, cut], u)
    pack_edges(lambda t, v: b_ref[t, v], bup_ref, bdown_ref, step)
    f_hot, f_row = fluid_hots(ff_ref)
    heat = []
    for ch in range(CH):
        h0 = h1 = h2 = h3 = None
        for t in range(6):
            at = (first + t) * CH + ch
            q = jnp.concatenate([q_ref[i, t * NV + NV - 1] for i in range(8)], axis=1)
            a, b = a_ref[t, NV - 1], b_ref[t, NV - 1]
            x0 = tab_ref[W0 + at] * b
            x1 = tab_ref[W1 + at] * a
            x2 = tab_ref[W1 + at] * q
            x3 = tab_ref[W2 + at] * a
            h0, h1, h2, h3 = (
                (x0, x1, x2, x3) if t == 0 else (h0 + x0, h1 + x1, h2 + x2, h3 + x3)
            )
        heat.append(h0 - step * h1)
        hq_ref[ch] = step * (step * h3 - h2)
    values = at_faces(jnp.stack(heat), f_hot, f_row) * fc_ref[...]
    for i in range(8):
        for k in range(4):
            q_ref[i, 30 + k] = values[:, k * CHUNK : (k + 1) * CHUNK]


def rotate_time(kron_ref, x):
    high, low = split(x)
    return jnp.dot(
        kron_ref[...], jnp.concatenate([high, low, high], axis=0), preferred_element_type=F32
    )


def local_step(ps_ref):
    start = pl.multiple_of(lax.axis_index("inst") * CHUNK, CHUNK)
    return ps_ref[:, pl.ds(start, CHUNK)]


def turned(ref):
    return jnp.concatenate(
        [
            jnp.concatenate(
                [ref[j, t * NV + v] for j in range(8) for t in range(6)], axis=0
            )
            for v in range(NV)
        ],
        axis=1,
    )


def derive_kernel(kron_ref, a_ref, ps_ref, g_ref):
    step = local_step(ps_ref)
    wide = jnp.concatenate([step] * NV, axis=1)
    d = rotate_time(kron_ref, turned(a_ref))
    g_ref[...] = (d.reshape(NT, ROWS, NV * CHUNK) * wide[None]).reshape(NT * ROWS, NV * CHUNK)


def middle_kernel(jx_ref, jz_ref, tab_ref, b_ref, s_ref, ps_ref, up_ref, down_ref, hq_ref, c_ref, hc_ref, parts):
    first = lax.axis_index("inst") * 6
    for t in range(6):
        for v in range(NV):
            before, after = halo_pair(up_ref, down_ref, t, v)
            dx, dz, rest = stencil_parts(b_ref[t, v], before, after)
            parts[0, v], parts[1, v], parts[2, v] = dx, dz, rest
        for i in range(8):
            cut = pl.ds(i * CHUNK, CHUNK)
            dx = [parts[0, v, :, cut] for v in range(NV)]
            dz = [parts[1, v, :, cut] for v in range(NV)]
            for u in range(NV):
                space = convect(jx_ref, jz_ref, dx, dz, parts[2, u, :, cut], u)
                c_ref[t, u, :, cut] = b_ref[t, u, :, cut] + ps_ref[:, cut] * (s_ref[t, u, :, cut] + space)
    for ch in range(CH):
        total = hq_ref[ch]
        for t in range(6):
            total += tab_ref[W0 + (first + t) * CH + ch] * c_ref[t, NV - 1]
        hc_ref[ch] = total


def metal_update(m, before, after, cond, heat):
    row = row_index(MSPAN)
    out = []
    for ch in range(CH):
        a = m[ch]
        east = pltpu.roll(jnp.where(row == 0, after[ch], a), 7, 0)
        west = pltpu.roll(jnp.where(row == 7, before[ch], a), 1, 0)
        north, south = span_sides(a)
        laplace = east + west + north + south - 4.0 * a
        h = ch % NH
        turn = -heat_capacity * h * m[ch + NH] if ch < NH else heat_capacity * h * m[ch - NH]
        out.append(a + metal_step * (heat[ch] + cond * laplace - sigma_metal * a - turn))
    return out


def metal_edges(m, up_ref, down_ref):
    up_ref[...] = jnp.concatenate([m[ch][7:8] for ch in range(CH)], axis=0)
    down_ref[...] = jnp.concatenate([m[ch][0:1] for ch in range(CH)], axis=0)


def metal_sides(up_ref, down_ref):
    before = [jnp.broadcast_to(up_ref[ch : ch + 1], (ROWS, MSPAN)) for ch in range(CH)]
    after = [jnp.broadcast_to(down_ref[ch : ch + 1], (ROWS, MSPAN)) for ch in range(CH)]
    return before, after


def heat_sum(blocks_ref, lead):
    tiles = []
    for k in range(4):
        total = blocks_ref[0, lead + k]
        for j in range(1, 8):
            total += blocks_ref[j, lead + k]
        tiles.append(total)
    return jnp.concatenate(tiles, axis=1)


def second_kernel(
    kron_ref, tab_ref, q_ref, g_ref, ps_ref, m_ref, mup_ref, mdown_ref, cond_ref, fc_ref, ff_ref, mf_ref, hc_ref,
    v_ref, m_out, mup_out, mdown_out, e_ref,
):
    first = lax.axis_index("inst") * 6
    step = ps_ref[...]
    coeff = fc_ref[...]
    m_hot, m_row = metal_hots(mf_ref)
    f_hot, f_row = fluid_hots(ff_ref)
    source = onto_cells(heat_sum(q_ref, 30), m_hot, m_row)
    before, after = metal_sides(mup_ref, mdown_ref)
    m = metal_update(m_ref[...], before, after, cond_ref[...], source)
    for ch in range(CH):
        m_out[ch] = m[ch]
    metal_edges(m, mup_out, mdown_out)
    cells = onto_cells(at_faces(jnp.stack(m), m_hot, m_row) * coeff, f_hot, f_row)
    for t in range(6):
        e_ref[t] = step * combine(tab_ref, SYNTH, first + t, cells)
    heat = []
    for ch in range(CH):
        total = hc_ref[ch]
        for t in range(6):
            total += tab_ref[W0 + (first + t) * CH + ch] * e_ref[t]
        heat.append(total)
    values = at_faces(jnp.stack(heat), f_hot, f_row) * coeff
    for i in range(8):
        for k in range(4):
            v_ref[i, 30 + k] = values[:, k * CHUNK : (k + 1) * CHUNK]
    d = rotate_time(kron_ref, turned(q_ref) - g_ref[...])
    minus = -local_step(ps_ref)
    for j in range(8):
        for t in range(6):
            at = (j * 6 + t) * ROWS
            for v in range(NV):
                v_ref[j, t * NV + v] = minus * d[at : at + ROWS, v * CHUNK : (v + 1) * CHUNK]


def last_kernel(v_ref, c_ref, e_ref, m_ref, mup_ref, mdown_ref, cond_ref, mf_ref, out_ref, m_out):
    for i in range(8):
        cut = pl.ds(i * CHUNK, CHUNK)
        for t in range(6):
            for v in range(NV):
                total = c_ref[t, v, :, cut] + v_ref[i, t * NV + v]
                if v == NV - 1:
                    total = total + e_ref[t, :, cut]
                out_ref[t, v, :, cut] = total
    m_hot, m_row = metal_hots(mf_ref)
    source = onto_cells(heat_sum(v_ref, 30), m_hot, m_row)
    before, after = metal_sides(mup_ref, mdown_ref)
    m = metal_update(m_ref[...], before, after, cond_ref[...], source)
    for ch in range(CH):
        m_out[ch] = m[ch]


def exchange(up, down):
    n = lax.axis_size("space")
    forward = [(i, (i + 1) % n) for i in range(n)]
    back = [(j, i) for i, j in forward]
    return lax.ppermute(up, "space", forward), lax.ppermute(down, "space", back)


def turn(x):
    return lax.all_to_all(x, "inst", 0, 0, tiled=True)


def local(a0, source, ps, jx, jz, metal, cond, coeff, ff, mf):
    kron = jnp.asarray(KRON)
    tab = jnp.asarray(FLAT)
    coeff, ff, mf = (x.reshape(1, NF) for x in (coeff, ff, mf))
    metal = metal.reshape(CH, ROWS, MSPAN)
    up, down = call(edges_kernel, [shape(8, ROWS, SPAN)] * 2, 2)(a0, ps)
    up, down = exchange(up, down)
    (blocks,) = call(blocks_kernel, [shape(8, 30, ROWS, CHUNK)], 1)(a0)
    a_turned = turn(blocks)
    mup, mdown = exchange(metal[:, ROWS - 1], metal[:, 0])
    (e0,) = call(energy_kernel, [shape(6, ROWS, SPAN)], 5, smem=(0,))(tab, metal, coeff, ff, mf)
    parts = pltpu.VMEM((6, NV, ROWS, SPAN), F32)
    q, b, bup, bdown, hq = call(
        first_kernel,
        [shape(8, 34, ROWS, CHUNK), shape(6, NV, ROWS, SPAN)] + [shape(8, ROWS, SPAN)] * 3,
        11,
        smem=(0, 1, 2),
        scratch=[parts],
    )(tab, jx, jz, a0, source, ps, up, down, e0, coeff, ff)
    q_turned = turn(q)
    bup, bdown = exchange(bup, bdown)
    (g,) = call(derive_kernel, [shape(NT * ROWS, NV * CHUNK)], 3)(kron, a_turned, ps)
    c, hc = call(
        middle_kernel,
        [shape(6, NV, ROWS, SPAN), shape(CH, ROWS, SPAN)],
        9,
        smem=(0, 1, 2),
        scratch=[pltpu.VMEM((3, NV, ROWS, SPAN), F32)],
    )(jx, jz, tab, b, source, ps, bup, bdown, hq)
    v, metal, mup, mdown, e1 = call(
        second_kernel,
        [shape(8, 34, ROWS, CHUNK), shape(CH, ROWS, MSPAN)]
        + [shape(CH, MSPAN)] * 2
        + [shape(6, ROWS, SPAN)],
        13,
        smem=(1,),
    )(kron, tab, q_turned, g, ps, metal, mup, mdown, cond, coeff, ff, mf, hc)
    v = turn(v)
    mup, mdown = exchange(mup, mdown)
    out, metal = call(
        last_kernel, [shape(6, NV, ROWS, SPAN), shape(CH, ROWS, MSPAN)], 8
    )(v, c, e1, metal, mup, mdown, cond, mf)
    return out, metal.reshape(2, NH, ROWS, MSPAN)


def solution(mesh):
    return jax.shard_map(
        local,
        mesh=mesh,
        in_specs=(
            P("inst", None, "space", None),
            P("inst", None, "space", None),
            P("space", None),
            P(),
            P(),
            P(None, None, "space", None),
            P("space", None),
            P("space"),
            P("space"),
            P("space"),
        ),
        out_specs=(P("inst", None, "space", None), P(None, None, "space", None)),
        check_vma=False,
    )
```

```python
import math

import jax
import jax.numpy as jnp
import ml_dtypes
import numpy as np
from jax import lax
from jax.experimental import pallas as pl
from jax.experimental.pallas import tpu as pltpu
from jax.sharding import PartitionSpec as P

NT, NV, NH = 48, 5, 4
ROWS, SPAN, MSPAN, NF = 8, 1024, 512, 512
CHUNK = 128
CH = 2 * NH
F32, BF16 = jnp.float32, jnp.bfloat16

damping_fourth = 1.0 / 32.0
viscous_coef = 0.1
sigma_fluid = 0.5
metal_step = 0.2
sigma_metal = 0.5
heat_capacity = 0.5
flux_scale = 4.0


def tables():
    t = np.arange(NT)
    offset = t[:, None] - t[None, :]
    angle = np.where(offset == 0, 0.5, math.pi * offset / NT)
    spectral = np.where(
        offset == 0, 0.0, 0.5 * (1.0 - 2.0 * (offset % 2)) * np.cos(angle) / np.sin(angle)
    )
    phase = 2.0 * math.pi * ((np.arange(NH)[:, None] * t[None, :]) % NT) / NT
    synth = np.concatenate([np.cos(phase), -np.sin(phase)])
    w0 = synth * (flux_scale / NT)
    w1 = w0 @ spectral
    w2 = w1 @ spectral
    high = spectral.astype(np.float32).astype(ml_dtypes.bfloat16)
    low = (spectral - high.astype(np.float64)).astype(np.float32).astype(ml_dtypes.bfloat16)
    eye = np.eye(ROWS, dtype=np.float32)
    kron_high = np.kron(high.astype(np.float32), eye)
    kron_low = np.kron(low.astype(np.float32), eye)
    kron = np.concatenate([kron_high, kron_high, kron_low], axis=1).astype(ml_dtypes.bfloat16)
    flat = np.concatenate([m.T.reshape(-1) for m in (synth, w0, w1, w2)]).astype(np.float32)
    return kron, flat


KRON, FLAT = tables()
SYNTH, W0, W1, W2 = (i * NT * CH for i in range(4))


class Loaded:
    def __init__(self, source, buffer, sems, cut):
        self.buffer, self.copies = buffer, []
        for i, index in enumerate(cut):
            self.copies.append(pltpu.make_async_copy(source.at[index], buffer.at[index], sems.at[i]))
        self.waiting = set(range(len(cut)))

    def start(self, i):
        self.copies[i].start()

    def piece(self, i):
        if i in self.waiting:
            self.waiting.remove(i)
            self.copies[i].wait()
        return self.buffer

    def whole(self):
        for i in range(len(self.copies)):
            self.piece(i)
        return self.buffer


class Stored:
    def __init__(self, target, buffer, sems):
        self.target, self.buffer, self.sems, self.copies = target, buffer, sems, []

    def put(self, index):
        copy = pltpu.make_async_copy(
            self.buffer.at[index], self.target.at[index], self.sems.at[len(self.copies)]
        )
        copy.start()
        self.copies.append(copy)

    def finish(self):
        for copy in self.copies:
            copy.wait()


WHOLE = (slice(None),)


def by_piece(n):
    return tuple(pl.ds(i, 1) for i in range(n))


def call(body, operands, results, scratch=(), flops=1 << 22, moved=1 << 22):
    space = {"smem": pltpu.SMEM, "vmem": pltpu.VMEM}
    modes = [mode for _, mode in operands]
    here = [isinstance(mode, str) for mode in modes]
    in_specs = [
        pl.BlockSpec(memory_space=space[m] if h else pltpu.HBM) for m, h in zip(modes, here)
    ]
    out_specs = [pl.BlockSpec(memory_space=pltpu.HBM if n else pltpu.VMEM) for _, n in results]
    buffers = []
    for array, mode in operands:
        if not isinstance(mode, str):
            buffers += [pltpu.VMEM(array.shape, array.dtype), pltpu.SemaphoreType.DMA((len(mode),))]
    for dims, n in results:
        if n > 0:
            buffers += [pltpu.VMEM(dims, F32), pltpu.SemaphoreType.DMA((n,))]

    def kernel(*refs):
        ins, refs = refs[: len(modes)], refs[len(modes) :]
        outs, refs = refs[: len(results)], list(refs[len(results) :])
        args, loads = [], []
        for ref, mode, h in zip(ins, modes, here):
            if h:
                args.append(ref)
            else:
                args.append(Loaded(ref, refs.pop(0), refs.pop(0), mode))
                loads.append(args[-1])
        for i in range(max([len(x.copies) for x in loads], default=0)):
            for x in loads:
                if i < len(x.copies):
                    x.start(i)
        stores = []
        for ref, (_, n) in zip(outs, results):
            if n > 0:
                args.append(Stored(ref, refs.pop(0), refs.pop(0)))
                stores.append(args[-1])
            else:
                args.append(ref)
        body(*args, *refs)
        for x in loads:
            x.whole()
        for x in stores:
            x.finish()

    return pl.pallas_call(
        kernel,
        out_shape=[pltpu.HBM(dims, F32) if n else shape(*dims) for dims, n in results],
        in_specs=in_specs,
        out_specs=out_specs,
        scratch_shapes=buffers + list(scratch),
        compiler_params=pltpu.CompilerParams(vmem_limit_bytes=24 << 20),
        cost_estimate=pl.CostEstimate(flops=flops, bytes_accessed=moved, transcendentals=0),
    )(
        *[a if h else pltpu.with_memory_space_constraint(a, pltpu.HBM) for (a, _), h in zip(operands, here)]
    )


def shape(*dims):
    return jax.ShapeDtypeStruct(dims, F32)


def row_index(n=SPAN):
    return lax.broadcasted_iota(jnp.int32, (ROWS, n), 0)


def split(x):
    high = x.astype(BF16)
    return high, (x - high.astype(F32)).astype(BF16)


def one_hot(index, n):
    cell = lax.broadcasted_iota(jnp.int32, (n, NF), 0)
    return jnp.where(cell == index, 1.0, 0.0).astype(BF16)


def at_faces(field, span_hot, row_hot):
    n = field.shape[-1]
    both = jnp.concatenate(split(field.reshape(CH * ROWS, n)), axis=0)
    picked = jnp.dot(both, span_hot, preferred_element_type=F32)
    picked = (picked[: CH * ROWS] + picked[CH * ROWS :]).reshape(CH, ROWS, NF)
    return jnp.sum(picked * row_hot[None], axis=1)


def onto_cells(values, span_hot, row_hot):
    spread = (values[:, None, :] * row_hot[None]).reshape(CH * ROWS, NF)
    both = jnp.concatenate(split(spread), axis=0)
    out = lax.dot_general(both, span_hot, (((1,), (1,)), ((), ())), preferred_element_type=F32)
    return (out[: CH * ROWS] + out[CH * ROWS :]).reshape(CH, ROWS, span_hot.shape[0])


def fluid_hots(ff_ref):
    cell = ff_ref[...]
    span = one_hot(cell & (SPAN - 1), SPAN)
    rows = jnp.where(row_index(NF) == (cell >> 10), 1.0, 0.0)
    return span, rows


def metal_hots(mf_ref):
    cell = mf_ref[...]
    span = one_hot(cell & (MSPAN - 1), MSPAN)
    rows = jnp.where(row_index(NF) == (cell >> 9), 1.0, 0.0)
    return span, rows


def span_sides(a):
    n = a.shape[-1]
    lane = lax.broadcasted_iota(jnp.int32, a.shape, a.ndim - 1)
    north = jnp.where(lane == n - 1, 0.0, pltpu.roll(a, n - 1, a.ndim - 1))
    south = jnp.where(lane == 0, 0.0, pltpu.roll(a, 1, a.ndim - 1))
    return north, south


def stencil_parts(a, before, after):
    row = row_index(a.shape[-1])
    east_one = pltpu.roll(jnp.where(row == 0, after, a), 7, 0)
    east_two = pltpu.roll(jnp.where(row < 2, after, a), 6, 0)
    west_one = pltpu.roll(jnp.where(row == 7, before, a), 1, 0)
    west_two = pltpu.roll(jnp.where(row >= 6, before, a), 2, 0)
    north, south = span_sides(a)
    rest = (
        (4.0 * damping_fourth) * (east_one + west_one)
        - damping_fourth * (east_two + west_two)
        + viscous_coef * (north + south)
        - (6.0 * damping_fourth + 2.0 * viscous_coef + sigma_fluid) * a
    )
    return east_one - west_one, north - south, rest


def edge_tile(ref, tile):
    return jnp.concatenate([ref[2 * tile], ref[2 * tile + 1]], axis=1)


def halo_pair(up_ref, down_ref, t, v):
    tile, slot = (t, v) if v < 4 else (6 + t // 4, t % 4)
    before = pltpu.roll(edge_tile(up_ref, tile), (6 - 2 * slot) % 8, 0)
    after = pltpu.roll(edge_tile(down_ref, tile), (8 - 2 * slot) % 8, 0)
    return before, after


def pack_tile(blocks, tile, up_ref, down_ref):
    row = row_index()
    up = down = None
    for slot, a in enumerate(blocks):
        u = pltpu.roll(a, (2 * slot + 2) % 8, 0) if (2 * slot + 2) % 8 else a
        d = pltpu.roll(a, 2 * slot, 0) if slot else a
        mine = (row >> 1) == slot
        up = u if up is None else jnp.where(mine, u, up)
        down = d if down is None else jnp.where(mine, d, down)
    for half in range(2):
        cut = slice(half * 512, half * 512 + 512)
        up_ref[2 * tile + half] = up[:, cut]
        down_ref[2 * tile + half] = down[:, cut]


def pack_last(get, extra, up_ref, down_ref):
    pack_tile([get(t) for t in range(4)], 6, up_ref, down_ref)
    pack_tile([get(4), get(5), extra, extra], 7, up_ref, down_ref)


def prepare_kernel(a, ps, m_ref, up, down, blocks, sems):
    copies = []
    for t in range(6):
        ref = a.piece(t)
        pack_tile([ref[t, v] for v in range(4)], t, up.buffer, down.buffer)
    pack_last(lambda t: a.buffer[t, NV - 1], ps[...], up.buffer, down.buffer)
    metal_edges(m_ref, up.buffer.at[16], down.buffer.at[16])
    up.put(slice(None))
    down.put(slice(None))
    for i in range(8):
        copies.append(
            pltpu.make_async_copy(
                a.buffer.at[:, :, :, pl.ds(i * CHUNK, CHUNK)], blocks.at[i], sems.at[i]
            )
        )
        copies[-1].start()
    for copy in copies:
        copy.wait()


def energy_kernel(tab_ref, m_ref, fc_ref, ff_ref, mf_ref, e):
    first = lax.axis_index("inst") * 6
    m_hot, m_row = metal_hots(mf_ref)
    f_hot, f_row = fluid_hots(ff_ref)
    values = at_faces(m_ref[...], m_hot, m_row) * fc_ref[...]
    cells = onto_cells(values, f_hot, f_row)
    for t in range(6):
        e.buffer[t] = combine(tab_ref, SYNTH, first + t, cells)
        e.put(pl.ds(t, 1))


def combine(tab_ref, base, t, fields):
    total = tab_ref[base + t * CH] * fields[0]
    for ch in range(1, CH):
        if ch != NH:
            total += tab_ref[base + t * CH + ch] * fields[ch]
    return total


def convect(jx_ref, jz_ref, dx, dz, rest, u):
    out = rest
    for v in range(NV):
        out = out - (0.5 * jx_ref[u, v]) * dx[v] - (0.5 * jz_ref[u, v]) * dz[v]
    return out


def first_kernel(
    tab_ref, jx_ref, jz_ref, a_in, s_in, ps_ref, up_ref, down_ref, e_in, fc_ref, ff_ref, m_ref, cond_ref,
    q, b_out, bup, bdown, hq, m_out,
    parts,
):
    first = lax.axis_index("inst") * 6
    step = ps_ref[...]
    step_before = pltpu.roll(edge_tile(up_ref, 7), 2, 0)
    step_after = pltpu.roll(edge_tile(down_ref, 7), 4, 0)
    q_ref, b_ref = q.buffer, b_out.buffer
    for t in range(6):
        a_ref, s_ref, e_ref = a_in.piece(t), s_in.piece(t), e_in.piece(t)
        for v in range(NV):
            a = a_ref[t, v]
            before, after = halo_pair(up_ref, down_ref, t, v)
            dx, dz, rest = stencil_parts(a, before, after)
            parts[0, v], parts[1, v], parts[2, v] = dx, dz, rest
            dx, dz, rest = stencil_parts(step * a, step_before * before, step_after * after)
            parts[3, v], parts[4, v], parts[5, v] = dx, dz, rest
        for i in range(8):
            cut = pl.ds(i * CHUNK, CHUNK)
            dx = [parts[0, v, :, cut] for v in range(NV)]
            dz = [parts[1, v, :, cut] for v in range(NV)]
            px = [parts[3, v, :, cut] for v in range(NV)]
            pz = [parts[4, v, :, cut] for v in range(NV)]
            for u in range(NV):
                a = a_ref[t, u, :, cut]
                space = convect(jx_ref, jz_ref, dx, dz, parts[2, u, :, cut], u)
                source = s_ref[t, u, :, cut] + space
                if u == NV - 1:
                    source = source + e_ref[t, :, cut]
                b = a + ps_ref[:, cut] * source
                b_ref[t, u, :, cut] = b
                q_ref[i, t * NV + u] = a + b + convect(jx_ref, jz_ref, px, pz, parts[5, u, :, cut], u)
        q.put((slice(None), pl.ds(t * NV, NV)))
        b_out.put(pl.ds(t, 1))
        pack_tile([b_ref[t, v] for v in range(4)], t, bup.buffer, bdown.buffer)
    pack_last(lambda t: b_ref[t, NV - 1], step, bup.buffer, bdown.buffer)
    bup.put(slice(None))
    bdown.put(slice(None))
    f_hot, f_row = fluid_hots(ff_ref)
    heat = []
    for ch in range(CH):
        h0 = h1 = h2 = h3 = None
        for t in range(6):
            at = (first + t) * CH + ch
            q4 = jnp.concatenate([q_ref[i, t * NV + NV - 1] for i in range(8)], axis=1)
            a, b = a_in.buffer[t, NV - 1], b_ref[t, NV - 1]
            x0 = tab_ref[W0 + at] * b
            x1 = tab_ref[W1 + at] * a
            x2 = tab_ref[W1 + at] * q4
            x3 = tab_ref[W2 + at] * a
            h0, h1, h2, h3 = (
                (x0, x1, x2, x3) if t == 0 else (h0 + x0, h1 + x1, h2 + x2, h3 + x3)
            )
        heat.append(h0 - step * h1)
        hq.buffer[ch] = step * (step * h3 - h2)
    hq.put(slice(None))
    values = at_faces(jnp.stack(heat), f_hot, f_row) * fc_ref[...]
    for i in range(8):
        for k in range(4):
            q_ref[i, 30 + k] = values[:, k * CHUNK : (k + 1) * CHUNK]
    q.put((slice(None), pl.ds(30, 4)))
    before, after = metal_sides(up_ref.at[16], down_ref.at[16])
    m = metal_update(m_ref, before, after, cond_ref[...])
    for ch in range(CH):
        m_out.buffer[ch] = m[ch]
    m_out.put(slice(None))


def rotate_time(kron, x):
    high, low = split(x)
    return jnp.dot(kron, jnp.concatenate([high, low, high], axis=0), preferred_element_type=F32)


def local_step(ps_ref):
    start = pl.multiple_of(lax.axis_index("inst") * CHUNK, CHUNK)
    return ps_ref[:, pl.ds(start, CHUNK)]


def turned(get):
    return jnp.concatenate(
        [
            jnp.concatenate([get(j, t, v) for j in range(8) for t in range(6)], axis=0)
            for v in range(NV)
        ],
        axis=1,
    )


def derive_kernel(kron, a, ps_ref, g):
    wide = jnp.concatenate([local_step(ps_ref)] * NV, axis=1)
    a_ref = a.whole()
    x = turned(lambda j, t, v: a_ref[j, t, v])
    d = rotate_time(kron.whole()[...], x)
    g.buffer[...] = (d.reshape(NT, ROWS, NV * CHUNK) * wide[None]).reshape(NT * ROWS, NV * CHUNK)
    g.put(slice(None))


def middle_kernel(tab_ref, jx_ref, jz_ref, b_in, s_in, ps_ref, up_ref, down_ref, hq_in, c_out, hc, parts):
    first = lax.axis_index("inst") * 6
    c_ref = c_out.buffer
    for t in range(6):
        b_ref, s_ref = b_in.piece(t), s_in.piece(t)
        for v in range(NV):
            before, after = halo_pair(up_ref, down_ref, t, v)
            dx, dz, rest = stencil_parts(b_ref[t, v], before, after)
            parts[0, v], parts[1, v], parts[2, v] = dx, dz, rest
        for i in range(8):
            cut = pl.ds(i * CHUNK, CHUNK)
            dx = [parts[0, v, :, cut] for v in range(NV)]
            dz = [parts[1, v, :, cut] for v in range(NV)]
            for u in range(NV):
                space = convect(jx_ref, jz_ref, dx, dz, parts[2, u, :, cut], u)
                c_ref[t, u, :, cut] = b_ref[t, u, :, cut] + ps_ref[:, cut] * (s_ref[t, u, :, cut] + space)
        c_out.put(pl.ds(t, 1))
    hq_ref = hq_in.whole()
    for ch in range(CH):
        total = hq_ref[ch]
        for t in range(6):
            total += tab_ref[W0 + (first + t) * CH + ch] * c_ref[t, NV - 1]
        hc.buffer[ch] = total
    hc.put(slice(None))


def metal_update(m, before, after, cond):
    row = row_index(MSPAN)
    out = []
    for ch in range(CH):
        a = m[ch]
        east = pltpu.roll(jnp.where(row == 0, after[ch], a), 7, 0)
        west = pltpu.roll(jnp.where(row == 7, before[ch], a), 1, 0)
        north, south = span_sides(a)
        laplace = east + west + north + south - 4.0 * a
        h = ch % NH
        turn = -heat_capacity * h * m[ch + NH] if ch < NH else heat_capacity * h * m[ch - NH]
        out.append(a + metal_step * (cond * laplace - sigma_metal * a - turn))
    return out


def metal_edges(m, up_ref, down_ref):
    up_ref[...] = jnp.concatenate([m[ch][7:8] for ch in range(CH)], axis=0)
    down_ref[...] = jnp.concatenate([m[ch][0:1] for ch in range(CH)], axis=0)


def metal_sides(up_ref, down_ref):
    before = [jnp.broadcast_to(up_ref[ch : ch + 1], (ROWS, MSPAN)) for ch in range(CH)]
    after = [jnp.broadcast_to(down_ref[ch : ch + 1], (ROWS, MSPAN)) for ch in range(CH)]
    return before, after


def heat_sum(blocks_ref):
    tiles = []
    for k in range(4):
        total = blocks_ref[0, 30 + k]
        for j in range(1, 8):
            total += blocks_ref[j, 30 + k]
        tiles.append(total)
    return jnp.concatenate(tiles, axis=1)


def second_kernel(
    tab_ref, q, g, kron, ps_ref, m_in, fc_ref, ff_ref, mf_ref, hc,
    v, m_out, mup, mdown, e,
):
    first = lax.axis_index("inst") * 6
    step = ps_ref[...]
    coeff = fc_ref[...]
    m_hot, m_row = metal_hots(mf_ref)
    f_hot, f_row = fluid_hots(ff_ref)
    q_ref, v_ref = q.whole(), v.buffer
    source = onto_cells(heat_sum(q_ref), m_hot, m_row)
    m_ref = m_in.whole()
    m = [m_ref[ch] + metal_step * source[ch] for ch in range(CH)]
    for ch in range(CH):
        m_out.buffer[ch] = m[ch]
    m_out.put(slice(None))
    metal_edges(m, mup.buffer, mdown.buffer)
    mup.put(slice(None))
    mdown.put(slice(None))
    cells = onto_cells(at_faces(jnp.stack(m), m_hot, m_row) * coeff, f_hot, f_row)
    for t in range(6):
        e.buffer[t] = step * combine(tab_ref, SYNTH, first + t, cells)
    e.put(slice(None))
    hc_ref = hc.whole()
    heat = []
    for ch in range(CH):
        total = hc_ref[ch]
        for t in range(6):
            total += tab_ref[W0 + (first + t) * CH + ch] * e.buffer[t]
        heat.append(total)
    values = at_faces(jnp.stack(heat), f_hot, f_row) * coeff
    for i in range(8):
        for k in range(4):
            v_ref[i, 30 + k] = values[:, k * CHUNK : (k + 1) * CHUNK]
    x = turned(lambda j, t, u: q_ref[j, t * NV + u]) - g.whole()[...]
    kron_ref = kron.whole()
    minus = -local_step(ps_ref)
    for half in range(2):
        d = rotate_time(kron_ref[pl.ds(half * 192, 192), :], x)
        for j in range(4):
            for t in range(6):
                at = (j * 6 + t) * ROWS
                for u in range(NV):
                    v_ref[half * 4 + j, t * NV + u] = minus * d[at : at + ROWS, u * CHUNK : (u + 1) * CHUNK]
        v.put(pl.ds(half * 4, 4))


def last_kernel(v, c, e, m_in, mup_ref, mdown_ref, cond_ref, mf_ref, out, m_out):
    for t in range(6):
        v_ref, c_ref, e_ref = v.piece(t), c.piece(t), e.whole()
        for i in range(8):
            cut = pl.ds(i * CHUNK, CHUNK)
            for u in range(NV):
                total = c_ref[t, u, :, cut] + v_ref[i, t * NV + u]
                if u == NV - 1:
                    total = total + e_ref[t, :, cut]
                out.buffer[t, u, :, cut] = total
        out.put(pl.ds(t, 1))
    m_hot, m_row = metal_hots(mf_ref)
    source = onto_cells(heat_sum(v.whole()), m_hot, m_row)
    before, after = metal_sides(mup_ref, mdown_ref)
    m = metal_update(m_in.whole(), before, after, cond_ref[...])
    for ch in range(CH):
        m_out.buffer[ch] = m[ch] + metal_step * source[ch]
    m_out.put(slice(None))


def exchange(up, down):
    n = lax.axis_size("space")
    forward = [(i, (i + 1) % n) for i in range(n)]
    back = [(j, i) for i, j in forward]
    return lax.ppermute(up, "space", forward), lax.ppermute(down, "space", back)


def turn(x):
    return lax.all_to_all(x, "inst", 0, 0, tiled=True)


SIX = by_piece(6)
EDGES = (17, ROWS, 512)
FLUID = (6, NV, ROWS, SPAN)
METAL = (CH, ROWS, MSPAN)
BLOCKS = (8, 34, ROWS, CHUNK)


def local(a0, source, ps, jx, jz, metal, cond, coeff, ff, mf):
    kron = jnp.asarray(KRON)
    tab = jnp.asarray(FLAT)
    coeff, ff, mf = (x.reshape(1, NF) for x in (coeff, ff, mf))
    metal = metal.reshape(CH, ROWS, MSPAN)
    up, down, blocks = call(
        prepare_kernel,
        [(a0, SIX), (ps, "vmem"), (metal, "vmem")],
        [(EDGES, 1), (EDGES, 1), ((8, 6, NV, ROWS, CHUNK), -1)],
        scratch=[pltpu.SemaphoreType.DMA((8,))],
    )
    up, down = exchange(up, down)
    a_turned = turn(blocks)
    (e0,) = call(
        energy_kernel,
        [(tab, "smem"), (metal, "vmem"), (coeff, "vmem"), (ff, "vmem"), (mf, "vmem")],
        [((6, ROWS, SPAN), 6)],
    )
    jacobians = [(tab, "smem"), (jx, "smem"), (jz, "smem")]
    q, b, bup, bdown, hq, metal = call(
        first_kernel,
        jacobians
        + [(a0, SIX), (source, SIX), (ps, "vmem"), (up, "vmem"), (down, "vmem"), (e0, SIX)]
        + [(coeff, "vmem"), (ff, "vmem"), (metal, "vmem"), (cond, "vmem")],
        [(BLOCKS, 7), (FLUID, 6), (EDGES, 1), (EDGES, 1), ((CH, ROWS, SPAN), 1), (METAL, 1)],
        scratch=[pltpu.VMEM((6, NV, ROWS, SPAN), F32)],
    )
    q_turned = turn(q)
    bup, bdown = exchange(bup, bdown)
    (g,) = call(
        derive_kernel,
        [(kron, WHOLE), (a_turned, WHOLE), (ps, "vmem")],
        [((NT * ROWS, NV * CHUNK), 1)],
    )
    c, hc = call(
        middle_kernel,
        jacobians
        + [(b, SIX), (source, SIX), (ps, "vmem"), (bup, "vmem"), (bdown, "vmem"), (hq, WHOLE)],
        [(FLUID, 6), ((CH, ROWS, SPAN), 1)],
        scratch=[pltpu.VMEM((3, NV, ROWS, SPAN), F32)],
    )
    v, metal, mup, mdown, e1 = call(
        second_kernel,
        [(tab, "smem"), (q_turned, WHOLE), (g, WHOLE), (kron, WHOLE), (ps, "vmem"), (metal, WHOLE)]
        + [(coeff, "vmem"), (ff, "vmem"), (mf, "vmem"), (hc, WHOLE)],
        [(BLOCKS, 2), (METAL, 1), ((CH, MSPAN), 1), ((CH, MSPAN), 1), ((6, ROWS, SPAN), 1)],
    )
    v = turn(v)
    mup, mdown = exchange(mup, mdown)
    pieces = tuple((slice(None), pl.ds(t * NV, NV)) for t in range(6)) + ((slice(None), pl.ds(30, 4)),)
    out, metal = call(
        last_kernel,
        [(v, pieces), (c, SIX), (e1, WHOLE), (metal, WHOLE), (mup, "vmem"), (mdown, "vmem")]
        + [(cond, "vmem"), (mf, "vmem")],
        [(FLUID, 6), (METAL, 1)],
    )
    return out, metal.reshape(2, NH, ROWS, MSPAN)


def solution(mesh):
    return jax.shard_map(
        local,
        mesh=mesh,
        in_specs=(
            P("inst", None, "space", None),
            P("inst", None, "space", None),
            P("space", None),
            P(),
            P(),
            P(None, None, "space", None),
            P("space", None),
            P("space"),
            P("space"),
            P("space"),
        ),
        out_specs=(P("inst", None, "space", None), P(None, None, "space", None)),
        check_vma=False,
    )
```

```python
import math

import jax
import jax.numpy as jnp
import ml_dtypes
import numpy as np
from jax import lax
from jax.experimental import pallas as pl
from jax.experimental.pallas import tpu as pltpu
from jax.sharding import PartitionSpec as P

NT, NV, NH = 48, 5, 4
ROWS, SPAN, MSPAN, NF = 8, 1024, 512, 512
CHUNK = 128
CH = 2 * NH
F32, BF16 = jnp.float32, jnp.bfloat16

damping_fourth = 1.0 / 32.0
viscous_coef = 0.1
sigma_fluid = 0.5
metal_step = 0.2
sigma_metal = 0.5
heat_capacity = 0.5
flux_scale = 4.0


def tables():
    t = np.arange(NT)
    offset = t[:, None] - t[None, :]
    angle = np.where(offset == 0, 0.5, math.pi * offset / NT)
    spectral = np.where(
        offset == 0, 0.0, 0.5 * (1.0 - 2.0 * (offset % 2)) * np.cos(angle) / np.sin(angle)
    )
    phase = 2.0 * math.pi * ((np.arange(NH)[:, None] * t[None, :]) % NT) / NT
    synth = np.concatenate([np.cos(phase), -np.sin(phase)])
    w0 = synth * (flux_scale / NT)
    w1 = w0 @ spectral
    w2 = w1 @ spectral
    block, inner = np.divmod(t, 6)
    relative = spectral[(6 * (block[:, None] + block[None, :]) + inner[:, None]) % NT, inner[None, :]]
    high = relative.astype(np.float32).astype(ml_dtypes.bfloat16)
    low = (relative - high.astype(np.float64)).astype(np.float32).astype(ml_dtypes.bfloat16)
    eye = np.eye(ROWS, dtype=np.float32)
    kron_high = np.kron(high.astype(np.float32), eye)
    kron_low = np.kron(low.astype(np.float32), eye)
    kron = np.concatenate([kron_high, kron_high, kron_low], axis=1).astype(ml_dtypes.bfloat16)
    flat = np.concatenate([m.T.reshape(-1) for m in (synth, w0, w1, w2)]).astype(np.float32)
    return kron, flat


KRON, FLAT = tables()
SYNTH, W0, W1, W2 = (i * NT * CH for i in range(4))


def call(body, operands, results, scratch=(), flops=1 << 22, moved=1 << 22):
    return pl.pallas_call(
        body,
        out_shape=[shape(*dims) for dims in results],
        in_specs=[pl.BlockSpec(memory_space=pltpu.SMEM if m else pltpu.VMEM) for _, m in operands],
        out_specs=[pl.BlockSpec(memory_space=pltpu.VMEM)] * len(results),
        scratch_shapes=list(scratch),
        compiler_params=pltpu.CompilerParams(vmem_limit_bytes=24 << 20),
        cost_estimate=pl.CostEstimate(flops=flops, bytes_accessed=moved, transcendentals=0),
    )(*[array for array, _ in operands])


def shape(*dims):
    return jax.ShapeDtypeStruct(dims, F32)


def row_index(n=SPAN):
    return lax.broadcasted_iota(jnp.int32, (ROWS, n), 0)


def split(x):
    high = x.astype(BF16)
    return high, (x - high.astype(F32)).astype(BF16)


def one_hot(index, n):
    cell = lax.broadcasted_iota(jnp.int32, (n, NF), 0)
    return jnp.where(cell == index, 1.0, 0.0).astype(BF16)


def at_faces(field, span_hot, row_hot):
    n = field.shape[-1]
    both = jnp.concatenate(split(field.reshape(CH * ROWS, n)), axis=0)
    picked = jnp.dot(both, span_hot, preferred_element_type=F32)
    picked = (picked[: CH * ROWS] + picked[CH * ROWS :]).reshape(CH, ROWS, NF)
    return jnp.sum(picked * row_hot[None], axis=1)


def onto_cells(values, span_hot, row_hot):
    spread = (values[:, None, :] * row_hot[None]).reshape(CH * ROWS, NF)
    both = jnp.concatenate(split(spread), axis=0)
    out = lax.dot_general(both, span_hot, (((1,), (1,)), ((), ())), preferred_element_type=F32)
    return (out[: CH * ROWS] + out[CH * ROWS :]).reshape(CH, ROWS, span_hot.shape[0])


def fluid_hots(ff_ref):
    cell = ff_ref[...]
    span = one_hot(cell & (SPAN - 1), SPAN)
    rows = jnp.where(row_index(NF) == (cell >> 10), 1.0, 0.0)
    return span, rows


def metal_hots(mf_ref):
    cell = mf_ref[...]
    span = one_hot(cell & (MSPAN - 1), MSPAN)
    rows = jnp.where(row_index(NF) == (cell >> 9), 1.0, 0.0)
    return span, rows


def span_sides(a):
    n = a.shape[-1]
    lane = lax.broadcasted_iota(jnp.int32, a.shape, a.ndim - 1)
    north = jnp.where(lane == n - 1, 0.0, pltpu.roll(a, n - 1, a.ndim - 1))
    south = jnp.where(lane == 0, 0.0, pltpu.roll(a, 1, a.ndim - 1))
    return north, south


def stencil_parts(a, before, after):
    row = row_index(a.shape[-1])
    east_one = pltpu.roll(jnp.where(row == 0, after, a), 7, 0)
    east_two = pltpu.roll(jnp.where(row < 2, after, a), 6, 0)
    west_one = pltpu.roll(jnp.where(row == 7, before, a), 1, 0)
    west_two = pltpu.roll(jnp.where(row >= 6, before, a), 2, 0)
    north, south = span_sides(a)
    rest = (
        (4.0 * damping_fourth) * (east_one + west_one)
        - damping_fourth * (east_two + west_two)
        + viscous_coef * (north + south)
        - (6.0 * damping_fourth + 2.0 * viscous_coef + sigma_fluid) * a
    )
    return east_one - west_one, north - south, rest


def edge_tile(ref, tile):
    return jnp.concatenate([ref[2 * tile], ref[2 * tile + 1]], axis=1)


def halo_pair(up_ref, down_ref, t, v):
    tile, slot = (t, v) if v < 4 else (6 + t // 4, t % 4)
    before = pltpu.roll(edge_tile(up_ref, tile), (6 - 2 * slot) % 8, 0)
    after = pltpu.roll(edge_tile(down_ref, tile), (8 - 2 * slot) % 8, 0)
    return before, after


def pack_tile(blocks, tile, up_ref, down_ref):
    row = row_index()
    up = down = None
    for slot, a in enumerate(blocks):
        u = pltpu.roll(a, (2 * slot + 2) % 8, 0) if (2 * slot + 2) % 8 else a
        d = pltpu.roll(a, 2 * slot, 0) if slot else a
        mine = (row >> 1) == slot
        up = u if up is None else jnp.where(mine, u, up)
        down = d if down is None else jnp.where(mine, d, down)
    for half in range(2):
        cut = slice(half * 512, half * 512 + 512)
        up_ref[2 * tile + half] = up[:, cut]
        down_ref[2 * tile + half] = down[:, cut]


def pack_last(get, extra, up_ref, down_ref):
    pack_tile([get(t) for t in range(4)], 6, up_ref, down_ref)
    pack_tile([get(4), get(5), extra, extra], 7, up_ref, down_ref)


def prepare_kernel(a_ref, ps_ref, m_ref, up_ref, down_ref):
    for t in range(6):
        pack_tile([a_ref[t, v] for v in range(4)], t, up_ref, down_ref)
    pack_last(lambda t: a_ref[t, NV - 1], ps_ref[...], up_ref, down_ref)
    metal_edges(m_ref, up_ref.at[16], down_ref.at[16])


def chunk_of(k):
    return pl.ds(pl.multiple_of(lax.rem(lax.axis_index("inst") + k, 8) * CHUNK, CHUNK), CHUNK)


def blocks_kernel(a_ref, *out_refs):
    for k, out_ref in enumerate(out_refs):
        cut = chunk_of(k)
        for t in range(6):
            for v in range(NV):
                out_ref[t * NV + v] = a_ref[t, v, :, cut]


def energy_kernel(tab_ref, m_ref, fc_ref, ff_ref, mf_ref, e_ref):
    first = lax.axis_index("inst") * 6
    m_hot, m_row = metal_hots(mf_ref)
    f_hot, f_row = fluid_hots(ff_ref)
    values = at_faces(m_ref[...], m_hot, m_row) * fc_ref[...]
    cells = onto_cells(values, f_hot, f_row)
    for t in range(6):
        e_ref[t] = combine(tab_ref, SYNTH, first + t, cells)


def combine(tab_ref, base, t, fields):
    total = tab_ref[base + t * CH] * fields[0]
    for ch in range(1, CH):
        if ch != NH:
            total += tab_ref[base + t * CH + ch] * fields[ch]
    return total


def convect(jx_ref, jz_ref, dx, dz, rest, u):
    out = rest
    for v in range(NV):
        out = out - (0.5 * jx_ref[u, v]) * dx[v] - (0.5 * jz_ref[u, v]) * dz[v]
    return out


def first_kernel(
    tab_ref, jx_ref, jz_ref, a_ref, s_ref, ps_ref, up_ref, down_ref, e_ref, fc_ref, ff_ref, m_ref, cond_ref,
    *refs,
):
    q_refs, (b_ref, bup_ref, bdown_ref, hq_ref, m_out, parts, q4_ref) = refs[:8], refs[8:]
    first = lax.axis_index("inst") * 6
    step = ps_ref[...]
    step_before = pltpu.roll(edge_tile(up_ref, 7), 2, 0)
    step_after = pltpu.roll(edge_tile(down_ref, 7), 4, 0)
    cuts = [chunk_of(k) for k in range(8)]
    for t in range(6):
        for v in range(NV):
            a = a_ref[t, v]
            before, after = halo_pair(up_ref, down_ref, t, v)
            dx, dz, rest = stencil_parts(a, before, after)
            parts[0, v], parts[1, v], parts[2, v] = dx, dz, rest
            dx, dz, rest = stencil_parts(step * a, step_before * before, step_after * after)
            parts[3, v], parts[4, v], parts[5, v] = dx, dz, rest
        for i in range(8):
            cut = cuts[i]
            dx = [parts[0, v, :, cut] for v in range(NV)]
            dz = [parts[1, v, :, cut] for v in range(NV)]
            px = [parts[3, v, :, cut] for v in range(NV)]
            pz = [parts[4, v, :, cut] for v in range(NV)]
            for u in range(NV):
                a = a_ref[t, u, :, cut]
                space = convect(jx_ref, jz_ref, dx, dz, parts[2, u, :, cut], u)
                source = s_ref[t, u, :, cut] + space
                if u == NV - 1:
                    source = source + e_ref[t, :, cut]
                b = a + ps_ref[:, cut] * source
                b_ref[t, u, :, cut] = b
                q = a + b + convect(jx_ref, jz_ref, px, pz, parts[5, u, :, cut], u)
                q_refs[i][t * NV + u] = q
                if u == NV - 1:
                    q4_ref[t, :, cut] = q
        pack_tile([b_ref[t, v] for v in range(4)], t, bup_ref, bdown_ref)
    pack_last(lambda t: b_ref[t, NV - 1], step, bup_ref, bdown_ref)
    f_hot, f_row = fluid_hots(ff_ref)
    heat = []
    for ch in range(CH):
        h0 = h1 = h2 = h3 = None
        for t in range(6):
            at = (first + t) * CH + ch
            a, b = a_ref[t, NV - 1], b_ref[t, NV - 1]
            x0 = tab_ref[W0 + at] * b
            x1 = tab_ref[W1 + at] * a
            x2 = tab_ref[W1 + at] * q4_ref[t]
            x3 = tab_ref[W2 + at] * a
            h0, h1, h2, h3 = (
                (x0, x1, x2, x3) if t == 0 else (h0 + x0, h1 + x1, h2 + x2, h3 + x3)
            )
        heat.append(h0 - step * h1)
        hq_ref[ch] = step * (step * h3 - h2)
    values = at_faces(jnp.stack(heat), f_hot, f_row) * fc_ref[...]
    put_heat(q_refs, values)
    before, after = metal_sides(up_ref.at[16], down_ref.at[16])
    m = metal_update(m_ref, before, after, cond_ref[...])
    for ch in range(CH):
        m_out[ch] = m[ch]


def put_heat(refs, values):
    for ref in refs:
        for k in range(4):
            ref[30 + k] = values[:, k * CHUNK : (k + 1) * CHUNK]


def rotate_time(kron, x):
    high, low = split(x)
    return jnp.dot(kron, jnp.concatenate([high, low, high], axis=0), preferred_element_type=F32)


def local_step(ps_ref):
    start = pl.multiple_of(lax.axis_index("inst") * CHUNK, CHUNK)
    return ps_ref[:, pl.ds(start, CHUNK)]


def turned(get):
    return jnp.concatenate(
        [
            jnp.concatenate([get(j, t, v) for j in range(8) for t in range(6)], axis=0)
            for v in range(NV)
        ],
        axis=1,
    )


def derive_kernel(kron_ref, ps_ref, *refs):
    a_refs, g_ref = refs[:8], refs[8]
    wide = jnp.concatenate([local_step(ps_ref)] * NV, axis=1)
    x = turned(lambda j, t, v: a_refs[j][t * NV + v])
    d = rotate_time(kron_ref[...], x)
    d = (d.reshape(NT, ROWS, NV * CHUNK) * wide[None]).reshape(NT * ROWS, NV * CHUNK)
    for k in range(8):
        at = ((8 - k) % 8) * 6 * ROWS
        g_ref[pl.ds(k * 6 * ROWS, 6 * ROWS), :] = d[at : at + 6 * ROWS]


def middle_kernel(tab_ref, jx_ref, jz_ref, b_ref, s_ref, ps_ref, up_ref, down_ref, hq_ref, g_ref, c_ref, hc_ref, parts):
    first = lax.axis_index("inst") * 6
    for t in range(6):
        for v in range(NV):
            before, after = halo_pair(up_ref, down_ref, t, v)
            dx, dz, rest = stencil_parts(b_ref[t, v], before, after)
            parts[0, v], parts[1, v], parts[2, v] = dx, dz, rest
        for i in range(8):
            cut = pl.ds(i * CHUNK, CHUNK)
            dx = [parts[0, v, :, cut] for v in range(NV)]
            dz = [parts[1, v, :, cut] for v in range(NV)]
            for u in range(NV):
                space = convect(jx_ref, jz_ref, dx, dz, parts[2, u, :, cut], u)
                c_ref[t, u, :, cut] = b_ref[t, u, :, cut] + ps_ref[:, cut] * (s_ref[t, u, :, cut] + space)
    for ch in range(CH):
        total = hq_ref[ch]
        for t in range(6):
            total += tab_ref[W0 + (first + t) * CH + ch] * c_ref[t, NV - 1]
        hc_ref[ch] = total


def metal_update(m, before, after, cond):
    row = row_index(MSPAN)
    out = []
    for ch in range(CH):
        a = m[ch]
        east = pltpu.roll(jnp.where(row == 0, after[ch], a), 7, 0)
        west = pltpu.roll(jnp.where(row == 7, before[ch], a), 1, 0)
        north, south = span_sides(a)
        laplace = east + west + north + south - 4.0 * a
        h = ch % NH
        turn = -heat_capacity * h * m[ch + NH] if ch < NH else heat_capacity * h * m[ch - NH]
        out.append(a + metal_step * (cond * laplace - sigma_metal * a - turn))
    return out


def metal_edges(m, up_ref, down_ref):
    up_ref[...] = jnp.concatenate([m[ch][7:8] for ch in range(CH)], axis=0)
    down_ref[...] = jnp.concatenate([m[ch][0:1] for ch in range(CH)], axis=0)


def metal_sides(up_ref, down_ref):
    before = [jnp.broadcast_to(up_ref[ch : ch + 1], (ROWS, MSPAN)) for ch in range(CH)]
    after = [jnp.broadcast_to(down_ref[ch : ch + 1], (ROWS, MSPAN)) for ch in range(CH)]
    return before, after


def heat_sum(refs):
    tiles = []
    for k in range(4):
        total = refs[0][30 + k]
        for ref in refs[1:]:
            total += ref[30 + k]
        tiles.append(total)
    return jnp.concatenate(tiles, axis=1)


def second_kernel(
    tab_ref, g_ref, kron_ref, ps_ref, m_ref, fc_ref, ff_ref, mf_ref, hc_ref,
    *refs,
):
    q_refs, v_refs, (m_out, mup_ref, mdown_ref, e_ref) = refs[:8], refs[8:16], refs[16:]
    first = lax.axis_index("inst") * 6
    step = ps_ref[...]
    coeff = fc_ref[...]
    m_hot, m_row = metal_hots(mf_ref)
    f_hot, f_row = fluid_hots(ff_ref)
    source = onto_cells(heat_sum(q_refs), m_hot, m_row)
    m = [m_ref[ch] + metal_step * source[ch] for ch in range(CH)]
    for ch in range(CH):
        m_out[ch] = m[ch]
    metal_edges(m, mup_ref, mdown_ref)
    cells = onto_cells(at_faces(jnp.stack(m), m_hot, m_row) * coeff, f_hot, f_row)
    for t in range(6):
        e_ref[t] = step * combine(tab_ref, SYNTH, first + t, cells)
    heat = []
    for ch in range(CH):
        total = hc_ref[ch]
        for t in range(6):
            total += tab_ref[W0 + (first + t) * CH + ch] * e_ref[t]
        heat.append(total)
    put_heat(v_refs, at_faces(jnp.stack(heat), f_hot, f_row) * coeff)
    x = turned(lambda j, t, u: q_refs[j][t * NV + u]) - g_ref[...]
    d = rotate_time(kron_ref[...], x)
    minus = -local_step(ps_ref)
    for j in range(8):
        for t in range(6):
            at = (j * 6 + t) * ROWS
            for u in range(NV):
                v_refs[j][t * NV + u] = minus * d[at : at + ROWS, u * CHUNK : (u + 1) * CHUNK]


def last_kernel(c_ref, e_ref, m_ref, mup_ref, mdown_ref, cond_ref, mf_ref, *refs):
    v_refs, (out_ref, m_out) = refs[:8], refs[8:]
    for k in range(8):
        cut = chunk_of(8 - k)
        for t in range(6):
            for u in range(NV):
                total = c_ref[t, u, :, cut] + v_refs[k][t * NV + u]
                if u == NV - 1:
                    total = total + e_ref[t, :, cut]
                out_ref[t, u, :, cut] = total
    m_hot, m_row = metal_hots(mf_ref)
    source = onto_cells(heat_sum(v_refs), m_hot, m_row)
    before, after = metal_sides(mup_ref, mdown_ref)
    m = metal_update(m_ref, before, after, cond_ref[...])
    for ch in range(CH):
        m_out[ch] = m[ch] + metal_step * source[ch]


def exchange(up, down):
    n = lax.axis_size("space")
    forward = [(i, (i + 1) % n) for i in range(n)]
    back = [(j, i) for i, j in forward]
    return lax.ppermute(up, "space", forward), lax.ppermute(down, "space", back)


def turn(blocks):
    n = len(blocks)
    return [blocks[0]] + [
        lax.ppermute(blocks[k], "inst", [(i, (i + k) % n) for i in range(n)]) for k in range(1, n)
    ]


EDGES = (17, ROWS, 512)
FLUID = (6, NV, ROWS, SPAN)
ONE = (6, ROWS, SPAN)
METAL = (CH, ROWS, MSPAN)
HARMONICS = (CH, ROWS, SPAN)
BLOCK = (34, ROWS, CHUNK)


def plain(*arrays):
    return [(array, False) for array in arrays]


def local(a0, source, ps, jx, jz, metal, cond, coeff, ff, mf):
    kron = jnp.asarray(KRON)
    tab = jnp.asarray(FLAT)
    coeff, ff, mf = (x.reshape(1, NF) for x in (coeff, ff, mf))
    metal = metal.reshape(METAL)
    up, down = call(prepare_kernel, plain(a0, ps, metal), [EDGES] * 2)
    up, down = exchange(up, down)
    a_turned = turn(call(blocks_kernel, plain(a0), [(30, ROWS, CHUNK)] * 8))
    (e0,) = call(energy_kernel, [(tab, True)] + plain(metal, coeff, ff, mf), [ONE])
    scalars = [(tab, True), (jx, True), (jz, True)]
    *q, b, bup, bdown, hq, metal = call(
        first_kernel,
        scalars + plain(a0, source, ps, up, down, e0, coeff, ff, metal, cond),
        [BLOCK] * 8 + [FLUID, EDGES, EDGES, HARMONICS, METAL],
        scratch=[pltpu.VMEM((6, NV, ROWS, SPAN), F32), pltpu.VMEM(ONE, F32)],
    )
    q_turned = turn(q)
    bup, bdown = exchange(bup, bdown)
    (g,) = call(derive_kernel, plain(kron, ps, *a_turned), [(NT * ROWS, NV * CHUNK)])
    c, hc = call(
        middle_kernel,
        scalars + plain(b, source, ps, bup, bdown, hq, g),
        [FLUID, HARMONICS],
        scratch=[pltpu.VMEM((3, NV, ROWS, SPAN), F32)],
    )
    *v, metal, mup, mdown, e1 = call(
        second_kernel,
        [(tab, True)] + plain(g, kron, ps, metal, coeff, ff, mf, hc, *q_turned),
        [BLOCK] * 8 + [METAL, (CH, MSPAN), (CH, MSPAN), ONE],
    )
    v = turn(v)
    mup, mdown = exchange(mup, mdown)
    out, metal = call(last_kernel, plain(c, e1, metal, mup, mdown, cond, mf, *v), [FLUID, METAL])
    return out, metal.reshape(2, NH, ROWS, MSPAN)


def solution(mesh):
    return jax.shard_map(
        local,
        mesh=mesh,
        in_specs=(
            P("inst", None, "space", None),
            P("inst", None, "space", None),
            P("space", None),
            P(),
            P(),
            P(None, None, "space", None),
            P("space", None),
            P("space"),
            P("space"),
            P("space"),
        ),
        out_specs=(P("inst", None, "space", None), P(None, None, "space", None)),
        check_vma=False,
    )
```

```python
import math

import jax
import jax.numpy as jnp
import ml_dtypes
import numpy as np
from jax import lax
from jax.experimental import pallas as pl
from jax.experimental.pallas import tpu as pltpu
from jax.sharding import PartitionSpec as P

NT, NV, NH = 48, 5, 4
ROWS, SPAN, MSPAN, NF = 8, 1024, 512, 512
CHUNK = 128
CH = 2 * NH
F32, BF16 = jnp.float32, jnp.bfloat16

damping_fourth = 1.0 / 32.0
viscous_coef = 0.1
sigma_fluid = 0.5
metal_step = 0.2
sigma_metal = 0.5
heat_capacity = 0.5
flux_scale = 4.0


def tables():
    t = np.arange(NT)
    offset = t[:, None] - t[None, :]
    angle = np.where(offset == 0, 0.5, math.pi * offset / NT)
    spectral = np.where(
        offset == 0, 0.0, 0.5 * (1.0 - 2.0 * (offset % 2)) * np.cos(angle) / np.sin(angle)
    )
    phase = 2.0 * math.pi * ((np.arange(NH)[:, None] * t[None, :]) % NT) / NT
    synth = np.concatenate([np.cos(phase), -np.sin(phase)])
    w0 = synth * (flux_scale / NT)
    w1 = w0 @ spectral
    w2 = w1 @ spectral
    high = spectral.astype(np.float32).astype(ml_dtypes.bfloat16)
    low = (spectral - high.astype(np.float64)).astype(np.float32).astype(ml_dtypes.bfloat16)
    eye = np.eye(ROWS, dtype=np.float32)
    kron_high = np.kron(high.astype(np.float32), eye)
    kron_low = np.kron(low.astype(np.float32), eye)
    kron = np.concatenate([kron_high, kron_high, kron_low], axis=1).astype(ml_dtypes.bfloat16)
    flat = np.concatenate([m.T.reshape(-1) for m in (synth, w0, w1, w2)]).astype(np.float32)
    return kron, flat


KRON, FLAT = tables()
SYNTH, W0, W1, W2 = (i * NT * CH for i in range(4))


class Loaded:
    def __init__(self, source, buffer, sems, cut):
        self.buffer, self.copies = buffer, []
        for i, index in enumerate(cut):
            self.copies.append(pltpu.make_async_copy(source.at[index], buffer.at[index], sems.at[i]))
        self.waiting = set(range(len(cut)))

    def start(self, i):
        self.copies[i].start()

    def piece(self, i):
        if i in self.waiting:
            self.waiting.remove(i)
            self.copies[i].wait()
        return self.buffer

    def whole(self):
        for i in range(len(self.copies)):
            self.piece(i)
        return self.buffer


class Held:
    def __init__(self, ref):
        self.buffer = ref

    def piece(self, i):
        return self.buffer

    def whole(self):
        return self.buffer

    def put(self, index):
        pass


class Stored:
    def __init__(self, target, buffer, sems):
        self.target, self.buffer, self.sems, self.copies = target, buffer, sems, []

    def put(self, index):
        copy = pltpu.make_async_copy(
            self.buffer.at[index], self.target.at[index], self.sems.at[len(self.copies)]
        )
        copy.start()
        self.copies.append(copy)

    def finish(self):
        for copy in self.copies:
            copy.wait()


WHOLE = (slice(None),)


def by_piece(n):
    return tuple(pl.ds(i, 1) for i in range(n))


def call(body, operands, results, scratch=(), flops=1 << 20, moved=1 << 20):
    space = {"smem": pltpu.SMEM, "vmem": pltpu.VMEM, "held": pltpu.VMEM}
    modes = [mode for _, mode in operands]
    here = [isinstance(mode, str) for mode in modes]
    in_specs = [
        pl.BlockSpec(memory_space=space[m] if h else pltpu.HBM) for m, h in zip(modes, here)
    ]
    out_specs = [pl.BlockSpec(memory_space=pltpu.HBM if n else pltpu.VMEM) for _, n in results]
    buffers = []
    for array, mode in operands:
        if not isinstance(mode, str):
            buffers += [pltpu.VMEM(array.shape, array.dtype), pltpu.SemaphoreType.DMA((len(mode),))]
    for dims, n in results:
        if n > 0:
            buffers += [pltpu.VMEM(dims, F32), pltpu.SemaphoreType.DMA((n,))]

    def kernel(*refs):
        ins, refs = refs[: len(modes)], refs[len(modes) :]
        outs, refs = refs[: len(results)], list(refs[len(results) :])
        args, loads = [], []
        for ref, mode, h in zip(ins, modes, here):
            if h:
                args.append(Held(ref) if mode == "held" else ref)
            else:
                args.append(Loaded(ref, refs.pop(0), refs.pop(0), mode))
                loads.append(args[-1])
        for i in range(max([len(x.copies) for x in loads], default=0)):
            for x in loads:
                if i < len(x.copies):
                    x.start(i)
        stores = []
        for ref, (_, n) in zip(outs, results):
            if n > 0:
                args.append(Stored(ref, refs.pop(0), refs.pop(0)))
                stores.append(args[-1])
            else:
                args.append(ref if n else Held(ref))
        body(*args, *refs)
        for x in loads:
            x.whole()
        for x in stores:
            x.finish()

    return pl.pallas_call(
        kernel,
        out_shape=[pltpu.HBM(dims, F32) if n else shape(*dims) for dims, n in results],
        in_specs=in_specs,
        out_specs=out_specs,
        scratch_shapes=buffers + list(scratch),
        compiler_params=pltpu.CompilerParams(vmem_limit_bytes=24 << 20),
        cost_estimate=pl.CostEstimate(flops=flops, bytes_accessed=moved, transcendentals=0),
    )(
        *[a if h else pltpu.with_memory_space_constraint(a, pltpu.HBM) for (a, _), h in zip(operands, here)]
    )


def shape(*dims):
    return jax.ShapeDtypeStruct(dims, F32)


def row_index(n=SPAN):
    return lax.broadcasted_iota(jnp.int32, (ROWS, n), 0)


def split(x):
    high = x.astype(BF16)
    return high, (x - high.astype(F32)).astype(BF16)


def one_hot(index, n):
    cell = lax.broadcasted_iota(jnp.int32, (n, NF), 0)
    return jnp.where(cell == index, 1.0, 0.0).astype(BF16)


def at_faces(field, span_hot, row_hot):
    n = field.shape[-1]
    both = jnp.concatenate(split(field.reshape(CH * ROWS, n)), axis=0)
    picked = jnp.dot(both, span_hot, preferred_element_type=F32)
    picked = (picked[: CH * ROWS] + picked[CH * ROWS :]).reshape(CH, ROWS, NF)
    return jnp.sum(picked * row_hot[None], axis=1)


def onto_cells(values, span_hot, row_hot):
    spread = (values[:, None, :] * row_hot[None]).reshape(CH * ROWS, NF)
    both = jnp.concatenate(split(spread), axis=0)
    out = lax.dot_general(both, span_hot, (((1,), (1,)), ((), ())), preferred_element_type=F32)
    return (out[: CH * ROWS] + out[CH * ROWS :]).reshape(CH, ROWS, span_hot.shape[0])


def fluid_hots(ff_ref):
    cell = ff_ref[...]
    span = one_hot(cell & (SPAN - 1), SPAN)
    rows = jnp.where(row_index(NF) == (cell >> 10), 1.0, 0.0)
    return span, rows


def metal_hots(mf_ref):
    cell = mf_ref[...]
    span = one_hot(cell & (MSPAN - 1), MSPAN)
    rows = jnp.where(row_index(NF) == (cell >> 9), 1.0, 0.0)
    return span, rows


def span_sides(a):
    n = a.shape[-1]
    lane = lax.broadcasted_iota(jnp.int32, a.shape, a.ndim - 1)
    north = jnp.where(lane == n - 1, 0.0, pltpu.roll(a, n - 1, a.ndim - 1))
    south = jnp.where(lane == 0, 0.0, pltpu.roll(a, 1, a.ndim - 1))
    return north, south


def stencil_parts(a, before, after):
    row = row_index(a.shape[-1])
    east_one = pltpu.roll(jnp.where(row == 0, after, a), 7, 0)
    east_two = pltpu.roll(jnp.where(row < 2, after, a), 6, 0)
    west_one = pltpu.roll(jnp.where(row == 7, before, a), 1, 0)
    west_two = pltpu.roll(jnp.where(row >= 6, before, a), 2, 0)
    north, south = span_sides(a)
    rest = (
        (4.0 * damping_fourth) * (east_one + west_one)
        - damping_fourth * (east_two + west_two)
        + viscous_coef * (north + south)
        - (6.0 * damping_fourth + 2.0 * viscous_coef + sigma_fluid) * a
    )
    return east_one - west_one, north - south, rest


def edge_tile(ref, tile):
    return jnp.concatenate([ref[2 * tile], ref[2 * tile + 1]], axis=1)


def halo_pair(up_ref, down_ref, t, v):
    tile, slot = (t, v) if v < 4 else (6 + t // 4, t % 4)
    before = pltpu.roll(edge_tile(up_ref, tile), (6 - 2 * slot) % 8, 0)
    after = pltpu.roll(edge_tile(down_ref, tile), (8 - 2 * slot) % 8, 0)
    return before, after


def pack_tile(blocks, tile, up_ref, down_ref):
    row = row_index()
    up = down = None
    for slot, a in enumerate(blocks):
        u = pltpu.roll(a, (2 * slot + 2) % 8, 0) if (2 * slot + 2) % 8 else a
        d = pltpu.roll(a, 2 * slot, 0) if slot else a
        mine = (row >> 1) == slot
        up = u if up is None else jnp.where(mine, u, up)
        down = d if down is None else jnp.where(mine, d, down)
    for half in range(2):
        cut = slice(half * 512, half * 512 + 512)
        up_ref[2 * tile + half] = up[:, cut]
        down_ref[2 * tile + half] = down[:, cut]


def pack_last(get, extra, up_ref, down_ref):
    pack_tile([get(t) for t in range(4)], 6, up_ref, down_ref)
    pack_tile([get(4), get(5), extra, extra], 7, up_ref, down_ref)


def prepare_kernel(a_ref, ps_ref, m_ref, up, down):
    for t in range(6):
        pack_tile([a_ref[t, v] for v in range(4)], t, up.buffer, down.buffer)
        for x in (up, down):
            x.put(pl.ds(2 * t, 2))
    pack_last(lambda t: a_ref[t, NV - 1], ps_ref[...], up.buffer, down.buffer)
    metal_edges(m_ref, up.buffer.at[16], down.buffer.at[16])
    for x in (up, down):
        x.put(pl.ds(12, 5))


def blocks_kernel(a_ref, blocks, sems):
    copies = [
        pltpu.make_async_copy(
            a_ref.at[:, :, :, pl.ds(i * CHUNK, CHUNK)], blocks.at[i], sems.at[i]
        )
        for i in range(8)
    ]
    for copy in copies:
        copy.start()
    for copy in copies:
        copy.wait()


def energy_kernel(tab_ref, m_ref, fc_ref, ff_ref, mf_ref, e):
    first = lax.axis_index("inst") * 6
    m_hot, m_row = metal_hots(mf_ref)
    f_hot, f_row = fluid_hots(ff_ref)
    values = at_faces(m_ref[...], m_hot, m_row) * fc_ref[...]
    cells = onto_cells(values, f_hot, f_row)
    for t in range(6):
        e.buffer[t] = combine(tab_ref, SYNTH, first + t, cells)
        e.put(pl.ds(t, 1))


def combine(tab_ref, base, t, fields):
    total = tab_ref[base + t * CH] * fields[0]
    for ch in range(1, CH):
        if ch != NH:
            total += tab_ref[base + t * CH + ch] * fields[ch]
    return total


def convect(jx_ref, jz_ref, dx, dz, rest, u):
    out = rest
    for v in range(NV):
        out = out - (0.5 * jx_ref[u, v]) * dx[v] - (0.5 * jz_ref[u, v]) * dz[v]
    return out


def first_kernel(
    tab_ref, jx_ref, jz_ref, a_in, s_in, ps_ref, up_ref, down_ref, e_in, fc_ref, ff_ref, m_ref, cond_ref,
    q, b_out, bup, bdown, hq, m_out,
    parts,
):
    first = lax.axis_index("inst") * 6
    step = ps_ref[...]
    step_before = pltpu.roll(edge_tile(up_ref, 7), 2, 0)
    step_after = pltpu.roll(edge_tile(down_ref, 7), 4, 0)
    q_ref, b_ref = q.buffer, b_out.buffer
    for t in range(6):
        a_ref, s_ref, e_ref = a_in.piece(t), s_in.piece(t), e_in.piece(t)
        for v in range(NV):
            a = a_ref[t, v]
            before, after = halo_pair(up_ref, down_ref, t, v)
            dx, dz, rest = stencil_parts(a, before, after)
            parts[0, v], parts[1, v], parts[2, v] = dx, dz, rest
            dx, dz, rest = stencil_parts(step * a, step_before * before, step_after * after)
            parts[3, v], parts[4, v], parts[5, v] = dx, dz, rest
        for i in range(8):
            cut = pl.ds(i * CHUNK, CHUNK)
            dx = [parts[0, v, :, cut] for v in range(NV)]
            dz = [parts[1, v, :, cut] for v in range(NV)]
            px = [parts[3, v, :, cut] for v in range(NV)]
            pz = [parts[4, v, :, cut] for v in range(NV)]
            for u in range(NV):
                a = a_ref[t, u, :, cut]
                space = convect(jx_ref, jz_ref, dx, dz, parts[2, u, :, cut], u)
                source = s_ref[t, u, :, cut] + space
                if u == NV - 1:
                    source = source + e_ref[t, :, cut]
                b = a + ps_ref[:, cut] * source
                b_ref[t, u, :, cut] = b
                q_ref[i, t * NV + u] = a + b + convect(jx_ref, jz_ref, px, pz, parts[5, u, :, cut], u)
        q.put((slice(None), pl.ds(t * NV, NV)))
        b_out.put(pl.ds(t, 1))
        pack_tile([b_ref[t, v] for v in range(4)], t, bup.buffer, bdown.buffer)
    pack_last(lambda t: b_ref[t, NV - 1], step, bup.buffer, bdown.buffer)
    bup.put(slice(None))
    bdown.put(slice(None))
    f_hot, f_row = fluid_hots(ff_ref)
    heat = []
    for ch in range(CH):
        h0 = h1 = h2 = h3 = None
        for t in range(6):
            at = (first + t) * CH + ch
            q4 = jnp.concatenate([q_ref[i, t * NV + NV - 1] for i in range(8)], axis=1)
            a, b = a_in.buffer[t, NV - 1], b_ref[t, NV - 1]
            x0 = tab_ref[W0 + at] * b
            x1 = tab_ref[W1 + at] * a
            x2 = tab_ref[W1 + at] * q4
            x3 = tab_ref[W2 + at] * a
            h0, h1, h2, h3 = (
                (x0, x1, x2, x3) if t == 0 else (h0 + x0, h1 + x1, h2 + x2, h3 + x3)
            )
        heat.append(h0 - step * h1)
        hq.buffer[ch] = step * (step * h3 - h2)
    hq.put(slice(None))
    values = at_faces(jnp.stack(heat), f_hot, f_row) * fc_ref[...]
    for i in range(8):
        for k in range(4):
            q_ref[i, 30 + k] = values[:, k * CHUNK : (k + 1) * CHUNK]
    q.put((slice(None), pl.ds(30, 4)))
    before, after = metal_sides(up_ref.at[16], down_ref.at[16])
    m = metal_update(m_ref, before, after, cond_ref[...])
    for ch in range(CH):
        m_out.buffer[ch] = m[ch]
    m_out.put(slice(None))


def rotate_time(kron, x):
    high, low = split(x)
    return jnp.dot(kron, jnp.concatenate([high, low, high], axis=0), preferred_element_type=F32)


def local_step(ps_ref):
    start = pl.multiple_of(lax.axis_index("inst") * CHUNK, CHUNK)
    return ps_ref[:, pl.ds(start, CHUNK)]


def turned(get):
    return jnp.concatenate(
        [
            jnp.concatenate([get(j, t, v) for j in range(8) for t in range(6)], axis=0)
            for v in range(NV)
        ],
        axis=1,
    )


def derive_kernel(kron_ref, a_ref, ps_ref, g):
    wide = jnp.concatenate([local_step(ps_ref)] * NV, axis=1)
    x = turned(lambda j, t, v: a_ref[j, t, v])
    d = rotate_time(kron_ref[...], x)
    g.buffer[...] = (d.reshape(NT, ROWS, NV * CHUNK) * wide[None]).reshape(NT * ROWS, NV * CHUNK)
    g.put(slice(None))


def middle_kernel(
    tab_ref, jx_ref, jz_ref, b_in, s_in, ps_ref, up_ref, down_ref, hq_in, g_ref,
    c_out, hc,
    parts,
):
    first = lax.axis_index("inst") * 6
    c_ref = c_out.buffer
    for t in range(6):
        b_ref, s_ref = b_in.piece(t), s_in.piece(t)
        for v in range(NV):
            before, after = halo_pair(up_ref, down_ref, t, v)
            dx, dz, rest = stencil_parts(b_ref[t, v], before, after)
            parts[0, v], parts[1, v], parts[2, v] = dx, dz, rest
        for i in range(8):
            cut = pl.ds(i * CHUNK, CHUNK)
            dx = [parts[0, v, :, cut] for v in range(NV)]
            dz = [parts[1, v, :, cut] for v in range(NV)]
            for u in range(NV):
                space = convect(jx_ref, jz_ref, dx, dz, parts[2, u, :, cut], u)
                c_ref[t, u, :, cut] = b_ref[t, u, :, cut] + ps_ref[:, cut] * (s_ref[t, u, :, cut] + space)
        c_out.put(pl.ds(t, 1))
    hq_ref = hq_in.whole()
    for ch in range(CH):
        total = hq_ref[ch]
        for t in range(6):
            total += tab_ref[W0 + (first + t) * CH + ch] * c_ref[t, NV - 1]
        hc.buffer[ch] = total
    hc.put(slice(None))


def metal_update(m, before, after, cond):
    row = row_index(MSPAN)
    out = []
    for ch in range(CH):
        a = m[ch]
        east = pltpu.roll(jnp.where(row == 0, after[ch], a), 7, 0)
        west = pltpu.roll(jnp.where(row == 7, before[ch], a), 1, 0)
        north, south = span_sides(a)
        laplace = east + west + north + south - 4.0 * a
        h = ch % NH
        turn = -heat_capacity * h * m[ch + NH] if ch < NH else heat_capacity * h * m[ch - NH]
        out.append(a + metal_step * (cond * laplace - sigma_metal * a - turn))
    return out


def metal_edges(m, up_ref, down_ref):
    up_ref[...] = jnp.concatenate([m[ch][7:8] for ch in range(CH)], axis=0)
    down_ref[...] = jnp.concatenate([m[ch][0:1] for ch in range(CH)], axis=0)


def metal_sides(up_ref, down_ref):
    before = [jnp.broadcast_to(up_ref[ch : ch + 1], (ROWS, MSPAN)) for ch in range(CH)]
    after = [jnp.broadcast_to(down_ref[ch : ch + 1], (ROWS, MSPAN)) for ch in range(CH)]
    return before, after


def heat_sum(blocks_ref):
    tiles = []
    for k in range(4):
        total = blocks_ref[0, 30 + k]
        for j in range(1, 8):
            total += blocks_ref[j, 30 + k]
        tiles.append(total)
    return jnp.concatenate(tiles, axis=1)


def second_kernel(
    tab_ref, q, g, kron, ps_ref, m_in, fc_ref, ff_ref, mf_ref, hc,
    v, m_out, mup, mdown, e,
):
    first = lax.axis_index("inst") * 6
    step = ps_ref[...]
    coeff = fc_ref[...]
    m_hot, m_row = metal_hots(mf_ref)
    f_hot, f_row = fluid_hots(ff_ref)
    q_ref, v_ref = q.whole(), v.buffer
    source = onto_cells(heat_sum(q_ref), m_hot, m_row)
    m_ref = m_in.whole()
    m = [m_ref[ch] + metal_step * source[ch] for ch in range(CH)]
    for ch in range(CH):
        m_out.buffer[ch] = m[ch]
    m_out.put(slice(None))
    metal_edges(m, mup.buffer, mdown.buffer)
    mup.put(slice(None))
    mdown.put(slice(None))
    cells = onto_cells(at_faces(jnp.stack(m), m_hot, m_row) * coeff, f_hot, f_row)
    for t in range(6):
        e.buffer[t] = step * combine(tab_ref, SYNTH, first + t, cells)
    e.put(slice(None))
    hc_ref = hc.whole()
    heat = []
    for ch in range(CH):
        total = hc_ref[ch]
        for t in range(6):
            total += tab_ref[W0 + (first + t) * CH + ch] * e.buffer[t]
        heat.append(total)
    values = at_faces(jnp.stack(heat), f_hot, f_row) * coeff
    for i in range(8):
        for k in range(4):
            v_ref[i, 30 + k] = values[:, k * CHUNK : (k + 1) * CHUNK]
    x = turned(lambda j, t, u: q_ref[j, t * NV + u]) - g.whole()[...]
    kron_ref = kron.whole()
    minus = -local_step(ps_ref)
    for half in range(2):
        d = rotate_time(kron_ref[pl.ds(half * 192, 192), :], x)
        for j in range(4):
            for t in range(6):
                at = (j * 6 + t) * ROWS
                for u in range(NV):
                    v_ref[half * 4 + j, t * NV + u] = minus * d[at : at + ROWS, u * CHUNK : (u + 1) * CHUNK]
        v.put(pl.ds(half * 4, 4))


def last_kernel(v, c, e, m_in, mup_ref, mdown_ref, cond_ref, mf_ref, out, m_out):
    for t in range(6):
        v_ref, c_ref, e_ref = v.piece(t), c.piece(t), e.whole()
        for i in range(8):
            cut = pl.ds(i * CHUNK, CHUNK)
            for u in range(NV):
                total = c_ref[t, u, :, cut] + v_ref[i, t * NV + u]
                if u == NV - 1:
                    total = total + e_ref[t, :, cut]
                out.buffer[t, u, :, cut] = total
        out.put(pl.ds(t, 1))
    m_hot, m_row = metal_hots(mf_ref)
    source = onto_cells(heat_sum(v.whole()), m_hot, m_row)
    before, after = metal_sides(mup_ref, mdown_ref)
    m = metal_update(m_in.whole(), before, after, cond_ref[...])
    for ch in range(CH):
        m_out.buffer[ch] = m[ch] + metal_step * source[ch]
    m_out.put(slice(None))


def exchange(up, down):
    n = lax.axis_size("space")
    forward = [(i, (i + 1) % n) for i in range(n)]
    back = [(j, i) for i, j in forward]
    return lax.ppermute(up, "space", forward), lax.ppermute(down, "space", back)


def turn(x):
    return lax.all_to_all(x, "inst", 0, 0, tiled=True)


SIX = by_piece(6)
EDGES = (17, ROWS, 512)
FLUID = (6, NV, ROWS, SPAN)
METAL = (CH, ROWS, MSPAN)
BLOCKS = (8, 34, ROWS, CHUNK)


LONG = 1 << 36


def plain(*arrays):
    return [(array, "vmem") for array in arrays]


def held(*arrays):
    return [(array, "held") for array in arrays]


def local(a0, source, ps, jx, jz, metal, cond, coeff, ff, mf):
    kron = jnp.asarray(KRON)
    tab = jnp.asarray(FLAT)
    coeff, ff, mf = (x.reshape(1, NF) for x in (coeff, ff, mf))
    metal = metal.reshape(METAL)
    up, down = call(prepare_kernel, plain(a0, ps, metal), [(EDGES, 7), (EDGES, 7)])
    up, down = exchange(up, down)
    (blocks,) = call(
        blocks_kernel,
        plain(a0),
        [((8, 6, NV, ROWS, CHUNK), -1)],
        scratch=[pltpu.SemaphoreType.DMA((8,))],
    )
    a_turned = turn(blocks)
    scalars = [(tab, "smem"), (jx, "smem"), (jz, "smem")]
    (e0,) = call(
        energy_kernel, scalars[:1] + plain(metal, coeff, ff, mf), [((6, ROWS, SPAN), 6)]
    )
    q, b, bup, bdown, hq, metal = call(
        first_kernel,
        scalars + held(a0, source) + plain(ps, up, down) + held(e0) + plain(coeff, ff, metal, cond),
        [(BLOCKS, 7), (FLUID, 6), (EDGES, 1), (EDGES, 1), ((CH, ROWS, SPAN), 1), (METAL, 1)],
        scratch=[pltpu.VMEM((6, NV, ROWS, SPAN), F32)],
        flops=LONG,
    )
    q_turned = turn(q)
    bup, bdown = exchange(bup, bdown)
    (g,) = call(derive_kernel, plain(kron, a_turned, ps), [((NT * ROWS, NV * CHUNK), 0)])
    c, hc = call(
        middle_kernel,
        scalars + held(b, source) + plain(ps, bup, bdown) + held(hq) + plain(g),
        [(FLUID, 0), ((CH, ROWS, SPAN), 0)],
        scratch=[pltpu.VMEM((3, NV, ROWS, SPAN), F32)],
        flops=LONG,
    )
    v, metal, mup, mdown, e1 = call(
        second_kernel,
        scalars[:1] + held(q_turned, g) + [(kron, WHOLE)] + plain(ps) + held(metal)
        + plain(coeff, ff, mf) + held(hc),
        [(BLOCKS, 2), (METAL, 1), ((CH, MSPAN), 1), ((CH, MSPAN), 1), ((6, ROWS, SPAN), 1)],
    )
    v = turn(v)
    mup, mdown = exchange(mup, mdown)
    out, metal = call(
        last_kernel, held(v, c, e1, metal) + plain(mup, mdown, cond, mf), [(FLUID, 6), (METAL, 1)]
    )
    return out, metal.reshape(2, NH, ROWS, MSPAN)


def solution(mesh):
    return jax.shard_map(
        local,
        mesh=mesh,
        in_specs=(
            P("inst", None, "space", None),
            P("inst", None, "space", None),
            P("space", None),
            P(),
            P(),
            P(None, None, "space", None),
            P("space", None),
            P("space"),
            P("space"),
            P("space"),
        ),
        out_specs=(P("inst", None, "space", None), P(None, None, "space", None)),
        check_vma=False,
    )
```

```python
import math

import jax
import jax.numpy as jnp
import ml_dtypes
import numpy as np
from jax import lax
from jax.experimental import pallas as pl
from jax.experimental.pallas import tpu as pltpu
from jax.sharding import PartitionSpec as P

NT, NV, NH = 48, 5, 4
ROWS, SPAN, MSPAN, NF = 8, 1024, 512, 512
CHUNK = 128
CH = 2 * NH
F32, BF16 = jnp.float32, jnp.bfloat16

damping_fourth = 1.0 / 32.0
viscous_coef = 0.1
sigma_fluid = 0.5
metal_step = 0.2
sigma_metal = 0.5
heat_capacity = 0.5
flux_scale = 4.0


def tables():
    t = np.arange(NT)
    offset = t[:, None] - t[None, :]
    angle = np.where(offset == 0, 0.5, math.pi * offset / NT)
    spectral = np.where(
        offset == 0, 0.0, 0.5 * (1.0 - 2.0 * (offset % 2)) * np.cos(angle) / np.sin(angle)
    )
    phase = 2.0 * math.pi * ((np.arange(NH)[:, None] * t[None, :]) % NT) / NT
    synth = np.concatenate([np.cos(phase), -np.sin(phase)])
    w0 = synth * (flux_scale / NT)
    w1 = w0 @ spectral
    w2 = w1 @ spectral
    high = spectral.astype(np.float32).astype(ml_dtypes.bfloat16)
    low = (spectral - high.astype(np.float64)).astype(np.float32).astype(ml_dtypes.bfloat16)
    eye = np.eye(ROWS, dtype=np.float32)
    kron_high = np.kron(high.astype(np.float32), eye)
    kron_low = np.kron(low.astype(np.float32), eye)
    kron = np.concatenate([kron_high, kron_high, kron_low], axis=1).astype(ml_dtypes.bfloat16)
    flat = np.concatenate([m.T.reshape(-1) for m in (synth, w0, w1, w2)]).astype(np.float32)
    return kron, flat


KRON, FLAT = tables()
SYNTH, W0, W1, W2 = (i * NT * CH for i in range(4))


class Loaded:
    def __init__(self, source, buffer, sems, cut):
        self.buffer, self.copies = buffer, []
        for i, index in enumerate(cut):
            self.copies.append(pltpu.make_async_copy(source.at[index], buffer.at[index], sems.at[i]))
        self.waiting = set(range(len(cut)))

    def start(self, i):
        self.copies[i].start()

    def piece(self, i):
        if i in self.waiting:
            self.waiting.remove(i)
            self.copies[i].wait()
        return self.buffer

    def whole(self):
        for i in range(len(self.copies)):
            self.piece(i)
        return self.buffer


class Held:
    def __init__(self, ref):
        self.buffer = ref

    def piece(self, i):
        return self.buffer

    def whole(self):
        return self.buffer

    def put(self, index):
        pass


class Stored:
    def __init__(self, target, buffer, sems):
        self.target, self.buffer, self.sems, self.copies = target, buffer, sems, []

    def put(self, index):
        copy = pltpu.make_async_copy(
            self.buffer.at[index], self.target.at[index], self.sems.at[len(self.copies)]
        )
        copy.start()
        self.copies.append(copy)

    def finish(self):
        for copy in self.copies:
            copy.wait()


WHOLE = (slice(None),)


def by_piece(n):
    return tuple(pl.ds(i, 1) for i in range(n))


def call(body, operands, results, scratch=(), flops=1 << 20, moved=1 << 20):
    space = {"smem": pltpu.SMEM, "vmem": pltpu.VMEM, "held": pltpu.VMEM}
    modes = [mode for _, mode in operands]
    here = [isinstance(mode, str) for mode in modes]
    in_specs = [
        pl.BlockSpec(memory_space=space[m] if h else pltpu.HBM) for m, h in zip(modes, here)
    ]
    out_specs = [pl.BlockSpec(memory_space=pltpu.HBM if n else pltpu.VMEM) for _, n in results]
    buffers = []
    for array, mode in operands:
        if not isinstance(mode, str):
            buffers += [pltpu.VMEM(array.shape, array.dtype), pltpu.SemaphoreType.DMA((len(mode),))]
    for dims, n in results:
        if n > 0:
            buffers += [pltpu.VMEM(dims, F32), pltpu.SemaphoreType.DMA((n,))]

    def kernel(*refs):
        ins, refs = refs[: len(modes)], refs[len(modes) :]
        outs, refs = refs[: len(results)], list(refs[len(results) :])
        args, loads = [], []
        for ref, mode, h in zip(ins, modes, here):
            if h:
                args.append(Held(ref) if mode == "held" else ref)
            else:
                args.append(Loaded(ref, refs.pop(0), refs.pop(0), mode))
                loads.append(args[-1])
        for i in range(max([len(x.copies) for x in loads], default=0)):
            for x in loads:
                if i < len(x.copies):
                    x.start(i)
        stores = []
        for ref, (_, n) in zip(outs, results):
            if n > 0:
                args.append(Stored(ref, refs.pop(0), refs.pop(0)))
                stores.append(args[-1])
            else:
                args.append(ref if n else Held(ref))
        body(*args, *refs)
        for x in loads:
            x.whole()
        for x in stores:
            x.finish()

    return pl.pallas_call(
        kernel,
        out_shape=[pltpu.HBM(dims, F32) if n else shape(*dims) for dims, n in results],
        in_specs=in_specs,
        out_specs=out_specs,
        scratch_shapes=buffers + list(scratch),
        compiler_params=pltpu.CompilerParams(vmem_limit_bytes=24 << 20),
        cost_estimate=pl.CostEstimate(flops=flops, bytes_accessed=moved, transcendentals=0),
    )(
        *[a if h else pltpu.with_memory_space_constraint(a, pltpu.HBM) for (a, _), h in zip(operands, here)]
    )


def shape(*dims):
    return jax.ShapeDtypeStruct(dims, F32)


def row_index(n=SPAN):
    return lax.broadcasted_iota(jnp.int32, (ROWS, n), 0)


def split(x):
    high = x.astype(BF16)
    return high, (x - high.astype(F32)).astype(BF16)


def one_hot(index, n):
    cell = lax.broadcasted_iota(jnp.int32, (n, NF), 0)
    return jnp.where(cell == index, 1.0, 0.0).astype(BF16)


def at_faces(field, span_hot, row_hot):
    n = field.shape[-1]
    both = jnp.concatenate(split(field.reshape(CH * ROWS, n)), axis=0)
    picked = jnp.dot(both, span_hot, preferred_element_type=F32)
    picked = (picked[: CH * ROWS] + picked[CH * ROWS :]).reshape(CH, ROWS, NF)
    return jnp.sum(picked * row_hot[None], axis=1)


def onto_cells(values, span_hot, row_hot):
    spread = (values[:, None, :] * row_hot[None]).reshape(CH * ROWS, NF)
    both = jnp.concatenate(split(spread), axis=0)
    out = lax.dot_general(both, span_hot, (((1,), (1,)), ((), ())), preferred_element_type=F32)
    return (out[: CH * ROWS] + out[CH * ROWS :]).reshape(CH, ROWS, span_hot.shape[0])


def fluid_hots(ff_ref):
    cell = ff_ref[...]
    span = one_hot(cell & (SPAN - 1), SPAN)
    rows = jnp.where(row_index(NF) == (cell >> 10), 1.0, 0.0)
    return span, rows


def metal_hots(mf_ref):
    cell = mf_ref[...]
    span = one_hot(cell & (MSPAN - 1), MSPAN)
    rows = jnp.where(row_index(NF) == (cell >> 9), 1.0, 0.0)
    return span, rows


def span_sides(a):
    n = a.shape[-1]
    lane = lax.broadcasted_iota(jnp.int32, a.shape, a.ndim - 1)
    north = jnp.where(lane == n - 1, 0.0, pltpu.roll(a, n - 1, a.ndim - 1))
    south = jnp.where(lane == 0, 0.0, pltpu.roll(a, 1, a.ndim - 1))
    return north, south


def stencil_parts(a, before, after):
    row = row_index(a.shape[-1])
    east_one = pltpu.roll(jnp.where(row == 0, after, a), 7, 0)
    east_two = pltpu.roll(jnp.where(row < 2, after, a), 6, 0)
    west_one = pltpu.roll(jnp.where(row == 7, before, a), 1, 0)
    west_two = pltpu.roll(jnp.where(row >= 6, before, a), 2, 0)
    north, south = span_sides(a)
    rest = (
        (4.0 * damping_fourth) * (east_one + west_one)
        - damping_fourth * (east_two + west_two)
        + viscous_coef * (north + south)
        - (6.0 * damping_fourth + 2.0 * viscous_coef + sigma_fluid) * a
    )
    return east_one - west_one, north - south, rest


def edge_tile(ref, tile):
    return jnp.concatenate([ref[2 * tile], ref[2 * tile + 1]], axis=1)


def halo_pair(up_ref, down_ref, t, v):
    tile, slot = (t, v) if v < 4 else (6 + t // 4, t % 4)
    before = pltpu.roll(edge_tile(up_ref, tile), (6 - 2 * slot) % 8, 0)
    after = pltpu.roll(edge_tile(down_ref, tile), (8 - 2 * slot) % 8, 0)
    return before, after


def pack_tile(blocks, tile, up_ref, down_ref):
    row = row_index()
    up = down = None
    for slot, a in enumerate(blocks):
        u = pltpu.roll(a, (2 * slot + 2) % 8, 0) if (2 * slot + 2) % 8 else a
        d = pltpu.roll(a, 2 * slot, 0) if slot else a
        mine = (row >> 1) == slot
        up = u if up is None else jnp.where(mine, u, up)
        down = d if down is None else jnp.where(mine, d, down)
    for half in range(2):
        cut = slice(half * 512, half * 512 + 512)
        up_ref[2 * tile + half] = up[:, cut]
        down_ref[2 * tile + half] = down[:, cut]


def pack_last(get, extra, up_ref, down_ref):
    pack_tile([get(t) for t in range(4)], 6, up_ref, down_ref)
    pack_tile([get(4), get(5), extra, extra], 7, up_ref, down_ref)


def prepare_kernel(a, ps, m_in, up, down):
    for t in range(6):
        ref = a.piece(t)
        pack_tile([ref[t, v] for v in range(4)], t, up.buffer, down.buffer)
        for x in (up, down):
            x.put(pl.ds(2 * t, 2))
    pack_last(lambda t: a.buffer[t, NV - 1], ps.whole()[...], up.buffer, down.buffer)
    metal_edges(m_in.whole(), up.buffer.at[16], down.buffer.at[16])
    for x in (up, down):
        x.put(pl.ds(12, 5))


def energy_kernel(tab_ref, m_ref, fc_ref, ff_ref, mf_ref, e):
    first = lax.axis_index("inst") * 6
    m_hot, m_row = metal_hots(mf_ref)
    f_hot, f_row = fluid_hots(ff_ref)
    values = at_faces(m_ref[...], m_hot, m_row) * fc_ref[...]
    cells = onto_cells(values, f_hot, f_row)
    for t in range(6):
        e.buffer[t] = combine(tab_ref, SYNTH, first + t, cells)
        e.put(pl.ds(t, 1))


def combine(tab_ref, base, t, fields):
    total = tab_ref[base + t * CH] * fields[0]
    for ch in range(1, CH):
        if ch != NH:
            total += tab_ref[base + t * CH + ch] * fields[ch]
    return total


def convect(jx_ref, jz_ref, dx, dz, rest, u):
    out = rest
    for v in range(NV):
        out = out - (0.5 * jx_ref[u, v]) * dx[v] - (0.5 * jz_ref[u, v]) * dz[v]
    return out


def inner_kernel(jx_ref, jz_ref, a_ref, s_ref, ps_ref, e_ref, b, q, parts):
    step = ps_ref[...]
    for t in range(6):
        for v in range(NV):
            a = a_ref[t, v]
            dx, dz, rest = stencil_parts(a, 0.0, 0.0)
            parts[0, v], parts[1, v], parts[2, v] = dx, dz, rest
            dx, dz, rest = stencil_parts(step * a, 0.0, 0.0)
            parts[3, v], parts[4, v], parts[5, v] = dx, dz, rest
        for i in range(8):
            cut = pl.ds(i * CHUNK, CHUNK)
            dx = [parts[0, v, :, cut] for v in range(NV)]
            dz = [parts[1, v, :, cut] for v in range(NV)]
            px = [parts[3, v, :, cut] for v in range(NV)]
            pz = [parts[4, v, :, cut] for v in range(NV)]
            for u in range(NV):
                a = a_ref[t, u, :, cut]
                space = convect(jx_ref, jz_ref, dx, dz, parts[2, u, :, cut], u)
                source = s_ref[t, u, :, cut] + space
                if u == NV - 1:
                    source = source + e_ref[t, :, cut]
                inner = a + ps_ref[:, cut] * source
                b.buffer[t, u, :, cut] = inner
                q.buffer[t, u, :, cut] = a + inner + convect(jx_ref, jz_ref, px, pz, parts[5, u, :, cut], u)


def edge_terms(up_ref, down_ref, half, t, v):
    tile, slot = (t, v) if v < 4 else (6 + t // 4, t % 4)
    row = row_index(512)
    up, down = up_ref[2 * tile + half], down_ref[2 * tile + half]
    east_one = pltpu.roll(down, (7 - 2 * slot) % 8, 0)
    west_one = pltpu.roll(up, (7 - 2 * slot) % 8, 0)
    east_two = pltpu.roll(down, (6 - 2 * slot) % 8, 0)
    west_two = pltpu.roll(up, (8 - 2 * slot) % 8, 0)
    one = jnp.where(row == 7, east_one, jnp.where(row == 0, west_one, 0.0))
    two = jnp.where(row >= 6, east_two, jnp.where(row < 2, west_two, 0.0))
    return one, two


def first_kernel(
    tab_ref, jx_ref, jz_ref, a_ref, bi_ref, qi_ref, ps_ref, up_ref, down_ref, fc_ref, ff_ref, m_ref, cond_ref,
    q, b_out, bup, bdown, hq, m_out,
    q4_ref, sems,
):
    first = lax.axis_index("inst") * 6
    copies = [
        pltpu.make_async_copy(
            a_ref.at[:, :, :, pl.ds(i * CHUNK, CHUNK)], q.target.at[i, pl.ds(6, 6)], sems.at[i]
        )
        for i in range(8)
    ]
    for copy in copies:
        copy.start()
    step = ps_ref[...]
    q_ref, b_ref = q.buffer, b_out.buffer
    sign = jnp.where(row_index(512) == 0, 0.5, -0.5)
    step_edges = []
    for half in range(2):
        tile = 14 + half
        row = row_index(512)
        up, down = up_ref[tile], down_ref[tile]
        one = jnp.where(row == 7, pltpu.roll(down, 3, 0), pltpu.roll(up, 3, 0))
        two = jnp.where(row >= 6, pltpu.roll(down, 2, 0), pltpu.roll(up, 4, 0))
        step_edges.append((one, two))
    for t in range(6):
        for half in range(2):
            wide = pl.ds(half * 512, 512)
            here = ps_ref[:, wide]
            step_one, step_two = step_edges[half]
            edges = [edge_terms(up_ref, down_ref, half, t, v) for v in range(NV)]
            for u in range(NV):
                total = jx_ref[u, 0] * edges[0][0]
                for v in range(1, NV):
                    total += jx_ref[u, v] * edges[v][0]
                one = sign * total + (4.0 * damping_fourth) * edges[u][0]
                two = damping_fourth * edges[u][1]
                change = here * (one - two)
                b_ref[t, u, :, wide] = bi_ref[t, u, :, wide] + change
                value = qi_ref[t, u, :, wide] + change + (step_one * one - step_two * two)
                for i in range(4):
                    q_ref[4 * half + i, t, u] = value[:, i * CHUNK : (i + 1) * CHUNK]
                if u == NV - 1:
                    q4_ref[t, :, wide] = value
        q.put((slice(None), pl.ds(t, 1)))
        b_out.put(pl.ds(t, 1))
        pack_tile([b_ref[t, v] for v in range(4)], t, bup.buffer, bdown.buffer)
    pack_last(lambda t: b_ref[t, NV - 1], step, bup.buffer, bdown.buffer)
    bup.put(slice(None))
    bdown.put(slice(None))
    f_hot, f_row = fluid_hots(ff_ref)
    heat = []
    for ch in range(CH):
        h0 = h1 = h2 = h3 = None
        for t in range(6):
            at = (first + t) * CH + ch
            a, b = a_ref[t, NV - 1], b_ref[t, NV - 1]
            x0 = tab_ref[W0 + at] * b
            x1 = tab_ref[W1 + at] * a
            x2 = tab_ref[W1 + at] * q4_ref[t]
            x3 = tab_ref[W2 + at] * a
            h0, h1, h2, h3 = (
                (x0, x1, x2, x3) if t == 0 else (h0 + x0, h1 + x1, h2 + x2, h3 + x3)
            )
        heat.append(h0 - step * h1)
        hq.buffer[ch] = step * (step * h3 - h2)
    hq.put(slice(None))
    values = at_faces(jnp.stack(heat), f_hot, f_row) * fc_ref[...]
    for i in range(8):
        for k in range(4):
            q_ref[i, 12, k] = values[:, k * CHUNK : (k + 1) * CHUNK]
        q_ref[i, 12, 4] = jnp.zeros((ROWS, CHUNK), F32)
    q.put((slice(None), pl.ds(12, 1)))
    before, after = metal_sides(up_ref.at[16], down_ref.at[16])
    m = metal_update(m_ref, before, after, cond_ref[...])
    for ch in range(CH):
        m_out.buffer[ch] = m[ch]
    m_out.put(slice(None))
    for copy in copies:
        copy.wait()


def rotate_time(kron, x):
    high, low = split(x)
    return jnp.dot(kron, jnp.concatenate([high, low, high], axis=0), preferred_element_type=F32)


def local_step(ps_ref):
    start = pl.multiple_of(lax.axis_index("inst") * CHUNK, CHUNK)
    return ps_ref[:, pl.ds(start, CHUNK)]


def turned(get):
    return jnp.concatenate(
        [
            jnp.concatenate([get(j, t, v) for j in range(8) for t in range(6)], axis=0)
            for v in range(NV)
        ],
        axis=1,
    )


def middle_kernel(
    tab_ref, jx_ref, jz_ref, b_in, s_in, ps_ref, up_ref, down_ref, hq_in,
    c_out, hc,
    parts,
):
    first = lax.axis_index("inst") * 6
    c_ref = c_out.buffer
    for t in range(6):
        b_ref, s_ref = b_in.piece(t), s_in.piece(t)
        for v in range(NV):
            before, after = halo_pair(up_ref, down_ref, t, v)
            dx, dz, rest = stencil_parts(b_ref[t, v], before, after)
            parts[0, v], parts[1, v], parts[2, v] = dx, dz, rest
        for i in range(8):
            cut = pl.ds(i * CHUNK, CHUNK)
            dx = [parts[0, v, :, cut] for v in range(NV)]
            dz = [parts[1, v, :, cut] for v in range(NV)]
            for u in range(NV):
                space = convect(jx_ref, jz_ref, dx, dz, parts[2, u, :, cut], u)
                c_ref[t, u, :, cut] = b_ref[t, u, :, cut] + ps_ref[:, cut] * (s_ref[t, u, :, cut] + space)
        c_out.put(pl.ds(t, 1))
    hq_ref = hq_in.whole()
    for ch in range(CH):
        total = hq_ref[ch]
        for t in range(6):
            total += tab_ref[W0 + (first + t) * CH + ch] * c_ref[t, NV - 1]
        hc.buffer[ch] = total
    hc.put(slice(None))


def metal_update(m, before, after, cond):
    row = row_index(MSPAN)
    out = []
    for ch in range(CH):
        a = m[ch]
        east = pltpu.roll(jnp.where(row == 0, after[ch], a), 7, 0)
        west = pltpu.roll(jnp.where(row == 7, before[ch], a), 1, 0)
        north, south = span_sides(a)
        laplace = east + west + north + south - 4.0 * a
        h = ch % NH
        turn = -heat_capacity * h * m[ch + NH] if ch < NH else heat_capacity * h * m[ch - NH]
        out.append(a + metal_step * (cond * laplace - sigma_metal * a - turn))
    return out


def metal_edges(m, up_ref, down_ref):
    up_ref[...] = jnp.concatenate([m[ch][7:8] for ch in range(CH)], axis=0)
    down_ref[...] = jnp.concatenate([m[ch][0:1] for ch in range(CH)], axis=0)


def metal_sides(up_ref, down_ref):
    before = [jnp.broadcast_to(up_ref[ch : ch + 1], (ROWS, MSPAN)) for ch in range(CH)]
    after = [jnp.broadcast_to(down_ref[ch : ch + 1], (ROWS, MSPAN)) for ch in range(CH)]
    return before, after


def heat_sum(get):
    tiles = []
    for k in range(4):
        total = get(0, k)
        for j in range(1, 8):
            total += get(j, k)
        tiles.append(total)
    return jnp.concatenate(tiles, axis=1)


def second_kernel(
    tab_ref, q_ref, kron_ref, ps_ref, m_ref, fc_ref, ff_ref, mf_ref, hc_ref,
    v, m_out, mup, mdown, e,
):
    first = lax.axis_index("inst") * 6
    v_ref = v.buffer
    near = local_step(ps_ref)
    wide = jnp.concatenate([near] * NV, axis=1)[None]
    d = rotate_time(kron_ref[...], turned(lambda j, t, u: q_ref[j, 6 + t, u]))
    d = (d.reshape(NT, ROWS, NV * CHUNK) * wide).reshape(NT * ROWS, NV * CHUNK)
    x = turned(lambda j, t, u: q_ref[j, t, u]) - d
    for half in range(2):
        d = rotate_time(kron_ref[pl.ds(half * 192, 192), :], x)
        for j in range(4):
            for t in range(6):
                at = (j * 6 + t) * ROWS
                for u in range(NV):
                    v_ref[half * 4 + j, t * NV + u] = -near * d[at : at + ROWS, u * CHUNK : (u + 1) * CHUNK]
        v.put((pl.ds(half * 4, 4), pl.ds(0, 30)))
    step = ps_ref[...]
    coeff = fc_ref[...]
    m_hot, m_row = metal_hots(mf_ref)
    f_hot, f_row = fluid_hots(ff_ref)
    source = onto_cells(heat_sum(lambda j, k: q_ref[j, 12, k]), m_hot, m_row)
    m = [m_ref[ch] + metal_step * source[ch] for ch in range(CH)]
    for ch in range(CH):
        m_out.buffer[ch] = m[ch]
    m_out.put(slice(None))
    metal_edges(m, mup.buffer, mdown.buffer)
    mup.put(slice(None))
    mdown.put(slice(None))
    cells = onto_cells(at_faces(jnp.stack(m), m_hot, m_row) * coeff, f_hot, f_row)
    for t in range(6):
        e.buffer[t] = step * combine(tab_ref, SYNTH, first + t, cells)
    e.put(slice(None))
    heat = []
    for ch in range(CH):
        total = hc_ref[ch]
        for t in range(6):
            total += tab_ref[W0 + (first + t) * CH + ch] * e.buffer[t]
        heat.append(total)
    values = at_faces(jnp.stack(heat), f_hot, f_row) * coeff
    for i in range(8):
        for k in range(4):
            v_ref[i, 30 + k] = values[:, k * CHUNK : (k + 1) * CHUNK]
    v.put((slice(None), pl.ds(30, 4)))


def last_kernel(v, c, e, m_in, mup_ref, mdown_ref, cond_ref, mf_ref, out, m_out):
    for t in range(6):
        v_ref, c_ref, e_ref = v.piece(t), c.piece(t), e.whole()
        for i in range(8):
            cut = pl.ds(i * CHUNK, CHUNK)
            for u in range(NV):
                total = c_ref[t, u, :, cut] + v_ref[i, t * NV + u]
                if u == NV - 1:
                    total = total + e_ref[t, :, cut]
                out.buffer[t, u, :, cut] = total
        out.put(pl.ds(t, 1))
    m_hot, m_row = metal_hots(mf_ref)
    source = onto_cells(heat_sum(lambda j, k: v.buffer[j, 30 + k]), m_hot, m_row)
    before, after = metal_sides(mup_ref, mdown_ref)
    m = metal_update(m_in.whole(), before, after, cond_ref[...])
    for ch in range(CH):
        m_out.buffer[ch] = m[ch] + metal_step * source[ch]
    m_out.put(slice(None))


def exchange(up, down):
    n = lax.axis_size("space")
    forward = [(i, (i + 1) % n) for i in range(n)]
    back = [(j, i) for i, j in forward]
    return lax.ppermute(up, "space", forward), lax.ppermute(down, "space", back)


def turn(x):
    return lax.all_to_all(x, "inst", 0, 0, tiled=True)


SIX = by_piece(6)
EDGES = (17, ROWS, 512)
FLUID = (6, NV, ROWS, SPAN)
METAL = (CH, ROWS, MSPAN)
BLOCKS = (8, 34, ROWS, CHUNK)


LONG = 1 << 36


def plain(*arrays):
    return [(array, "vmem") for array in arrays]


def held(*arrays):
    return [(array, "held") for array in arrays]


def local(a0, source, ps, jx, jz, metal, cond, coeff, ff, mf):
    kron = jnp.asarray(KRON)
    tab = jnp.asarray(FLAT)
    coeff, ff, mf = (x.reshape(1, NF) for x in (coeff, ff, mf))
    metal = metal.reshape(METAL)
    up, down = call(
        prepare_kernel, [(a0, SIX), (ps, WHOLE), (metal, WHOLE)], [(EDGES, 7), (EDGES, 7)]
    )
    up, down = exchange(up, down)
    scalars = [(tab, "smem"), (jx, "smem"), (jz, "smem")]
    (e0,) = call(
        energy_kernel, scalars[:1] + plain(metal, coeff, ff, mf), [((6, ROWS, SPAN), 0)]
    )
    b, q = call(
        inner_kernel,
        scalars[1:] + plain(a0, source, ps, e0),
        [(FLUID, 0), (FLUID, 0)],
        scratch=[pltpu.VMEM((6, NV, ROWS, SPAN), F32)],
    )
    q, b, bup, bdown, hq, metal = call(
        first_kernel,
        scalars + plain(a0, b, q, ps, up, down, coeff, ff, metal, cond),
        [((8, 13, NV, ROWS, CHUNK), 7), (FLUID, 6), (EDGES, 1), (EDGES, 1), ((CH, ROWS, SPAN), 1), (METAL, 1)],
        scratch=[pltpu.VMEM((6, ROWS, SPAN), F32), pltpu.SemaphoreType.DMA((8,))],
    )
    q_turned = turn(q)
    bup, bdown = exchange(bup, bdown)
    c, hc = call(
        middle_kernel,
        scalars + held(b, source) + plain(ps, bup, bdown) + held(hq),
        [(FLUID, 0), ((CH, ROWS, SPAN), 0)],
        scratch=[pltpu.VMEM((3, NV, ROWS, SPAN), F32)],
        flops=LONG,
    )
    v, metal, mup, mdown, e1 = call(
        second_kernel,
        scalars[:1] + plain(q_turned, kron, ps, metal, coeff, ff, mf, hc),
        [(BLOCKS, 3), (METAL, 1), ((CH, MSPAN), 1), ((CH, MSPAN), 1), ((6, ROWS, SPAN), 1)],
    )
    v = turn(v)
    mup, mdown = exchange(mup, mdown)
    out, metal = call(
        last_kernel, held(v, c, e1, metal) + plain(mup, mdown, cond, mf), [(FLUID, 6), (METAL, 1)]
    )
    return out, metal.reshape(2, NH, ROWS, MSPAN)


def solution(mesh):
    return jax.shard_map(
        local,
        mesh=mesh,
        in_specs=(
            P("inst", None, "space", None),
            P("inst", None, "space", None),
            P("space", None),
            P(),
            P(),
            P(None, None, "space", None),
            P("space", None),
            P("space"),
            P("space"),
            P("space"),
        ),
        out_specs=(P("inst", None, "space", None), P(None, None, "space", None)),
        check_vma=False,
    )
```

```python
import math

import jax
import jax.numpy as jnp
import ml_dtypes
import numpy as np
from jax import lax
from jax.experimental import pallas as pl
from jax.experimental.pallas import tpu as pltpu
from jax.sharding import PartitionSpec as P

NT, NV, NH = 48, 5, 4
ROWS, SPAN, MSPAN, NF = 8, 1024, 512, 512
CHUNK = 128
CH = 2 * NH
F32, BF16 = jnp.float32, jnp.bfloat16

damping_fourth = 1.0 / 32.0
viscous_coef = 0.1
sigma_fluid = 0.5
metal_step = 0.2
sigma_metal = 0.5
heat_capacity = 0.5
flux_scale = 4.0


def tables():
    t = np.arange(NT)
    offset = t[:, None] - t[None, :]
    angle = np.where(offset == 0, 0.5, math.pi * offset / NT)
    spectral = np.where(
        offset == 0, 0.0, 0.5 * (1.0 - 2.0 * (offset % 2)) * np.cos(angle) / np.sin(angle)
    )
    phase = 2.0 * math.pi * ((np.arange(NH)[:, None] * t[None, :]) % NT) / NT
    synth = np.concatenate([np.cos(phase), -np.sin(phase)])
    w0 = synth * (flux_scale / NT)
    w1 = w0 @ spectral
    w2 = w1 @ spectral
    high = spectral.astype(np.float32).astype(ml_dtypes.bfloat16)
    low = (spectral - high.astype(np.float64)).astype(np.float32).astype(ml_dtypes.bfloat16)
    eye = np.eye(ROWS, dtype=np.float32)
    kron_high = np.kron(high.astype(np.float32), eye)
    kron_low = np.kron(low.astype(np.float32), eye)
    kron = np.concatenate([kron_high, kron_high, kron_low], axis=1).astype(ml_dtypes.bfloat16)
    flat = np.concatenate([m.T.reshape(-1) for m in (synth, w0, w1, w2)]).astype(np.float32)
    return kron, flat


KRON, FLAT = tables()
SYNTH, W0, W1, W2 = (i * NT * CH for i in range(4))


class Loaded:
    def __init__(self, source, buffer, sems, cut):
        self.buffer, self.copies = buffer, []
        for i, index in enumerate(cut):
            self.copies.append(pltpu.make_async_copy(source.at[index], buffer.at[index], sems.at[i]))
        self.waiting = set(range(len(cut)))

    def start(self, i):
        self.copies[i].start()

    def piece(self, i):
        if i in self.waiting:
            self.waiting.remove(i)
            self.copies[i].wait()
        return self.buffer

    def whole(self):
        for i in range(len(self.copies)):
            self.piece(i)
        return self.buffer

    def __getitem__(self, index):
        return self.whole()[index]


class Held:
    def __init__(self, ref):
        self.buffer = ref

    def piece(self, i):
        return self.buffer

    def whole(self):
        return self.buffer

    def put(self, index):
        pass


class Stored:
    def __init__(self, target, buffer, sems):
        self.target, self.buffer, self.sems, self.copies = target, buffer, sems, []

    def put(self, index):
        copy = pltpu.make_async_copy(
            self.buffer.at[index], self.target.at[index], self.sems.at[len(self.copies)]
        )
        copy.start()
        self.copies.append(copy)

    def finish(self):
        for copy in self.copies:
            copy.wait()


WHOLE = (slice(None),)


def by_piece(n):
    return tuple(pl.ds(i, 1) for i in range(n))


def call(body, operands, results, scratch=(), flops=1 << 20, moved=1 << 20):
    space = {"smem": pltpu.SMEM, "vmem": pltpu.VMEM, "held": pltpu.VMEM}
    modes = [mode for _, mode in operands]
    here = [isinstance(mode, str) for mode in modes]
    in_specs = [
        pl.BlockSpec(memory_space=space[m] if h else pltpu.HBM) for m, h in zip(modes, here)
    ]
    out_specs = [pl.BlockSpec(memory_space=pltpu.HBM if n else pltpu.VMEM) for _, n in results]
    buffers = []
    for array, mode in operands:
        if not isinstance(mode, str):
            buffers += [pltpu.VMEM(array.shape, array.dtype), pltpu.SemaphoreType.DMA((len(mode),))]
    for dims, n in results:
        if n > 0:
            buffers += [pltpu.VMEM(dims, F32), pltpu.SemaphoreType.DMA((n,))]

    def kernel(*refs):
        ins, refs = refs[: len(modes)], refs[len(modes) :]
        outs, refs = refs[: len(results)], list(refs[len(results) :])
        args, loads = [], []
        for ref, mode, h in zip(ins, modes, here):
            if h:
                args.append(Held(ref) if mode == "held" else ref)
            else:
                args.append(Loaded(ref, refs.pop(0), refs.pop(0), mode))
                loads.append(args[-1])
        for i in range(max([len(x.copies) for x in loads], default=0)):
            for x in loads:
                if i < len(x.copies):
                    x.start(i)
        stores = []
        for ref, (_, n) in zip(outs, results):
            if n > 0:
                args.append(Stored(ref, refs.pop(0), refs.pop(0)))
                stores.append(args[-1])
            else:
                args.append(ref if n else Held(ref))
        body(*args, *refs)
        for x in loads:
            x.whole()
        for x in stores:
            x.finish()

    return pl.pallas_call(
        kernel,
        out_shape=[pltpu.HBM(dims, F32) if n else shape(*dims) for dims, n in results],
        in_specs=in_specs,
        out_specs=out_specs,
        scratch_shapes=buffers + list(scratch),
        compiler_params=pltpu.CompilerParams(vmem_limit_bytes=24 << 20),
        cost_estimate=pl.CostEstimate(flops=flops, bytes_accessed=moved, transcendentals=0),
    )(
        *[a if h else pltpu.with_memory_space_constraint(a, pltpu.HBM) for (a, _), h in zip(operands, here)]
    )


def shape(*dims):
    return jax.ShapeDtypeStruct(dims, F32)


def row_index(n=SPAN):
    return lax.broadcasted_iota(jnp.int32, (ROWS, n), 0)


def split(x):
    high = x.astype(BF16)
    return high, (x - high.astype(F32)).astype(BF16)


def one_hot(index, n):
    cell = lax.broadcasted_iota(jnp.int32, (n, NF), 0)
    return jnp.where(cell == index, 1.0, 0.0).astype(BF16)


def at_faces(field, span_hot, row_hot):
    n = field.shape[-1]
    both = jnp.concatenate(split(field.reshape(CH * ROWS, n)), axis=0)
    picked = jnp.dot(both, span_hot, preferred_element_type=F32)
    picked = (picked[: CH * ROWS] + picked[CH * ROWS :]).reshape(CH, ROWS, NF)
    return jnp.sum(picked * row_hot[None], axis=1)


def onto_cells(values, span_hot, row_hot):
    spread = (values[:, None, :] * row_hot[None]).reshape(CH * ROWS, NF)
    both = jnp.concatenate(split(spread), axis=0)
    out = lax.dot_general(both, span_hot, (((1,), (1,)), ((), ())), preferred_element_type=F32)
    return (out[: CH * ROWS] + out[CH * ROWS :]).reshape(CH, ROWS, span_hot.shape[0])


def fluid_hots(ff_ref):
    cell = ff_ref[...]
    span = one_hot(cell & (SPAN - 1), SPAN)
    rows = jnp.where(row_index(NF) == (cell >> 10), 1.0, 0.0)
    return span, rows


def metal_hots(mf_ref):
    cell = mf_ref[...]
    span = one_hot(cell & (MSPAN - 1), MSPAN)
    rows = jnp.where(row_index(NF) == (cell >> 9), 1.0, 0.0)
    return span, rows


def span_sides(a):
    n = a.shape[-1]
    lane = lax.broadcasted_iota(jnp.int32, a.shape, a.ndim - 1)
    north = jnp.where(lane == n - 1, 0.0, pltpu.roll(a, n - 1, a.ndim - 1))
    south = jnp.where(lane == 0, 0.0, pltpu.roll(a, 1, a.ndim - 1))
    return north, south


def stencil_parts(a, before, after):
    row = row_index(a.shape[-1])
    east_one = pltpu.roll(jnp.where(row == 0, after, a), 7, 0)
    east_two = pltpu.roll(jnp.where(row < 2, after, a), 6, 0)
    west_one = pltpu.roll(jnp.where(row == 7, before, a), 1, 0)
    west_two = pltpu.roll(jnp.where(row >= 6, before, a), 2, 0)
    north, south = span_sides(a)
    rest = (
        (4.0 * damping_fourth) * (east_one + west_one)
        - damping_fourth * (east_two + west_two)
        + viscous_coef * (north + south)
        - (6.0 * damping_fourth + 2.0 * viscous_coef + sigma_fluid) * a
    )
    return east_one - west_one, north - south, rest


def edge_tile(ref, tile):
    return jnp.concatenate([ref[2 * tile], ref[2 * tile + 1]], axis=1)


def halo_pair(up_ref, down_ref, t, v):
    tile, slot = (t, v) if v < 4 else (6 + t // 4, t % 4)
    before = pltpu.roll(edge_tile(up_ref, tile), (6 - 2 * slot) % 8, 0)
    after = pltpu.roll(edge_tile(down_ref, tile), (8 - 2 * slot) % 8, 0)
    return before, after


def pack_tile(blocks, tile, up_ref, down_ref):
    row = row_index()
    up = down = None
    for slot, a in enumerate(blocks):
        u = pltpu.roll(a, (2 * slot + 2) % 8, 0) if (2 * slot + 2) % 8 else a
        d = pltpu.roll(a, 2 * slot, 0) if slot else a
        mine = (row >> 1) == slot
        up = u if up is None else jnp.where(mine, u, up)
        down = d if down is None else jnp.where(mine, d, down)
    for half in range(2):
        cut = slice(half * 512, half * 512 + 512)
        up_ref[2 * tile + half] = up[:, cut]
        down_ref[2 * tile + half] = down[:, cut]


def pack_last(get, extra, up_ref, down_ref):
    pack_tile([get(t) for t in range(4)], 6, up_ref, down_ref)
    pack_tile([get(4), get(5), extra, extra], 7, up_ref, down_ref)


def prepare_kernel(a, ps, m_in, up, down):
    for t in range(6):
        ref = a.piece(t)
        pack_tile([ref[t, v] for v in range(4)], t, up.buffer, down.buffer)
        for x in (up, down):
            x.put(pl.ds(2 * t, 2))
    pack_last(lambda t: a.buffer[t, NV - 1], ps.whole()[...], up.buffer, down.buffer)
    metal_edges(m_in.whole(), up.buffer.at[16], down.buffer.at[16])
    for x in (up, down):
        x.put(pl.ds(12, 5))


def energy_kernel(tab_ref, m_ref, fc_ref, ff_ref, mf_ref, e):
    first = lax.axis_index("inst") * 6
    m_hot, m_row = metal_hots(mf_ref)
    f_hot, f_row = fluid_hots(ff_ref)
    values = at_faces(m_ref[...], m_hot, m_row) * fc_ref[...]
    cells = onto_cells(values, f_hot, f_row)
    for t in range(6):
        e.buffer[t] = combine(tab_ref, SYNTH, first + t, cells)
        e.put(pl.ds(t, 1))


def combine(tab_ref, base, t, fields):
    total = tab_ref[base + t * CH] * fields[0]
    for ch in range(1, CH):
        if ch != NH:
            total += tab_ref[base + t * CH + ch] * fields[ch]
    return total


def convect(jx_ref, jz_ref, dx, dz, rest, u):
    out = rest
    for v in range(NV):
        out = out - (0.5 * jx_ref[u, v]) * dx[v] - (0.5 * jz_ref[u, v]) * dz[v]
    return out


def inner_kernel(jx_ref, jz_ref, a_in, s_in, ps_ref, e_ref, b, q, blocks, parts, sems):
    step = ps_ref[...]
    copies = []
    for t in range(6):
        a_ref, s_ref = a_in.piece(t), s_in.piece(t)
        for i in range(8):
            source = a_ref.at[t, :, :, pl.ds(i * CHUNK, CHUNK)]
            copies.append(pltpu.make_async_copy(source, blocks.at[i, t], sems.at[8 * t + i]))
            copies[-1].start()
        for v in range(NV):
            a = a_ref[t, v]
            dx, dz, rest = stencil_parts(a, 0.0, 0.0)
            parts[0, v], parts[1, v], parts[2, v] = dx, dz, rest
            dx, dz, rest = stencil_parts(step * a, 0.0, 0.0)
            parts[3, v], parts[4, v], parts[5, v] = dx, dz, rest
        for i in range(8):
            cut = pl.ds(i * CHUNK, CHUNK)
            dx = [parts[0, v, :, cut] for v in range(NV)]
            dz = [parts[1, v, :, cut] for v in range(NV)]
            px = [parts[3, v, :, cut] for v in range(NV)]
            pz = [parts[4, v, :, cut] for v in range(NV)]
            for u in range(NV):
                a = a_ref[t, u, :, cut]
                space = convect(jx_ref, jz_ref, dx, dz, parts[2, u, :, cut], u)
                source = s_ref[t, u, :, cut] + space
                if u == NV - 1:
                    source = source + e_ref[t, :, cut]
                inner = a + ps_ref[:, cut] * source
                b.buffer[t, u, :, cut] = inner
                q.buffer[t, u, :, cut] = a + inner + convect(jx_ref, jz_ref, px, pz, parts[5, u, :, cut], u)
        b.put(pl.ds(t, 1))
        q.put(pl.ds(t, 1))
    for copy in copies:
        copy.wait()


def edge_terms(up_ref, down_ref, half, t, v):
    tile, slot = (t, v) if v < 4 else (6 + t // 4, t % 4)
    row = row_index(512)
    up, down = up_ref[2 * tile + half], down_ref[2 * tile + half]
    one = pltpu.roll(jnp.where(row == 2 * slot, down, up), (7 - 2 * slot) % 8, 0)
    one = jnp.where((row == 0) | (row == 7), one, 0.0)
    east_two = pltpu.roll(down, (6 - 2 * slot) % 8, 0)
    west_two = pltpu.roll(up, (8 - 2 * slot) % 8, 0)
    two = jnp.where(row >= 6, east_two, jnp.where(row < 2, west_two, 0.0))
    return one, two


def first_kernel(
    tab_ref, jx_ref, jz_ref, a_ref, bi_ref, qi_ref, ps_ref, up_ref, down_ref, fc_ref, ff_ref, m_ref, cond_ref,
    q, b_out, bup, bdown, q4, m_out,
):
    first = lax.axis_index("inst") * 6
    step = ps_ref[...]
    q_ref, b_ref = q.buffer, b_out.buffer
    sign = jnp.where(row_index(512) == 0, 0.5, -0.5)
    step_edges = []
    for half in range(2):
        tile = 14 + half
        row = row_index(512)
        up, down = up_ref[tile], down_ref[tile]
        one = jnp.where(row == 7, pltpu.roll(down, 3, 0), pltpu.roll(up, 3, 0))
        two = jnp.where(row >= 6, pltpu.roll(down, 2, 0), pltpu.roll(up, 4, 0))
        step_edges.append((one, two))
    for t in range(6):
        for half in range(2):
            wide = pl.ds(half * 512, 512)
            here = ps_ref[:, wide]
            step_one, step_two = step_edges[half]
            edges = [edge_terms(up_ref, down_ref, half, t, v) for v in range(NV)]
            for u in range(NV):
                total = jx_ref[u, 0] * edges[0][0]
                for v in range(1, NV):
                    total += jx_ref[u, v] * edges[v][0]
                one = sign * total + (4.0 * damping_fourth) * edges[u][0]
                two = damping_fourth * edges[u][1]
                change = here * (one - two)
                b_ref[t, u, :, wide] = bi_ref[t, u, :, wide] + change
                value = qi_ref[t, u, :, wide] + change + (step_one * one - step_two * two)
                for i in range(4):
                    q_ref[4 * half + i, t * NV + u] = value[:, i * CHUNK : (i + 1) * CHUNK]
                if u == NV - 1:
                    q4.buffer[t, :, wide] = value
        q.put((slice(None), pl.ds(t * NV, NV)))
        b_out.put(pl.ds(t, 1))
        pack_tile([b_ref[t, v] for v in range(4)], t, bup.buffer, bdown.buffer)
    pack_last(lambda t: b_ref[t, NV - 1], step, bup.buffer, bdown.buffer)
    q4.put(slice(None))
    bup.put(slice(None))
    bdown.put(slice(None))
    f_hot, f_row = fluid_hots(ff_ref)
    heat = []
    for ch in range(CH):
        h0 = h1 = jnp.zeros((ROWS, SPAN), F32)
        for t in range(6 if ch != NH else 0):
            at = (first + t) * CH + ch
            h0 += tab_ref[W0 + at] * b_ref[t, NV - 1]
            h1 += tab_ref[W1 + at] * a_ref[t, NV - 1]
        heat.append(h0 - step * h1)
    values = at_faces(jnp.stack(heat), f_hot, f_row) * fc_ref[...]
    for i in range(8):
        for k in range(4):
            q_ref[i, 30 + k] = values[:, k * CHUNK : (k + 1) * CHUNK]
    q.put((slice(None), pl.ds(30, 4)))
    before, after = metal_sides(up_ref.at[16], down_ref.at[16])
    m = metal_update(m_ref, before, after, cond_ref[...])
    for ch in range(CH):
        m_out.buffer[ch] = m[ch]
    m_out.put(slice(None))


def rotate_time(kron, x):
    high, low = split(x)
    return jnp.dot(kron, jnp.concatenate([high, low, high], axis=0), preferred_element_type=F32)


def local_step(ps_ref):
    start = pl.multiple_of(lax.axis_index("inst") * CHUNK, CHUNK)
    return ps_ref[:, pl.ds(start, CHUNK)]


def turned(get):
    return jnp.concatenate(
        [
            jnp.concatenate([get(j, t, v) for j in range(8) for t in range(6)], axis=0)
            for v in range(NV)
        ],
        axis=1,
    )


def derive_kernel(kron_ref, a_ref, ps_ref, g):
    wide = jnp.concatenate([local_step(ps_ref)] * NV, axis=1)
    x = turned(lambda j, t, v: a_ref[j, t, v])
    d = rotate_time(kron_ref[...], x)
    g.buffer[...] = (d.reshape(NT, ROWS, NV * CHUNK) * wide[None]).reshape(NT * ROWS, NV * CHUNK)
    g.put(slice(None))


def middle_kernel(
    tab_ref, jx_ref, jz_ref, b_in, s_in, ps_ref, up_ref, down_ref, a_ref, q4_ref, g_ref,
    c_out, hc,
    parts,
):
    first = lax.axis_index("inst") * 6
    c_ref = c_out.buffer
    for t in range(6):
        b_ref, s_ref = b_in.piece(t), s_in.piece(t)
        for v in range(NV):
            before, after = halo_pair(up_ref, down_ref, t, v)
            dx, dz, rest = stencil_parts(b_ref[t, v], before, after)
            parts[0, v], parts[1, v], parts[2, v] = dx, dz, rest
        for i in range(8):
            cut = pl.ds(i * CHUNK, CHUNK)
            dx = [parts[0, v, :, cut] for v in range(NV)]
            dz = [parts[1, v, :, cut] for v in range(NV)]
            for u in range(NV):
                space = convect(jx_ref, jz_ref, dx, dz, parts[2, u, :, cut], u)
                c_ref[t, u, :, cut] = b_ref[t, u, :, cut] + ps_ref[:, cut] * (s_ref[t, u, :, cut] + space)
        c_out.put(pl.ds(t, 1))
    step = ps_ref[...]
    for ch in range(CH):
        h0 = h2 = h3 = jnp.zeros((ROWS, SPAN), F32)
        for t in range(6 if ch != NH else 0):
            at = (first + t) * CH + ch
            h0 += tab_ref[W0 + at] * c_ref[t, NV - 1]
            h2 += tab_ref[W1 + at] * q4_ref[t]
            h3 += tab_ref[W2 + at] * a_ref[t, NV - 1]
        hc.buffer[ch] = h0 + step * (step * h3 - h2)
    hc.put(slice(None))


def metal_update(m, before, after, cond):
    row = row_index(MSPAN)
    out = []
    for ch in range(CH):
        a = m[ch]
        east = pltpu.roll(jnp.where(row == 0, after[ch], a), 7, 0)
        west = pltpu.roll(jnp.where(row == 7, before[ch], a), 1, 0)
        north, south = span_sides(a)
        laplace = east + west + north + south - 4.0 * a
        h = ch % NH
        turn = -heat_capacity * h * m[ch + NH] if ch < NH else heat_capacity * h * m[ch - NH]
        out.append(a + metal_step * (cond * laplace - sigma_metal * a - turn))
    return out


def metal_edges(m, up_ref, down_ref):
    up_ref[...] = jnp.concatenate([m[ch][7:8] for ch in range(CH)], axis=0)
    down_ref[...] = jnp.concatenate([m[ch][0:1] for ch in range(CH)], axis=0)


def metal_sides(up_ref, down_ref):
    before = [jnp.broadcast_to(up_ref[ch : ch + 1], (ROWS, MSPAN)) for ch in range(CH)]
    after = [jnp.broadcast_to(down_ref[ch : ch + 1], (ROWS, MSPAN)) for ch in range(CH)]
    return before, after


def heat_sum(get):
    tiles = []
    for k in range(4):
        total = get(0, k)
        for j in range(1, 8):
            total += get(j, k)
        tiles.append(total)
    return jnp.concatenate(tiles, axis=1)


def second_kernel(
    tab_ref, q_ref, g_ref, kron_ref, ps_ref, m_ref, fc_ref, ff_ref, mf_ref, hc_ref,
    v, m_out, mup, mdown, e,
):
    first = lax.axis_index("inst") * 6
    v_ref = v.buffer
    near = local_step(ps_ref)
    x = turned(lambda j, t, u: q_ref[j, t * NV + u]) - g_ref[...]
    for half in range(2):
        d = rotate_time(kron_ref[pl.ds(half * 192, 192), :], x)
        for j in range(4):
            for t in range(6):
                at = (j * 6 + t) * ROWS
                for u in range(NV):
                    v_ref[half * 4 + j, t * NV + u] = -near * d[at : at + ROWS, u * CHUNK : (u + 1) * CHUNK]
        v.put((pl.ds(half * 4, 4), pl.ds(0, 30)))
    step = ps_ref[...]
    coeff = fc_ref[...]
    m_hot, m_row = metal_hots(mf_ref)
    f_hot, f_row = fluid_hots(ff_ref)
    source = onto_cells(heat_sum(lambda j, k: q_ref[j, 30 + k]), m_hot, m_row)
    m = [m_ref[ch] + metal_step * source[ch] for ch in range(CH)]
    for ch in range(CH):
        m_out.buffer[ch] = m[ch]
    m_out.put(slice(None))
    metal_edges(m, mup.buffer, mdown.buffer)
    mup.put(slice(None))
    mdown.put(slice(None))
    cells = onto_cells(at_faces(jnp.stack(m), m_hot, m_row) * coeff, f_hot, f_row)
    for t in range(6):
        e.buffer[t] = step * combine(tab_ref, SYNTH, first + t, cells)
    e.put(slice(None))
    heat = []
    for ch in range(CH):
        total = hc_ref[ch]
        for t in range(6):
            total += tab_ref[W0 + (first + t) * CH + ch] * e.buffer[t]
        heat.append(total)
    values = at_faces(jnp.stack(heat), f_hot, f_row) * coeff
    for i in range(8):
        for k in range(4):
            v_ref[i, 30 + k] = values[:, k * CHUNK : (k + 1) * CHUNK]
    v.put((slice(None), pl.ds(30, 4)))


def last_kernel(v, c, e, m_in, mup_ref, mdown_ref, cond_ref, mf_ref, out, m_out):
    for t in range(6):
        v_ref, c_ref, e_ref = v.piece(t), c.piece(t), e.whole()
        for i in range(8):
            cut = pl.ds(i * CHUNK, CHUNK)
            for u in range(NV):
                total = c_ref[t, u, :, cut] + v_ref[i, t * NV + u]
                if u == NV - 1:
                    total = total + e_ref[t, :, cut]
                out.buffer[t, u, :, cut] = total
        out.put(pl.ds(t, 1))
    m_hot, m_row = metal_hots(mf_ref)
    source = onto_cells(heat_sum(lambda j, k: v.buffer[j, 30 + k]), m_hot, m_row)
    before, after = metal_sides(mup_ref, mdown_ref)
    m = metal_update(m_in.whole(), before, after, cond_ref[...])
    for ch in range(CH):
        m_out.buffer[ch] = m[ch] + metal_step * source[ch]
    m_out.put(slice(None))


def exchange(up, down):
    n = lax.axis_size("space")
    forward = [(i, (i + 1) % n) for i in range(n)]
    back = [(j, i) for i, j in forward]
    return lax.ppermute(up, "space", forward), lax.ppermute(down, "space", back)


def turn(x):
    return lax.all_to_all(x, "inst", 0, 0, tiled=True)


SIX = by_piece(6)
EDGES = (17, ROWS, 512)
FLUID = (6, NV, ROWS, SPAN)
METAL = (CH, ROWS, MSPAN)
ONE = (6, ROWS, SPAN)
BLOCKS = (8, 34, ROWS, CHUNK)


LONG = 1 << 36


def plain(*arrays):
    return [(array, "vmem") for array in arrays]


def late(*arrays):
    return [(array, WHOLE) for array in arrays]


def held(*arrays):
    return [(array, "held") for array in arrays]


def local(a0, source, ps, jx, jz, metal, cond, coeff, ff, mf):
    kron = jnp.asarray(KRON)
    tab = jnp.asarray(FLAT)
    coeff, ff, mf = (x.reshape(1, NF) for x in (coeff, ff, mf))
    metal = metal.reshape(METAL)
    up, down = call(
        prepare_kernel, [(a0, SIX), (ps, WHOLE), (metal, WHOLE)], [(EDGES, 7), (EDGES, 7)]
    )
    up, down = exchange(up, down)
    scalars = [(tab, "smem"), (jx, "smem"), (jz, "smem")]
    last_variable = (a0, ((slice(None), pl.ds(NV - 1, 1)),))
    (e0,) = call(energy_kernel, scalars[:1] + late(metal, coeff, ff, mf), [(ONE, 0)])
    b, q, blocks = call(
        inner_kernel,
        scalars[1:] + [(a0, SIX), (source, SIX)] + late(ps) + plain(e0),
        [(FLUID, 6), (FLUID, 6), ((8, 6, NV, ROWS, CHUNK), -1)],
        scratch=[pltpu.VMEM((6, NV, ROWS, SPAN), F32), pltpu.SemaphoreType.DMA((48,))],
    )
    a_turned = turn(blocks)
    q, b, bup, bdown, q4, metal = call(
        first_kernel,
        scalars + [last_variable] + plain(b, q) + late(ps) + plain(up, down) + late(coeff, ff, metal, cond),
        [(BLOCKS, 7), (FLUID, 6), (EDGES, 1), (EDGES, 1), (ONE, 1), (METAL, 1)],
        flops=LONG,
    )
    q_turned = turn(q)
    bup, bdown = exchange(bup, bdown)
    (g,) = call(derive_kernel, plain(kron, a_turned) + late(ps), [((NT * ROWS, NV * CHUNK), 0)])
    c, hc = call(
        middle_kernel,
        scalars + [(b, SIX), (source, SIX)] + late(ps) + plain(bup, bdown) + [last_variable] + late(q4)
        + plain(g),
        [(FLUID, 0), ((CH, ROWS, SPAN), 0)],
        scratch=[pltpu.VMEM((3, NV, ROWS, SPAN), F32)],
        flops=LONG,
    )
    v, metal, mup, mdown, e1 = call(
        second_kernel,
        scalars[:1] + plain(q_turned, g, kron) + late(ps, metal, coeff, ff, mf) + plain(hc),
        [(BLOCKS, 3), (METAL, 1), ((CH, MSPAN), 1), ((CH, MSPAN), 1), (ONE, 1)],
    )
    v = turn(v)
    mup, mdown = exchange(mup, mdown)
    out, metal = call(
        last_kernel, held(v, c) + late(e1, metal) + plain(mup, mdown) + late(cond, mf), [(FLUID, 6), (METAL, 1)]
    )
    return out, metal.reshape(2, NH, ROWS, MSPAN)


def solution(mesh):
    return jax.shard_map(
        local,
        mesh=mesh,
        in_specs=(
            P("inst", None, "space", None),
            P("inst", None, "space", None),
            P("space", None),
            P(),
            P(),
            P(None, None, "space", None),
            P("space", None),
            P("space"),
            P("space"),
            P("space"),
        ),
        out_specs=(P("inst", None, "space", None), P(None, None, "space", None)),
        check_vma=False,
    )
```

```python
import math

import jax
import jax.numpy as jnp
import ml_dtypes
import numpy as np
from jax import lax
from jax.experimental import pallas as pl
from jax.experimental.pallas import tpu as pltpu
from jax.sharding import PartitionSpec as P

NT, NV, NH = 48, 5, 4
ROWS, SPAN, MSPAN, NF = 8, 1024, 512, 512
CHUNK = 128
CH = 2 * NH
F32, BF16 = jnp.float32, jnp.bfloat16

damping_fourth = 1.0 / 32.0
viscous_coef = 0.1
sigma_fluid = 0.5
metal_step = 0.2
sigma_metal = 0.5
heat_capacity = 0.5
flux_scale = 4.0


def tables():
    t = np.arange(NT)
    offset = t[:, None] - t[None, :]
    angle = np.where(offset == 0, 0.5, math.pi * offset / NT)
    spectral = np.where(
        offset == 0, 0.0, 0.5 * (1.0 - 2.0 * (offset % 2)) * np.cos(angle) / np.sin(angle)
    )
    phase = 2.0 * math.pi * ((np.arange(NH)[:, None] * t[None, :]) % NT) / NT
    synth = np.concatenate([np.cos(phase), -np.sin(phase)])
    w0 = synth * (flux_scale / NT)
    w1 = w0 @ spectral
    w2 = w1 @ spectral
    high = spectral.astype(np.float32).astype(ml_dtypes.bfloat16)
    low = (spectral - high.astype(np.float64)).astype(np.float32).astype(ml_dtypes.bfloat16)
    eye = np.eye(ROWS, dtype=np.float32)
    kron_high = np.kron(high.astype(np.float32), eye)
    kron_low = np.kron(low.astype(np.float32), eye)
    kron = np.concatenate([kron_high, kron_high, kron_low], axis=1).astype(ml_dtypes.bfloat16)
    flat = np.concatenate([m.T.reshape(-1) for m in (synth, w0, w1, w2)]).astype(np.float32)
    return kron, flat


KRON, FLAT = tables()
SYNTH, W0, W1, W2 = (i * NT * CH for i in range(4))


class Loaded:
    def __init__(self, source, buffer, sems, cut):
        self.buffer, self.copies = buffer, []
        for i, index in enumerate(cut):
            self.copies.append(pltpu.make_async_copy(source.at[index], buffer.at[index], sems.at[i]))
        self.waiting = set(range(len(cut)))

    def start(self, i):
        self.copies[i].start()

    def piece(self, i):
        if i in self.waiting:
            self.waiting.remove(i)
            self.copies[i].wait()
        return self.buffer

    def whole(self):
        for i in range(len(self.copies)):
            self.piece(i)
        return self.buffer

    def __getitem__(self, index):
        return self.whole()[index]


class Held:
    def __init__(self, ref):
        self.buffer = ref

    def piece(self, i):
        return self.buffer

    def whole(self):
        return self.buffer

    def put(self, index):
        pass


class Stored:
    def __init__(self, target, buffer, sems):
        self.target, self.buffer, self.sems, self.copies = target, buffer, sems, []

    def put(self, index):
        copy = pltpu.make_async_copy(
            self.buffer.at[index], self.target.at[index], self.sems.at[len(self.copies)]
        )
        copy.start()
        self.copies.append(copy)

    def finish(self):
        for copy in self.copies:
            copy.wait()


class Into:
    def __init__(self, result, cut):
        self.result, self.cut = result, cut

    def __len__(self):
        return len(self.cut)


WHOLE = (slice(None),)


def by_piece(n):
    return tuple(pl.ds(i, 1) for i in range(n))


def call(body, operands, results, scratch=(), flops=1 << 20, moved=1 << 20):
    space = {"smem": pltpu.SMEM, "vmem": pltpu.VMEM, "held": pltpu.VMEM}
    modes = [mode for _, mode in operands]
    here = [isinstance(mode, str) for mode in modes]
    in_specs = [
        pl.BlockSpec(memory_space=space[m] if h else pltpu.HBM) for m, h in zip(modes, here)
    ]
    out_specs = [pl.BlockSpec(memory_space=pltpu.HBM if n else pltpu.VMEM) for _, n in results]
    buffers = []
    kinds = {mode.result: array.dtype for array, mode in operands if isinstance(mode, Into)}
    for array, mode in operands:
        if isinstance(mode, tuple):
            buffers.append(pltpu.VMEM(array.shape, array.dtype))
        if not isinstance(mode, str):
            buffers.append(pltpu.SemaphoreType.DMA((len(mode),)))
    for dims, n in results:
        if n > 0:
            buffers += [pltpu.VMEM(dims, F32), pltpu.SemaphoreType.DMA((n,))]

    def kernel(*refs):
        ins, refs = refs[: len(modes)], refs[len(modes) :]
        outs, refs = refs[: len(results)], list(refs[len(results) :])
        args, loads = [], []
        for ref, mode, h in zip(ins, modes, here):
            if h:
                args.append(Held(ref) if mode == "held" else ref)
            else:
                into = isinstance(mode, Into)
                buffer = outs[mode.result] if into else refs.pop(0)
                args.append(Loaded(ref, buffer, refs.pop(0), mode.cut if into else mode))
                loads.append(args[-1])
        for i in range(max([len(x.copies) for x in loads], default=0)):
            for x in loads:
                if i < len(x.copies):
                    x.start(i)
        stores = []
        for ref, (_, n) in zip(outs, results):
            if n > 0:
                args.append(Stored(ref, refs.pop(0), refs.pop(0)))
                stores.append(args[-1])
            else:
                args.append(ref if n else Held(ref))
        body(*args, *refs)
        for x in loads:
            x.whole()
        for x in stores:
            x.finish()

    return pl.pallas_call(
        kernel,
        out_shape=[pltpu.HBM(dims, F32) if n else jax.ShapeDtypeStruct(dims, kinds.get(k, F32)) for k, (dims, n) in enumerate(results)],
        in_specs=in_specs,
        out_specs=out_specs,
        scratch_shapes=buffers + list(scratch),
        compiler_params=pltpu.CompilerParams(vmem_limit_bytes=24 << 20),
        cost_estimate=pl.CostEstimate(flops=flops, bytes_accessed=moved, transcendentals=0),
    )(
        *[a if h else pltpu.with_memory_space_constraint(a, pltpu.HBM) for (a, _), h in zip(operands, here)]
    )


def shape(*dims):
    return jax.ShapeDtypeStruct(dims, F32)


def row_index(n=SPAN):
    return lax.broadcasted_iota(jnp.int32, (ROWS, n), 0)


def split(x):
    high = x.astype(BF16)
    return high, (x - high.astype(F32)).astype(BF16)


def one_hot(index, n):
    cell = lax.broadcasted_iota(jnp.int32, (n, NF), 0)
    return jnp.where(cell == index, 1.0, 0.0).astype(BF16)


def at_faces(field, span_hot, row_hot):
    n = field.shape[-1]
    both = jnp.concatenate(split(field.reshape(CH * ROWS, n)), axis=0)
    picked = jnp.dot(both, span_hot, preferred_element_type=F32)
    picked = (picked[: CH * ROWS] + picked[CH * ROWS :]).reshape(CH, ROWS, NF)
    return jnp.sum(picked * row_hot[None], axis=1)


def onto_cells(values, span_hot, row_hot):
    spread = (values[:, None, :] * row_hot[None]).reshape(CH * ROWS, NF)
    both = jnp.concatenate(split(spread), axis=0)
    out = lax.dot_general(both, span_hot, (((1,), (1,)), ((), ())), preferred_element_type=F32)
    return (out[: CH * ROWS] + out[CH * ROWS :]).reshape(CH, ROWS, span_hot.shape[0])


def fluid_hots(ff_ref):
    cell = ff_ref[...]
    span = one_hot(cell & (SPAN - 1), SPAN)
    rows = jnp.where(row_index(NF) == (cell >> 10), 1.0, 0.0)
    return span, rows


def metal_hots(mf_ref):
    cell = mf_ref[...]
    span = one_hot(cell & (MSPAN - 1), MSPAN)
    rows = jnp.where(row_index(NF) == (cell >> 9), 1.0, 0.0)
    return span, rows


def span_sides(a):
    n = a.shape[-1]
    lane = lax.broadcasted_iota(jnp.int32, a.shape, a.ndim - 1)
    north = jnp.where(lane == n - 1, 0.0, pltpu.roll(a, n - 1, a.ndim - 1))
    south = jnp.where(lane == 0, 0.0, pltpu.roll(a, 1, a.ndim - 1))
    return north, south


def stencil_parts(a, before, after):
    row = row_index(a.shape[-1])
    east_one = pltpu.roll(jnp.where(row == 0, after, a), 7, 0)
    east_two = pltpu.roll(jnp.where(row < 2, after, a), 6, 0)
    west_one = pltpu.roll(jnp.where(row == 7, before, a), 1, 0)
    west_two = pltpu.roll(jnp.where(row >= 6, before, a), 2, 0)
    north, south = span_sides(a)
    rest = (
        (4.0 * damping_fourth) * (east_one + west_one)
        - damping_fourth * (east_two + west_two)
        + viscous_coef * (north + south)
        - (6.0 * damping_fourth + 2.0 * viscous_coef + sigma_fluid) * a
    )
    return east_one - west_one, north - south, rest


def edge_tile(ref, tile):
    return jnp.concatenate([ref[2 * tile], ref[2 * tile + 1]], axis=1)


def halo_pair(up_ref, down_ref, t, v):
    tile, slot = (t, v) if v < 4 else (6 + t // 4, t % 4)
    before = pltpu.roll(edge_tile(up_ref, tile), (6 - 2 * slot) % 8, 0)
    after = pltpu.roll(edge_tile(down_ref, tile), (8 - 2 * slot) % 8, 0)
    return before, after


def pack_tile(blocks, tile, up_ref, down_ref):
    row = row_index()
    up = down = None
    for slot, a in enumerate(blocks):
        u = pltpu.roll(a, (2 * slot + 2) % 8, 0) if (2 * slot + 2) % 8 else a
        d = pltpu.roll(a, 2 * slot, 0) if slot else a
        mine = (row >> 1) == slot
        up = u if up is None else jnp.where(mine, u, up)
        down = d if down is None else jnp.where(mine, d, down)
    for half in range(2):
        cut = slice(half * 512, half * 512 + 512)
        up_ref[2 * tile + half] = up[:, cut]
        down_ref[2 * tile + half] = down[:, cut]


def pack_last(get, extra, up_ref, down_ref):
    pack_tile([get(t) for t in range(4)], 6, up_ref, down_ref)
    pack_tile([get(4), get(5), extra, extra], 7, up_ref, down_ref)


def prepare_kernel(a, ps, m_in, fc, ff, mf, up, down, *copies):
    for t in range(6):
        ref = a.piece(t)
        pack_tile([ref[t, v] for v in range(4)], t, up.buffer, down.buffer)
        for x in (up, down):
            x.put(pl.ds(2 * t, 2))
    pack_last(lambda t: a.buffer[t, NV - 1], ps.whole()[...], up.buffer, down.buffer)
    metal_edges(m_in.whole(), up.buffer.at[16], down.buffer.at[16])
    for x in (up, down):
        x.put(pl.ds(12, 5))


def energy_kernel(tab_ref, m_ref, fc_ref, ff_ref, mf_ref, source, e, copied):
    first = lax.axis_index("inst") * 6
    m_hot, m_row = metal_hots(mf_ref)
    f_hot, f_row = fluid_hots(ff_ref)
    values = at_faces(m_ref[...], m_hot, m_row) * fc_ref[...]
    cells = onto_cells(values, f_hot, f_row)
    for t in range(6):
        e.buffer[t] = combine(tab_ref, SYNTH, first + t, cells)
        e.put(pl.ds(t, 1))


def combine(tab_ref, base, t, fields):
    total = tab_ref[base + t * CH] * fields[0]
    for ch in range(1, CH):
        if ch != NH:
            total += tab_ref[base + t * CH + ch] * fields[ch]
    return total


def convect(jx_ref, jz_ref, dx, dz, rest, u):
    out = rest
    for v in range(NV):
        out = out - (0.5 * jx_ref[u, v]) * dx[v] - (0.5 * jz_ref[u, v]) * dz[v]
    return out


def inner_kernel(jx_ref, jz_ref, a_ref, s_ref, ps_ref, e_ref, b, q, blocks, parts, sems):
    step = ps_ref[...]
    copies = []
    for t in range(6):
        for i in range(8):
            source = a_ref.at[t, :, :, pl.ds(i * CHUNK, CHUNK)]
            copies.append(pltpu.make_async_copy(source, blocks.at[i, t], sems.at[8 * t + i]))
            copies[-1].start()
        for v in range(NV):
            a = a_ref[t, v]
            dx, dz, rest = stencil_parts(a, 0.0, 0.0)
            parts[0, v], parts[1, v], parts[2, v] = dx, dz, rest
            dx, dz, rest = stencil_parts(step * a, 0.0, 0.0)
            parts[3, v], parts[4, v], parts[5, v] = dx, dz, rest
        for i in range(8):
            cut = pl.ds(i * CHUNK, CHUNK)
            dx = [parts[0, v, :, cut] for v in range(NV)]
            dz = [parts[1, v, :, cut] for v in range(NV)]
            px = [parts[3, v, :, cut] for v in range(NV)]
            pz = [parts[4, v, :, cut] for v in range(NV)]
            for u in range(NV):
                a = a_ref[t, u, :, cut]
                space = convect(jx_ref, jz_ref, dx, dz, parts[2, u, :, cut], u)
                source = s_ref[t, u, :, cut] + space
                if u == NV - 1:
                    source = source + e_ref[t, :, cut]
                inner = a + ps_ref[:, cut] * source
                b.buffer[t, u, :, cut] = inner
                q.buffer[t, u, :, cut] = a + inner + convect(jx_ref, jz_ref, px, pz, parts[5, u, :, cut], u)
        b.put(pl.ds(t, 1))
        q.put(pl.ds(t, 1))
    for copy in copies:
        copy.wait()


def edge_terms(up_ref, down_ref, half, t, v):
    tile, slot = (t, v) if v < 4 else (6 + t // 4, t % 4)
    row = row_index(512)
    up, down = up_ref[2 * tile + half], down_ref[2 * tile + half]
    one = pltpu.roll(jnp.where(row == 2 * slot, down, up), (7 - 2 * slot) % 8, 0)
    one = jnp.where((row == 0) | (row == 7), one, 0.0)
    east_two = pltpu.roll(down, (6 - 2 * slot) % 8, 0)
    west_two = pltpu.roll(up, (8 - 2 * slot) % 8, 0)
    two = jnp.where(row >= 6, east_two, jnp.where(row < 2, west_two, 0.0))
    return one, two


def first_kernel(
    tab_ref, jx_ref, jz_ref, a_ref, bi_ref, qi_ref, ps_ref, up_ref, down_ref, fc_ref, ff_ref, m_ref, cond_ref,
    q, b_out, bup, bdown, q4, m_out,
):
    first = lax.axis_index("inst") * 6
    step = ps_ref[...]
    q_ref, b_ref = q.buffer, b_out.buffer
    sign = jnp.where(row_index(512) == 0, 0.5, -0.5)
    step_edges = []
    for half in range(2):
        tile = 14 + half
        row = row_index(512)
        up, down = up_ref[tile], down_ref[tile]
        one = jnp.where(row == 7, pltpu.roll(down, 3, 0), pltpu.roll(up, 3, 0))
        two = jnp.where(row >= 6, pltpu.roll(down, 2, 0), pltpu.roll(up, 4, 0))
        step_edges.append((one, two))
    for t in range(6):
        for half in range(2):
            wide = pl.ds(half * 512, 512)
            here = ps_ref[:, wide]
            step_one, step_two = step_edges[half]
            edges = [edge_terms(up_ref, down_ref, half, t, v) for v in range(NV)]
            for u in range(NV):
                total = jx_ref[u, 0] * edges[0][0]
                for v in range(1, NV):
                    total += jx_ref[u, v] * edges[v][0]
                one = sign * total + (4.0 * damping_fourth) * edges[u][0]
                two = damping_fourth * edges[u][1]
                change = here * (one - two)
                b_ref[t, u, :, wide] = bi_ref[t, u, :, wide] + change
                value = qi_ref[t, u, :, wide] + change + (step_one * one - step_two * two)
                for i in range(4):
                    q_ref[4 * half + i, t * NV + u] = value[:, i * CHUNK : (i + 1) * CHUNK]
                if u == NV - 1:
                    q4.buffer[t, :, wide] = value
        q.put((slice(None), pl.ds(t * NV, NV)))
        b_out.put(pl.ds(t, 1))
        pack_tile([b_ref[t, v] for v in range(4)], t, bup.buffer, bdown.buffer)
    pack_last(lambda t: b_ref[t, NV - 1], step, bup.buffer, bdown.buffer)
    q4.put(slice(None))
    bup.put(slice(None))
    bdown.put(slice(None))
    f_hot, f_row = fluid_hots(ff_ref)
    heat = []
    for ch in range(CH):
        h0 = h1 = jnp.zeros((ROWS, SPAN), F32)
        for t in range(6 if ch != NH else 0):
            at = (first + t) * CH + ch
            h0 += tab_ref[W0 + at] * b_ref[t, NV - 1]
            h1 += tab_ref[W1 + at] * a_ref[t, NV - 1]
        heat.append(h0 - step * h1)
    values = at_faces(jnp.stack(heat), f_hot, f_row) * fc_ref[...]
    for i in range(8):
        for k in range(4):
            q_ref[i, 30 + k] = values[:, k * CHUNK : (k + 1) * CHUNK]
    q.put((slice(None), pl.ds(30, 4)))
    before, after = metal_sides(up_ref.at[16], down_ref.at[16])
    m = metal_update(m_ref, before, after, cond_ref[...])
    for ch in range(CH):
        m_out.buffer[ch] = m[ch]
    m_out.put(slice(None))


def rotate_time(kron, x):
    high, low = split(x)
    return jnp.dot(kron, jnp.concatenate([high, low, high], axis=0), preferred_element_type=F32)


def local_step(ps_ref):
    start = pl.multiple_of(lax.axis_index("inst") * CHUNK, CHUNK)
    return ps_ref[:, pl.ds(start, CHUNK)]


def turned(get):
    return jnp.concatenate(
        [
            jnp.concatenate([get(j, t, v) for j in range(8) for t in range(6)], axis=0)
            for v in range(NV)
        ],
        axis=1,
    )


def derive_kernel(kron_ref, a_ref, ps_ref, g):
    wide = jnp.concatenate([local_step(ps_ref)] * NV, axis=1)
    x = turned(lambda j, t, v: a_ref[j, t, v])
    d = rotate_time(kron_ref[...], x)
    g.buffer[...] = (d.reshape(NT, ROWS, NV * CHUNK) * wide[None]).reshape(NT * ROWS, NV * CHUNK)
    g.put(slice(None))


def middle_kernel(
    tab_ref, jx_ref, jz_ref, b_in, s_in, ps_ref, up_ref, down_ref, a_ref, q4_ref, g_ref,
    c_out, hc,
    parts,
):
    first = lax.axis_index("inst") * 6
    c_ref = c_out.buffer
    for t in range(6):
        b_ref, s_ref = b_in.piece(t), s_in.piece(t)
        for v in range(NV):
            before, after = halo_pair(up_ref, down_ref, t, v)
            dx, dz, rest = stencil_parts(b_ref[t, v], before, after)
            parts[0, v], parts[1, v], parts[2, v] = dx, dz, rest
        for i in range(8):
            cut = pl.ds(i * CHUNK, CHUNK)
            dx = [parts[0, v, :, cut] for v in range(NV)]
            dz = [parts[1, v, :, cut] for v in range(NV)]
            for u in range(NV):
                space = convect(jx_ref, jz_ref, dx, dz, parts[2, u, :, cut], u)
                c_ref[t, u, :, cut] = b_ref[t, u, :, cut] + ps_ref[:, cut] * (s_ref[t, u, :, cut] + space)
        c_out.put(pl.ds(t, 1))
    step = ps_ref[...]
    for ch in range(CH):
        h0 = h2 = h3 = jnp.zeros((ROWS, SPAN), F32)
        for t in range(6 if ch != NH else 0):
            at = (first + t) * CH + ch
            h0 += tab_ref[W0 + at] * c_ref[t, NV - 1]
            h2 += tab_ref[W1 + at] * q4_ref[t]
            h3 += tab_ref[W2 + at] * a_ref[t, NV - 1]
        hc.buffer[ch] = h0 + step * (step * h3 - h2)
    hc.put(slice(None))


def metal_update(m, before, after, cond):
    row = row_index(MSPAN)
    out = []
    for ch in range(CH):
        a = m[ch]
        east = pltpu.roll(jnp.where(row == 0, after[ch], a), 7, 0)
        west = pltpu.roll(jnp.where(row == 7, before[ch], a), 1, 0)
        north, south = span_sides(a)
        laplace = east + west + north + south - 4.0 * a
        h = ch % NH
        turn = -heat_capacity * h * m[ch + NH] if ch < NH else heat_capacity * h * m[ch - NH]
        out.append(a + metal_step * (cond * laplace - sigma_metal * a - turn))
    return out


def metal_edges(m, up_ref, down_ref):
    up_ref[...] = jnp.concatenate([m[ch][7:8] for ch in range(CH)], axis=0)
    down_ref[...] = jnp.concatenate([m[ch][0:1] for ch in range(CH)], axis=0)


def metal_sides(up_ref, down_ref):
    before = [jnp.broadcast_to(up_ref[ch : ch + 1], (ROWS, MSPAN)) for ch in range(CH)]
    after = [jnp.broadcast_to(down_ref[ch : ch + 1], (ROWS, MSPAN)) for ch in range(CH)]
    return before, after


def heat_sum(get):
    tiles = []
    for k in range(4):
        total = get(0, k)
        for j in range(1, 8):
            total += get(j, k)
        tiles.append(total)
    return jnp.concatenate(tiles, axis=1)


def second_kernel(
    tab_ref, q_ref, g_ref, kron_ref, ps_ref, m_ref, fc_ref, ff_ref, mf_ref, hc_ref,
    v, m_out, mup, mdown, e,
):
    first = lax.axis_index("inst") * 6
    v_ref = v.buffer
    near = local_step(ps_ref)
    x = turned(lambda j, t, u: q_ref[j, t * NV + u]) - g_ref[...]
    for half in range(2):
        d = rotate_time(kron_ref[pl.ds(half * 192, 192), :], x)
        for j in range(4):
            for t in range(6):
                at = (j * 6 + t) * ROWS
                for u in range(NV):
                    v_ref[half * 4 + j, t * NV + u] = -near * d[at : at + ROWS, u * CHUNK : (u + 1) * CHUNK]
        v.put((pl.ds(half * 4, 4), pl.ds(0, 30)))
    step = ps_ref[...]
    coeff = fc_ref[...]
    m_hot, m_row = metal_hots(mf_ref)
    f_hot, f_row = fluid_hots(ff_ref)
    source = onto_cells(heat_sum(lambda j, k: q_ref[j, 30 + k]), m_hot, m_row)
    m = [m_ref[ch] + metal_step * source[ch] for ch in range(CH)]
    for ch in range(CH):
        m_out.buffer[ch] = m[ch]
    m_out.put(slice(None))
    metal_edges(m, mup.buffer, mdown.buffer)
    mup.put(slice(None))
    mdown.put(slice(None))
    cells = onto_cells(at_faces(jnp.stack(m), m_hot, m_row) * coeff, f_hot, f_row)
    for t in range(6):
        e.buffer[t] = step * combine(tab_ref, SYNTH, first + t, cells)
    e.put(slice(None))
    heat = []
    for ch in range(CH):
        total = hc_ref[ch]
        for t in range(6):
            total += tab_ref[W0 + (first + t) * CH + ch] * e.buffer[t]
        heat.append(total)
    values = at_faces(jnp.stack(heat), f_hot, f_row) * coeff
    for i in range(8):
        for k in range(4):
            v_ref[i, 30 + k] = values[:, k * CHUNK : (k + 1) * CHUNK]
    v.put((slice(None), pl.ds(30, 4)))


def last_kernel(v, c, e, m_in, mup_ref, mdown_ref, cond_ref, mf_ref, out, m_out):
    for t in range(6):
        v_ref, c_ref, e_ref = v.piece(t), c.piece(t), e.whole()
        for i in range(8):
            cut = pl.ds(i * CHUNK, CHUNK)
            for u in range(NV):
                total = c_ref[t, u, :, cut] + v_ref[i, t * NV + u]
                if u == NV - 1:
                    total = total + e_ref[t, :, cut]
                out.buffer[t, u, :, cut] = total
        out.put(pl.ds(t, 1))
    m_hot, m_row = metal_hots(mf_ref)
    source = onto_cells(heat_sum(lambda j, k: v.buffer[j, 30 + k]), m_hot, m_row)
    before, after = metal_sides(mup_ref, mdown_ref)
    m = metal_update(m_in.whole(), before, after, cond_ref[...])
    for ch in range(CH):
        m_out.buffer[ch] = m[ch] + metal_step * source[ch]
    m_out.put(slice(None))


def exchange(up, down):
    n = lax.axis_size("space")
    forward = [(i, (i + 1) % n) for i in range(n)]
    back = [(j, i) for i, j in forward]
    return lax.ppermute(up, "space", forward), lax.ppermute(down, "space", back)


def turn(x):
    return lax.all_to_all(x, "inst", 0, 0, tiled=True)


SIX = by_piece(6)
EDGES = (17, ROWS, 512)
FLUID = (6, NV, ROWS, SPAN)
METAL = (CH, ROWS, MSPAN)
ONE = (6, ROWS, SPAN)
BLOCKS = (8, 34, ROWS, CHUNK)


LONG = 1 << 36


def plain(*arrays):
    return [(array, "vmem") for array in arrays]


def late(*arrays):
    return [(array, WHOLE) for array in arrays]


def held(*arrays):
    return [(array, "held") for array in arrays]


def local(a0, source, ps, jx, jz, metal, cond, coeff, ff, mf):
    kron = jnp.asarray(KRON)
    tab = jnp.asarray(FLAT)
    coeff, ff, mf = (x.reshape(1, NF) for x in (coeff, ff, mf))
    metal = metal.reshape(METAL)
    small = [(x, Into(3 + i, WHOLE)) for i, x in enumerate((ps, metal, coeff, ff, mf))]
    up, down, a_here, ps_here, metal_here, coeff_here, ff_here, mf_here = call(
        prepare_kernel,
        [(a0, Into(2, SIX))] + small,
        [(EDGES, 7), (EDGES, 7), (FLUID, 0), ((ROWS, SPAN), 0), (METAL, 0)] + [((1, NF), 0)] * 3,
    )
    up, down = exchange(up, down)
    scalars = [(tab, "smem"), (jx, "smem"), (jz, "smem")]
    last_variable = (a0, ((slice(None), pl.ds(NV - 1, 1)),))
    e0, source_here = call(
        energy_kernel,
        scalars[:1] + plain(metal_here, coeff_here, ff_here, mf_here) + [(source, Into(1, WHOLE))],
        [(ONE, 0), (FLUID, 0)],
    )
    b, q, blocks = call(
        inner_kernel,
        scalars[1:] + plain(a_here, source_here, ps_here, e0),
        [(FLUID, 6), (FLUID, 6), ((8, 6, NV, ROWS, CHUNK), -1)],
        scratch=[pltpu.VMEM((6, NV, ROWS, SPAN), F32), pltpu.SemaphoreType.DMA((48,))],
    )
    a_turned = turn(blocks)
    q, b, bup, bdown, q4, metal = call(
        first_kernel,
        scalars + [last_variable] + plain(b, q, ps, up, down, coeff, ff, metal, cond),
        [(BLOCKS, 7), (FLUID, 6), (EDGES, 1), (EDGES, 1), (ONE, 1), (METAL, 1)],
        flops=LONG,
    )
    q_turned = turn(q)
    bup, bdown = exchange(bup, bdown)
    (g,) = call(derive_kernel, plain(kron, a_turned, ps), [((NT * ROWS, NV * CHUNK), 0)])
    c, hc = call(
        middle_kernel,
        scalars + [(b, SIX), (source, SIX)] + late(ps) + plain(bup, bdown) + [last_variable] + late(q4)
        + plain(g),
        [(FLUID, 0), ((CH, ROWS, SPAN), 0)],
        scratch=[pltpu.VMEM((3, NV, ROWS, SPAN), F32)],
        flops=LONG,
    )
    v, metal, mup, mdown, e1 = call(
        second_kernel,
        scalars[:1] + plain(q_turned, g, kron, ps, metal, coeff, ff, mf, hc),
        [(BLOCKS, 3), (METAL, 1), ((CH, MSPAN), 1), ((CH, MSPAN), 1), (ONE, 1)],
    )
    v = turn(v)
    mup, mdown = exchange(mup, mdown)
    out, metal = call(
        last_kernel, held(v, c, e1, metal) + plain(mup, mdown, cond, mf), [(FLUID, 6), (METAL, 1)]
    )
    return out, metal.reshape(2, NH, ROWS, MSPAN)


def solution(mesh):
    return jax.shard_map(
        local,
        mesh=mesh,
        in_specs=(
            P("inst", None, "space", None),
            P("inst", None, "space", None),
            P("space", None),
            P(),
            P(),
            P(None, None, "space", None),
            P("space", None),
            P("space"),
            P("space"),
            P("space"),
        ),
        out_specs=(P("inst", None, "space", None), P(None, None, "space", None)),
        check_vma=False,
    )
```

```python
import math

import jax
import jax.numpy as jnp
import ml_dtypes
import numpy as np
from jax import lax
from jax.experimental import pallas as pl
from jax.experimental.pallas import tpu as pltpu
from jax.sharding import PartitionSpec as P

NT, NV, NH = 48, 5, 4
ROWS, SPAN, MSPAN, NF = 8, 1024, 512, 512
CHUNK = 128
CH = 2 * NH
F32, BF16 = jnp.float32, jnp.bfloat16

damping_fourth = 1.0 / 32.0
viscous_coef = 0.1
sigma_fluid = 0.5
metal_step = 0.2
sigma_metal = 0.5
heat_capacity = 0.5
flux_scale = 4.0


def tables():
    t = np.arange(NT)
    offset = t[:, None] - t[None, :]
    angle = np.where(offset == 0, 0.5, math.pi * offset / NT)
    spectral = np.where(
        offset == 0, 0.0, 0.5 * (1.0 - 2.0 * (offset % 2)) * np.cos(angle) / np.sin(angle)
    )
    phase = 2.0 * math.pi * ((np.arange(NH)[:, None] * t[None, :]) % NT) / NT
    synth = np.concatenate([np.cos(phase), -np.sin(phase)])
    w0 = synth * (flux_scale / NT)
    w1 = w0 @ spectral
    w2 = w1 @ spectral
    high = spectral.astype(np.float32).astype(ml_dtypes.bfloat16)
    low = (spectral - high.astype(np.float64)).astype(np.float32).astype(ml_dtypes.bfloat16)
    eye = np.eye(ROWS, dtype=np.float32)
    kron_high = np.kron(high.astype(np.float32), eye)
    kron_low = np.kron(low.astype(np.float32), eye)
    kron = np.concatenate([kron_high, kron_high, kron_low], axis=1).astype(ml_dtypes.bfloat16)
    flat = np.concatenate([m.T.reshape(-1) for m in (synth, w0, w1, w2)]).astype(np.float32)
    return kron, flat


KRON, FLAT = tables()
SYNTH, W0, W1, W2 = (i * NT * CH for i in range(4))


class Loaded:
    def __init__(self, source, buffer, sems, cut):
        self.buffer, self.copies = buffer, []
        for i, index in enumerate(cut):
            self.copies.append(pltpu.make_async_copy(source.at[index], buffer.at[index], sems.at[i]))
        self.waiting = set(range(len(cut)))

    def start(self, i):
        self.copies[i].start()

    def piece(self, i):
        if i in self.waiting:
            self.waiting.remove(i)
            self.copies[i].wait()
        return self.buffer

    def whole(self):
        for i in range(len(self.copies)):
            self.piece(i)
        return self.buffer

    def __getitem__(self, index):
        return self.whole()[index]


class Held:
    def __init__(self, ref):
        self.buffer = ref

    def piece(self, i):
        return self.buffer

    def whole(self):
        return self.buffer

    def put(self, index):
        pass


class Stored:
    def __init__(self, target, buffer, sems):
        self.target, self.buffer, self.sems, self.copies = target, buffer, sems, []

    def put(self, index):
        copy = pltpu.make_async_copy(
            self.buffer.at[index], self.target.at[index], self.sems.at[len(self.copies)]
        )
        copy.start()
        self.copies.append(copy)

    def finish(self):
        for copy in self.copies:
            copy.wait()


class Into:
    def __init__(self, result, cut):
        self.result, self.cut = result, cut

    def __len__(self):
        return len(self.cut)


WHOLE = (slice(None),)


def by_piece(n):
    return tuple(pl.ds(i, 1) for i in range(n))


def call(body, operands, results, scratch=(), flops=1 << 20, moved=1 << 20):
    space = {"idle": pltpu.HBM, "smem": pltpu.SMEM, "vmem": pltpu.VMEM, "held": pltpu.VMEM}
    modes = [mode for _, mode in operands]
    here = [isinstance(mode, str) for mode in modes]
    in_specs = [
        pl.BlockSpec(memory_space=space[m] if h else pltpu.HBM) for m, h in zip(modes, here)
    ]
    out_specs = [pl.BlockSpec(memory_space=pltpu.HBM if n else pltpu.VMEM) for _, n in results]
    buffers = []
    kinds = {mode.result: array.dtype for array, mode in operands if isinstance(mode, Into)}
    for array, mode in operands:
        if isinstance(mode, tuple):
            buffers.append(pltpu.VMEM(array.shape, array.dtype))
        if not isinstance(mode, str):
            buffers.append(pltpu.SemaphoreType.DMA((len(mode),)))
    for dims, n in results:
        if n > 0:
            buffers += [pltpu.VMEM(dims, F32), pltpu.SemaphoreType.DMA((n,))]

    def kernel(*refs):
        ins, refs = refs[: len(modes)], refs[len(modes) :]
        outs, refs = refs[: len(results)], list(refs[len(results) :])
        args, loads = [], []
        for ref, mode, h in zip(ins, modes, here):
            if h:
                args.append(Held(ref) if mode == "held" else ref)
            else:
                into = isinstance(mode, Into)
                buffer = outs[mode.result] if into else refs.pop(0)
                args.append(Loaded(ref, buffer, refs.pop(0), mode.cut if into else mode))
                loads.append(args[-1])
        for i in range(max([len(x.copies) for x in loads], default=0)):
            for x in loads:
                if i < len(x.copies):
                    x.start(i)
        stores = []
        for ref, (_, n) in zip(outs, results):
            if n > 0:
                args.append(Stored(ref, refs.pop(0), refs.pop(0)))
                stores.append(args[-1])
            else:
                args.append(ref if n else Held(ref))
        body(*args, *refs)
        for x in loads:
            x.whole()
        for x in stores:
            x.finish()

    return pl.pallas_call(
        kernel,
        out_shape=[pltpu.HBM(dims, F32) if n else jax.ShapeDtypeStruct(dims, kinds.get(k, F32)) for k, (dims, n) in enumerate(results)],
        in_specs=in_specs,
        out_specs=out_specs,
        scratch_shapes=buffers + list(scratch),
        compiler_params=pltpu.CompilerParams(vmem_limit_bytes=24 << 20),
        cost_estimate=pl.CostEstimate(flops=flops, bytes_accessed=moved, transcendentals=0),
    )(
        *[
            a if h and m != "idle" else pltpu.with_memory_space_constraint(a, pltpu.HBM)
            for (a, m), h in zip(operands, here)
        ]
    )


def shape(*dims):
    return jax.ShapeDtypeStruct(dims, F32)


def row_index(n=SPAN):
    return lax.broadcasted_iota(jnp.int32, (ROWS, n), 0)


def split(x):
    high = x.astype(BF16)
    return high, (x - high.astype(F32)).astype(BF16)


def one_hot(index, n):
    cell = lax.broadcasted_iota(jnp.int32, (n, NF), 0)
    return jnp.where(cell == index, 1.0, 0.0).astype(BF16)


def at_faces(field, span_hot, row_hot):
    n = field.shape[-1]
    both = jnp.concatenate(split(field.reshape(CH * ROWS, n)), axis=0)
    picked = jnp.dot(both, span_hot, preferred_element_type=F32)
    picked = (picked[: CH * ROWS] + picked[CH * ROWS :]).reshape(CH, ROWS, NF)
    return jnp.sum(picked * row_hot[None], axis=1)


def onto_cells(values, span_hot, row_hot):
    spread = (values[:, None, :] * row_hot[None]).reshape(CH * ROWS, NF)
    both = jnp.concatenate(split(spread), axis=0)
    out = lax.dot_general(both, span_hot, (((1,), (1,)), ((), ())), preferred_element_type=F32)
    return (out[: CH * ROWS] + out[CH * ROWS :]).reshape(CH, ROWS, span_hot.shape[0])


def fluid_hots(ff_ref):
    cell = ff_ref[...]
    span = one_hot(cell & (SPAN - 1), SPAN)
    rows = jnp.where(row_index(NF) == (cell >> 10), 1.0, 0.0)
    return span, rows


def metal_hots(mf_ref):
    cell = mf_ref[...]
    span = one_hot(cell & (MSPAN - 1), MSPAN)
    rows = jnp.where(row_index(NF) == (cell >> 9), 1.0, 0.0)
    return span, rows


def span_sides(a):
    n = a.shape[-1]
    lane = lax.broadcasted_iota(jnp.int32, a.shape, a.ndim - 1)
    north = jnp.where(lane == n - 1, 0.0, pltpu.roll(a, n - 1, a.ndim - 1))
    south = jnp.where(lane == 0, 0.0, pltpu.roll(a, 1, a.ndim - 1))
    return north, south


def stencil_parts(a, before, after):
    row = row_index(a.shape[-1])
    east_one = pltpu.roll(jnp.where(row == 0, after, a), 7, 0)
    east_two = pltpu.roll(jnp.where(row < 2, after, a), 6, 0)
    west_one = pltpu.roll(jnp.where(row == 7, before, a), 1, 0)
    west_two = pltpu.roll(jnp.where(row >= 6, before, a), 2, 0)
    north, south = span_sides(a)
    rest = (
        (4.0 * damping_fourth) * (east_one + west_one)
        - damping_fourth * (east_two + west_two)
        + viscous_coef * (north + south)
        - (6.0 * damping_fourth + 2.0 * viscous_coef + sigma_fluid) * a
    )
    return east_one - west_one, north - south, rest


def edge_tile(ref, tile):
    return jnp.concatenate([ref[2 * tile], ref[2 * tile + 1]], axis=1)


def halo_pair(up_ref, down_ref, t, v):
    tile, slot = (t, v) if v < 4 else (6 + t // 4, t % 4)
    before = pltpu.roll(edge_tile(up_ref, tile), (6 - 2 * slot) % 8, 0)
    after = pltpu.roll(edge_tile(down_ref, tile), (8 - 2 * slot) % 8, 0)
    return before, after


def pack_tile(blocks, tile, up_ref, down_ref):
    row = row_index()
    up = down = None
    for slot, a in enumerate(blocks):
        u = pltpu.roll(a, (2 * slot + 2) % 8, 0) if (2 * slot + 2) % 8 else a
        d = pltpu.roll(a, 2 * slot, 0) if slot else a
        mine = (row >> 1) == slot
        up = u if up is None else jnp.where(mine, u, up)
        down = d if down is None else jnp.where(mine, d, down)
    for half in range(2):
        cut = slice(half * 512, half * 512 + 512)
        up_ref[2 * tile + half] = up[:, cut]
        down_ref[2 * tile + half] = down[:, cut]


def pack_last(get, extra, up_ref, down_ref):
    pack_tile([get(t) for t in range(4)], 6, up_ref, down_ref)
    pack_tile([get(4), get(5), extra, extra], 7, up_ref, down_ref)


def prepare_kernel(a, ps, m_in, up, down, a_copy, ps_copy):
    for t in range(6):
        ref = a.piece(t)
        pack_tile([ref[t, v] for v in range(4)], t, up.buffer, down.buffer)
        for x in (up, down):
            x.put(pl.ds(2 * t, 2))
    pack_last(lambda t: a.buffer[t, NV - 1], ps.whole()[...], up.buffer, down.buffer)
    metal_edges(m_in.whole(), up.buffer.at[16], down.buffer.at[16])
    for x in (up, down):
        x.put(pl.ds(12, 5))


def energy_kernel(tab_ref, m_ref, fc_ref, ff_ref, mf_ref, after, e):
    first = lax.axis_index("inst") * 6
    m_hot, m_row = metal_hots(mf_ref)
    f_hot, f_row = fluid_hots(ff_ref)
    values = at_faces(m_ref[...], m_hot, m_row) * fc_ref[...]
    cells = onto_cells(values, f_hot, f_row)
    for t in range(6):
        e.buffer[t] = combine(tab_ref, SYNTH, first + t, cells)
        e.put(pl.ds(t, 1))


def combine(tab_ref, base, t, fields):
    total = tab_ref[base + t * CH] * fields[0]
    for ch in range(1, CH):
        if ch != NH:
            total += tab_ref[base + t * CH + ch] * fields[ch]
    return total


def convect(jx_ref, jz_ref, dx, dz, rest, u):
    out = rest
    for v in range(NV):
        out = out - (0.5 * jx_ref[u, v]) * dx[v] - (0.5 * jz_ref[u, v]) * dz[v]
    return out


def inner_kernel(jx_ref, jz_ref, a_ref, s_ref, ps_ref, b, q, blocks, parts, sems):
    step = ps_ref[...]
    copies = [
        pltpu.make_async_copy(
            a_ref.at[:, :, :, pl.ds(i * CHUNK, CHUNK)], blocks.at[i], sems.at[i]
        )
        for i in range(8)
    ]
    for copy in copies:
        copy.start()
    for t in range(6):
        for v in range(NV):
            a = a_ref[t, v]
            dx, dz, rest = stencil_parts(a, 0.0, 0.0)
            parts[0, v], parts[1, v], parts[2, v] = dx, dz, rest
            dx, dz, rest = stencil_parts(step * a, 0.0, 0.0)
            parts[3, v], parts[4, v], parts[5, v] = dx, dz, rest
        for i in range(8):
            cut = pl.ds(i * CHUNK, CHUNK)
            dx = [parts[0, v, :, cut] for v in range(NV)]
            dz = [parts[1, v, :, cut] for v in range(NV)]
            px = [parts[3, v, :, cut] for v in range(NV)]
            pz = [parts[4, v, :, cut] for v in range(NV)]
            for u in range(NV):
                a = a_ref[t, u, :, cut]
                space = convect(jx_ref, jz_ref, dx, dz, parts[2, u, :, cut], u)
                source = s_ref[t, u, :, cut] + space
                inner = a + ps_ref[:, cut] * source
                b.buffer[t, u, :, cut] = inner
                q.buffer[t, u, :, cut] = a + inner + convect(jx_ref, jz_ref, px, pz, parts[5, u, :, cut], u)
        b.put(pl.ds(t, 1))
        q.put(pl.ds(t, 1))
    for copy in copies:
        copy.wait()


def edge_terms(up_ref, down_ref, half, t, v):
    tile, slot = (t, v) if v < 4 else (6 + t // 4, t % 4)
    row = row_index(512)
    up, down = up_ref[2 * tile + half], down_ref[2 * tile + half]
    one = pltpu.roll(jnp.where(row == 2 * slot, down, up), (7 - 2 * slot) % 8, 0)
    one = jnp.where((row == 0) | (row == 7), one, 0.0)
    east_two = pltpu.roll(down, (6 - 2 * slot) % 8, 0)
    west_two = pltpu.roll(up, (8 - 2 * slot) % 8, 0)
    two = jnp.where(row >= 6, east_two, jnp.where(row < 2, west_two, 0.0))
    return one, two


def first_kernel(
    tab_ref, jx_ref, jz_ref, a_ref, bi_ref, qi_ref, e_ref, ps_ref, up_ref, down_ref, fc_ref, ff_ref, m_ref, cond_ref,
    q, b_out, bup, bdown, q4, m_out,
):
    first = lax.axis_index("inst") * 6
    step = ps_ref[...]
    q_ref, b_ref = q.buffer, b_out.buffer
    sign = jnp.where(row_index(512) == 0, 0.5, -0.5)
    step_edges = []
    for half in range(2):
        tile = 14 + half
        row = row_index(512)
        up, down = up_ref[tile], down_ref[tile]
        one = jnp.where(row == 7, pltpu.roll(down, 3, 0), pltpu.roll(up, 3, 0))
        two = jnp.where(row >= 6, pltpu.roll(down, 2, 0), pltpu.roll(up, 4, 0))
        step_edges.append((one, two))
    for t in range(6):
        for half in range(2):
            wide = pl.ds(half * 512, 512)
            here = ps_ref[:, wide]
            step_one, step_two = step_edges[half]
            edges = [edge_terms(up_ref, down_ref, half, t, v) for v in range(NV)]
            for u in range(NV):
                total = jx_ref[u, 0] * edges[0][0]
                for v in range(1, NV):
                    total += jx_ref[u, v] * edges[v][0]
                one = sign * total + (4.0 * damping_fourth) * edges[u][0]
                two = damping_fourth * edges[u][1]
                change = one - two
                if u == NV - 1:
                    change = change + e_ref[t, :, wide]
                change = here * change
                b_ref[t, u, :, wide] = bi_ref[t, u, :, wide] + change
                value = qi_ref[t, u, :, wide] + change + (step_one * one - step_two * two)
                for i in range(4):
                    q_ref[4 * half + i, t * NV + u] = value[:, i * CHUNK : (i + 1) * CHUNK]
                if u == NV - 1:
                    q4.buffer[t, :, wide] = value
        q.put((slice(None), pl.ds(t * NV, NV)))
        b_out.put(pl.ds(t, 1))
        pack_tile([b_ref[t, v] for v in range(4)], t, bup.buffer, bdown.buffer)
    pack_last(lambda t: b_ref[t, NV - 1], step, bup.buffer, bdown.buffer)
    q4.put(slice(None))
    bup.put(slice(None))
    bdown.put(slice(None))
    f_hot, f_row = fluid_hots(ff_ref)
    heat = []
    for ch in range(CH):
        h0 = h1 = jnp.zeros((ROWS, SPAN), F32)
        for t in range(6 if ch != NH else 0):
            at = (first + t) * CH + ch
            h0 += tab_ref[W0 + at] * b_ref[t, NV - 1]
            h1 += tab_ref[W1 + at] * a_ref[t, NV - 1]
        heat.append(h0 - step * h1)
    values = at_faces(jnp.stack(heat), f_hot, f_row) * fc_ref[...]
    for i in range(8):
        for k in range(4):
            q_ref[i, 30 + k] = values[:, k * CHUNK : (k + 1) * CHUNK]
    q.put((slice(None), pl.ds(30, 4)))
    before, after = metal_sides(up_ref.at[16], down_ref.at[16])
    m = metal_update(m_ref, before, after, cond_ref[...])
    for ch in range(CH):
        m_out.buffer[ch] = m[ch]
    m_out.put(slice(None))


def rotate_time(kron, x):
    high, low = split(x)
    return jnp.dot(kron, jnp.concatenate([high, low, high], axis=0), preferred_element_type=F32)


def local_step(ps_ref):
    start = pl.multiple_of(lax.axis_index("inst") * CHUNK, CHUNK)
    return ps_ref[:, pl.ds(start, CHUNK)]


def turned(get):
    return jnp.concatenate(
        [
            jnp.concatenate([get(j, t, v) for j in range(8) for t in range(6)], axis=0)
            for v in range(NV)
        ],
        axis=1,
    )


def derive_kernel(kron_ref, a_ref, ps_ref, g):
    wide = jnp.concatenate([local_step(ps_ref)] * NV, axis=1)
    x = turned(lambda j, t, v: a_ref[j, t, v])
    d = rotate_time(kron_ref[...], x)
    g.buffer[...] = (d.reshape(NT, ROWS, NV * CHUNK) * wide[None]).reshape(NT * ROWS, NV * CHUNK)
    g.put(slice(None))


def middle_kernel(
    tab_ref, jx_ref, jz_ref, b_in, s_in, ps_ref, up_ref, down_ref, a_ref, q4_ref, g_ref,
    c_out, hc,
    parts,
):
    first = lax.axis_index("inst") * 6
    c_ref = c_out.buffer
    for t in range(6):
        b_ref, s_ref = b_in.piece(t), s_in.piece(t)
        for v in range(NV):
            before, after = halo_pair(up_ref, down_ref, t, v)
            dx, dz, rest = stencil_parts(b_ref[t, v], before, after)
            parts[0, v], parts[1, v], parts[2, v] = dx, dz, rest
        for i in range(8):
            cut = pl.ds(i * CHUNK, CHUNK)
            dx = [parts[0, v, :, cut] for v in range(NV)]
            dz = [parts[1, v, :, cut] for v in range(NV)]
            for u in range(NV):
                space = convect(jx_ref, jz_ref, dx, dz, parts[2, u, :, cut], u)
                c_ref[t, u, :, cut] = b_ref[t, u, :, cut] + ps_ref[:, cut] * (s_ref[t, u, :, cut] + space)
        c_out.put(pl.ds(t, 1))
    step = ps_ref[...]
    for ch in range(CH):
        h0 = h2 = h3 = jnp.zeros((ROWS, SPAN), F32)
        for t in range(6 if ch != NH else 0):
            at = (first + t) * CH + ch
            h0 += tab_ref[W0 + at] * c_ref[t, NV - 1]
            h2 += tab_ref[W1 + at] * q4_ref[t]
            h3 += tab_ref[W2 + at] * a_ref[t, NV - 1]
        hc.buffer[ch] = h0 + step * (step * h3 - h2)
    hc.put(slice(None))


def metal_update(m, before, after, cond):
    row = row_index(MSPAN)
    out = []
    for ch in range(CH):
        a = m[ch]
        east = pltpu.roll(jnp.where(row == 0, after[ch], a), 7, 0)
        west = pltpu.roll(jnp.where(row == 7, before[ch], a), 1, 0)
        north, south = span_sides(a)
        laplace = east + west + north + south - 4.0 * a
        h = ch % NH
        turn = -heat_capacity * h * m[ch + NH] if ch < NH else heat_capacity * h * m[ch - NH]
        out.append(a + metal_step * (cond * laplace - sigma_metal * a - turn))
    return out


def metal_edges(m, up_ref, down_ref):
    up_ref[...] = jnp.concatenate([m[ch][7:8] for ch in range(CH)], axis=0)
    down_ref[...] = jnp.concatenate([m[ch][0:1] for ch in range(CH)], axis=0)


def metal_sides(up_ref, down_ref):
    before = [jnp.broadcast_to(up_ref[ch : ch + 1], (ROWS, MSPAN)) for ch in range(CH)]
    after = [jnp.broadcast_to(down_ref[ch : ch + 1], (ROWS, MSPAN)) for ch in range(CH)]
    return before, after


def heat_sum(get):
    tiles = []
    for k in range(4):
        total = get(0, k)
        for j in range(1, 8):
            total += get(j, k)
        tiles.append(total)
    return jnp.concatenate(tiles, axis=1)


def second_kernel(
    tab_ref, q_ref, g_ref, kron_ref, ps_ref, m_ref, fc_ref, ff_ref, mf_ref, hc_ref,
    v, m_out, mup, mdown, e,
):
    first = lax.axis_index("inst") * 6
    v_ref = v.buffer
    near = local_step(ps_ref)
    x = turned(lambda j, t, u: q_ref[j, t * NV + u]) - g_ref[...]
    for half in range(2):
        d = rotate_time(kron_ref[pl.ds(half * 192, 192), :], x)
        for j in range(4):
            for t in range(6):
                at = (j * 6 + t) * ROWS
                for u in range(NV):
                    v_ref[half * 4 + j, t * NV + u] = -near * d[at : at + ROWS, u * CHUNK : (u + 1) * CHUNK]
        v.put((pl.ds(half * 4, 4), pl.ds(0, 30)))
    step = ps_ref[...]
    coeff = fc_ref[...]
    m_hot, m_row = metal_hots(mf_ref)
    f_hot, f_row = fluid_hots(ff_ref)
    source = onto_cells(heat_sum(lambda j, k: q_ref[j, 30 + k]), m_hot, m_row)
    m = [m_ref[ch] + metal_step * source[ch] for ch in range(CH)]
    for ch in range(CH):
        m_out.buffer[ch] = m[ch]
    m_out.put(slice(None))
    metal_edges(m, mup.buffer, mdown.buffer)
    mup.put(slice(None))
    mdown.put(slice(None))
    cells = onto_cells(at_faces(jnp.stack(m), m_hot, m_row) * coeff, f_hot, f_row)
    for t in range(6):
        e.buffer[t] = step * combine(tab_ref, SYNTH, first + t, cells)
    e.put(slice(None))
    heat = []
    for ch in range(CH):
        total = hc_ref[ch]
        for t in range(6):
            total += tab_ref[W0 + (first + t) * CH + ch] * e.buffer[t]
        heat.append(total)
    values = at_faces(jnp.stack(heat), f_hot, f_row) * coeff
    for i in range(8):
        for k in range(4):
            v_ref[i, 30 + k] = values[:, k * CHUNK : (k + 1) * CHUNK]
    v.put((slice(None), pl.ds(30, 4)))


def last_kernel(v, c, e, m_in, mup_ref, mdown_ref, cond_ref, mf_ref, out, m_out):
    for t in range(6):
        v_ref, c_ref, e_ref = v.piece(t), c.piece(t), e.whole()
        for i in range(8):
            cut = pl.ds(i * CHUNK, CHUNK)
            for u in range(NV):
                total = c_ref[t, u, :, cut] + v_ref[i, t * NV + u]
                if u == NV - 1:
                    total = total + e_ref[t, :, cut]
                out.buffer[t, u, :, cut] = total
        out.put(pl.ds(t, 1))
    m_hot, m_row = metal_hots(mf_ref)
    source = onto_cells(heat_sum(lambda j, k: v.buffer[j, 30 + k]), m_hot, m_row)
    before, after = metal_sides(mup_ref, mdown_ref)
    m = metal_update(m_in.whole(), before, after, cond_ref[...])
    for ch in range(CH):
        m_out.buffer[ch] = m[ch] + metal_step * source[ch]
    m_out.put(slice(None))


def exchange(up, down):
    n = lax.axis_size("space")
    forward = [(i, (i + 1) % n) for i in range(n)]
    back = [(j, i) for i, j in forward]
    return lax.ppermute(up, "space", forward), lax.ppermute(down, "space", back)


def turn(x):
    return lax.all_to_all(x, "inst", 0, 0, tiled=True)


SIX = by_piece(6)
EDGES = (17, ROWS, 512)
FLUID = (6, NV, ROWS, SPAN)
METAL = (CH, ROWS, MSPAN)
ONE = (6, ROWS, SPAN)
BLOCKS = (8, 34, ROWS, CHUNK)


LONG = 1 << 36


def plain(*arrays):
    return [(array, "vmem") for array in arrays]


def late(*arrays):
    return [(array, WHOLE) for array in arrays]


def held(*arrays):
    return [(array, "held") for array in arrays]


def local(a0, source, ps, jx, jz, metal, cond, coeff, ff, mf):
    kron = jnp.asarray(KRON)
    tab = jnp.asarray(FLAT)
    coeff, ff, mf = (x.reshape(1, NF) for x in (coeff, ff, mf))
    metal = metal.reshape(METAL)
    up, down, a_here, ps_here = call(
        prepare_kernel,
        [(a0, Into(2, SIX)), (ps, Into(3, WHOLE))] + late(metal),
        [(EDGES, 7), (EDGES, 7), (FLUID, 0), ((ROWS, SPAN), 0)],
    )
    up, down = exchange(up, down)
    scalars = [(tab, "smem"), (jx, "smem"), (jz, "smem")]
    last_variable = (a0, ((slice(None), pl.ds(NV - 1, 1)),))
    b, q, blocks = call(
        inner_kernel,
        scalars[1:] + plain(a_here, source, ps_here),
        [(FLUID, 6), (FLUID, 6), ((8, 6, NV, ROWS, CHUNK), -1)],
        scratch=[pltpu.VMEM((6, NV, ROWS, SPAN), F32), pltpu.SemaphoreType.DMA((8,))],
    )
    (e0,) = call(
        energy_kernel,
        scalars[:1] + plain(metal, coeff, ff, mf) + [(blocks, "idle")],
        [(ONE, 0)],
        flops=LONG,
    )
    a_turned = turn(blocks)
    q, b, bup, bdown, q4, metal = call(
        first_kernel,
        scalars + [last_variable] + plain(b, q, e0, ps, up, down, coeff, ff, metal, cond),
        [(BLOCKS, 7), (FLUID, 6), (EDGES, 1), (EDGES, 1), (ONE, 1), (METAL, 1)],
    )
    q_turned = turn(q)
    bup, bdown = exchange(bup, bdown)
    (g,) = call(derive_kernel, plain(kron, a_turned, ps), [((NT * ROWS, NV * CHUNK), 0)])
    c, hc = call(
        middle_kernel,
        scalars + [(b, SIX), (source, SIX)] + late(ps) + plain(bup, bdown) + [last_variable] + late(q4)
        + plain(g),
        [(FLUID, 0), ((CH, ROWS, SPAN), 0)],
        scratch=[pltpu.VMEM((3, NV, ROWS, SPAN), F32)],
        flops=LONG,
    )
    v, metal, mup, mdown, e1 = call(
        second_kernel,
        scalars[:1] + plain(q_turned, g, kron, ps, metal, coeff, ff, mf, hc),
        [(BLOCKS, 3), (METAL, 1), ((CH, MSPAN), 1), ((CH, MSPAN), 1), (ONE, 1)],
    )
    v = turn(v)
    mup, mdown = exchange(mup, mdown)
    out, metal = call(
        last_kernel, held(v, c, e1, metal) + plain(mup, mdown, cond, mf), [(FLUID, 6), (METAL, 1)]
    )
    return out, metal.reshape(2, NH, ROWS, MSPAN)


def solution(mesh):
    return jax.shard_map(
        local,
        mesh=mesh,
        in_specs=(
            P("inst", None, "space", None),
            P("inst", None, "space", None),
            P("space", None),
            P(),
            P(),
            P(None, None, "space", None),
            P("space", None),
            P("space"),
            P("space"),
            P("space"),
        ),
        out_specs=(P("inst", None, "space", None), P(None, None, "space", None)),
        check_vma=False,
    )
```

```python
import math

import jax
import jax.numpy as jnp
import ml_dtypes
import numpy as np
from jax import lax
from jax.experimental import pallas as pl
from jax.experimental.pallas import tpu as pltpu
from jax.sharding import PartitionSpec as P

NT, NV, NH = 48, 5, 4
ROWS, SPAN, MSPAN, NF = 8, 1024, 512, 512
CHUNK = 128
CH = 2 * NH
F32, BF16 = jnp.float32, jnp.bfloat16

damping_fourth = 1.0 / 32.0
viscous_coef = 0.1
sigma_fluid = 0.5
metal_step = 0.2
sigma_metal = 0.5
heat_capacity = 0.5
flux_scale = 4.0


def tables():
    t = np.arange(NT)
    offset = t[:, None] - t[None, :]
    angle = np.where(offset == 0, 0.5, math.pi * offset / NT)
    spectral = np.where(
        offset == 0, 0.0, 0.5 * (1.0 - 2.0 * (offset % 2)) * np.cos(angle) / np.sin(angle)
    )
    phase = 2.0 * math.pi * ((np.arange(NH)[:, None] * t[None, :]) % NT) / NT
    synth = np.concatenate([np.cos(phase), -np.sin(phase)])
    w0 = synth * (flux_scale / NT)
    w1 = w0 @ spectral
    w2 = w1 @ spectral
    high = spectral.astype(np.float32).astype(ml_dtypes.bfloat16)
    low = (spectral - high.astype(np.float64)).astype(np.float32).astype(ml_dtypes.bfloat16)
    eye = np.eye(ROWS, dtype=np.float32)
    kron_high = np.kron(high.astype(np.float32), eye)
    kron_low = np.kron(low.astype(np.float32), eye)
    kron = np.concatenate([kron_high, kron_high, kron_low], axis=1).astype(ml_dtypes.bfloat16)
    flat = np.concatenate([m.T.reshape(-1) for m in (synth, w0, w1, w2)]).astype(np.float32)
    return kron, flat


KRON, FLAT = tables()
SYNTH, W0, W1, W2 = (i * NT * CH for i in range(4))


class Loaded:
    def __init__(self, source, buffer, sems, cut):
        self.buffer, self.copies = buffer, []
        for i, index in enumerate(cut):
            self.copies.append(pltpu.make_async_copy(source.at[index], buffer.at[index], sems.at[i]))
        self.waiting = set(range(len(cut)))

    def start(self, i):
        self.copies[i].start()

    def piece(self, i):
        if i in self.waiting:
            self.waiting.remove(i)
            self.copies[i].wait()
        return self.buffer

    def whole(self):
        for i in range(len(self.copies)):
            self.piece(i)
        return self.buffer

    def __getitem__(self, index):
        return self.whole()[index]


class Held:
    def __init__(self, ref):
        self.buffer = ref

    def piece(self, i):
        return self.buffer

    def whole(self):
        return self.buffer

    def put(self, index):
        pass


class Stored:
    def __init__(self, target, buffer, sems):
        self.target, self.buffer, self.sems, self.copies = target, buffer, sems, []

    def put(self, index):
        copy = pltpu.make_async_copy(
            self.buffer.at[index], self.target.at[index], self.sems.at[len(self.copies)]
        )
        copy.start()
        self.copies.append(copy)

    def finish(self):
        for copy in self.copies:
            copy.wait()


class Into:
    def __init__(self, result, cut):
        self.result, self.cut = result, cut

    def __len__(self):
        return len(self.cut)


WHOLE = (slice(None),)


def by_piece(n):
    return tuple(pl.ds(i, 1) for i in range(n))


def call(body, operands, results, scratch=(), flops=1 << 20, moved=1 << 20):
    space = {"idle": pltpu.HBM, "smem": pltpu.SMEM, "vmem": pltpu.VMEM, "held": pltpu.VMEM}
    modes = [mode for _, mode in operands]
    here = [isinstance(mode, str) for mode in modes]
    in_specs = [
        pl.BlockSpec(memory_space=space[m] if h else pltpu.HBM) for m, h in zip(modes, here)
    ]
    out_specs = [pl.BlockSpec(memory_space=pltpu.HBM if n else pltpu.VMEM) for _, n in results]
    buffers = []
    kinds = {mode.result: array.dtype for array, mode in operands if isinstance(mode, Into)}
    for array, mode in operands:
        if isinstance(mode, tuple):
            buffers.append(pltpu.VMEM(array.shape, array.dtype))
        if not isinstance(mode, str):
            buffers.append(pltpu.SemaphoreType.DMA((len(mode),)))
    for dims, n in results:
        if n > 0:
            buffers += [pltpu.VMEM(dims, F32), pltpu.SemaphoreType.DMA((n,))]

    def kernel(*refs):
        ins, refs = refs[: len(modes)], refs[len(modes) :]
        outs, refs = refs[: len(results)], list(refs[len(results) :])
        args, loads = [], []
        for ref, mode, h in zip(ins, modes, here):
            if h:
                args.append(Held(ref) if mode == "held" else ref)
            else:
                into = isinstance(mode, Into)
                buffer = outs[mode.result] if into else refs.pop(0)
                args.append(Loaded(ref, buffer, refs.pop(0), mode.cut if into else mode))
                loads.append(args[-1])
        for i in range(max([len(x.copies) for x in loads], default=0)):
            for x in loads:
                if i < len(x.copies):
                    x.start(i)
        stores = []
        for ref, (_, n) in zip(outs, results):
            if n > 0:
                args.append(Stored(ref, refs.pop(0), refs.pop(0)))
                stores.append(args[-1])
            else:
                args.append(ref if n else Held(ref))
        body(*args, *refs)
        for x in loads:
            x.whole()
        for x in stores:
            x.finish()

    return pl.pallas_call(
        kernel,
        out_shape=[pltpu.HBM(dims, F32) if n else jax.ShapeDtypeStruct(dims, kinds.get(k, F32)) for k, (dims, n) in enumerate(results)],
        in_specs=in_specs,
        out_specs=out_specs,
        scratch_shapes=buffers + list(scratch),
        compiler_params=pltpu.CompilerParams(vmem_limit_bytes=24 << 20),
        cost_estimate=pl.CostEstimate(flops=flops, bytes_accessed=moved, transcendentals=0),
    )(
        *[
            a if h and m != "idle" else pltpu.with_memory_space_constraint(a, pltpu.HBM)
            for (a, m), h in zip(operands, here)
        ]
    )


def shape(*dims):
    return jax.ShapeDtypeStruct(dims, F32)


def row_index(n=SPAN):
    return lax.broadcasted_iota(jnp.int32, (ROWS, n), 0)


def split(x):
    high = x.astype(BF16)
    return high, (x - high.astype(F32)).astype(BF16)


def one_hot(index, n):
    cell = lax.broadcasted_iota(jnp.int32, (n, NF), 0)
    return jnp.where(cell == index, 1.0, 0.0).astype(BF16)


def at_faces(field, span_hot, row_hot):
    n = field.shape[-1]
    both = jnp.concatenate(split(field.reshape(CH * ROWS, n)), axis=0)
    picked = jnp.dot(both, span_hot, preferred_element_type=F32)
    picked = (picked[: CH * ROWS] + picked[CH * ROWS :]).reshape(CH, ROWS, NF)
    return jnp.sum(picked * row_hot[None], axis=1)


def onto_cells(values, span_hot, row_hot):
    spread = (values[:, None, :] * row_hot[None]).reshape(CH * ROWS, NF)
    both = jnp.concatenate(split(spread), axis=0)
    out = lax.dot_general(both, span_hot, (((1,), (1,)), ((), ())), preferred_element_type=F32)
    return (out[: CH * ROWS] + out[CH * ROWS :]).reshape(CH, ROWS, span_hot.shape[0])


def fluid_hots(ff_ref):
    cell = ff_ref[...]
    span = one_hot(cell & (SPAN - 1), SPAN)
    rows = jnp.where(row_index(NF) == (cell >> 10), 1.0, 0.0)
    return span, rows


def metal_hots(mf_ref):
    cell = mf_ref[...]
    span = one_hot(cell & (MSPAN - 1), MSPAN)
    rows = jnp.where(row_index(NF) == (cell >> 9), 1.0, 0.0)
    return span, rows


def span_sides(a):
    n = a.shape[-1]
    lane = lax.broadcasted_iota(jnp.int32, a.shape, a.ndim - 1)
    north = jnp.where(lane == n - 1, 0.0, pltpu.roll(a, n - 1, a.ndim - 1))
    south = jnp.where(lane == 0, 0.0, pltpu.roll(a, 1, a.ndim - 1))
    return north, south


def stencil_parts(a, before, after):
    row = row_index(a.shape[-1])
    east_one = pltpu.roll(jnp.where(row == 0, after, a), 7, 0)
    east_two = pltpu.roll(jnp.where(row < 2, after, a), 6, 0)
    west_one = pltpu.roll(jnp.where(row == 7, before, a), 1, 0)
    west_two = pltpu.roll(jnp.where(row >= 6, before, a), 2, 0)
    north, south = span_sides(a)
    rest = (
        (4.0 * damping_fourth) * (east_one + west_one)
        - damping_fourth * (east_two + west_two)
        + viscous_coef * (north + south)
        - (6.0 * damping_fourth + 2.0 * viscous_coef + sigma_fluid) * a
    )
    return east_one - west_one, north - south, rest


def edge_tile(ref, tile):
    return jnp.concatenate([ref[2 * tile], ref[2 * tile + 1]], axis=1)


def halo_pair(up_ref, down_ref, t, v):
    tile, slot = (t, v) if v < 4 else (6 + t // 4, t % 4)
    before = pltpu.roll(edge_tile(up_ref, tile), (6 - 2 * slot) % 8, 0)
    after = pltpu.roll(edge_tile(down_ref, tile), (8 - 2 * slot) % 8, 0)
    return before, after


def pack_tile(blocks, tile, up_ref, down_ref):
    row = row_index()
    up = down = None
    for slot, a in enumerate(blocks):
        u = pltpu.roll(a, (2 * slot + 2) % 8, 0) if (2 * slot + 2) % 8 else a
        d = pltpu.roll(a, 2 * slot, 0) if slot else a
        mine = (row >> 1) == slot
        up = u if up is None else jnp.where(mine, u, up)
        down = d if down is None else jnp.where(mine, d, down)
    for half in range(2):
        cut = slice(half * 512, half * 512 + 512)
        up_ref[2 * tile + half] = up[:, cut]
        down_ref[2 * tile + half] = down[:, cut]


def pack_last(get, extra, up_ref, down_ref):
    pack_tile([get(t) for t in range(4)], 6, up_ref, down_ref)
    pack_tile([get(4), get(5), extra, extra], 7, up_ref, down_ref)


def prepare_kernel(a, ps, m_in, up, down):
    for t in range(6):
        a.piece(2 * t)
        ref = a.piece(2 * t + 1)
        pack_tile([ref[t, v] for v in range(4)], t, up.buffer, down.buffer)
        for x in (up, down):
            x.put(pl.ds(2 * t, 2))
    pack_last(lambda t: a.buffer[t, NV - 1], ps[...], up.buffer, down.buffer)
    metal_edges(m_in.whole(), up.buffer.at[16], down.buffer.at[16])
    for x in (up, down):
        x.put(pl.ds(12, 5))


def energy_kernel(tab_ref, m_ref, fc_ref, ff_ref, mf_ref, after, e):
    first = lax.axis_index("inst") * 6
    m_hot, m_row = metal_hots(mf_ref)
    f_hot, f_row = fluid_hots(ff_ref)
    values = at_faces(m_ref[...], m_hot, m_row) * fc_ref[...]
    cells = onto_cells(values, f_hot, f_row)
    for t in range(6):
        e.buffer[t] = combine(tab_ref, SYNTH, first + t, cells)
        e.put(pl.ds(t, 1))


def combine(tab_ref, base, t, fields):
    total = tab_ref[base + t * CH] * fields[0]
    for ch in range(1, CH):
        if ch != NH:
            total += tab_ref[base + t * CH + ch] * fields[ch]
    return total


def convect(jx_ref, jz_ref, dx, dz, rest, u):
    out = rest
    for v in range(NV):
        out = out - (0.5 * jx_ref[u, v]) * dx[v] - (0.5 * jz_ref[u, v]) * dz[v]
    return out


def inner_kernel(jx_ref, jz_ref, a_ref, s_ref, ps_ref, b, q, blocks, parts, sems):
    step = ps_ref[...]
    copies = [
        pltpu.make_async_copy(
            a_ref.at[:, :, :, pl.ds(i * CHUNK, CHUNK)], blocks.at[i], sems.at[i]
        )
        for i in range(8)
    ]
    for copy in copies:
        copy.start()
    for t in range(6):
        for v in range(NV):
            a = a_ref[t, v]
            dx, dz, rest = stencil_parts(a, 0.0, 0.0)
            parts[0, v], parts[1, v], parts[2, v] = dx, dz, rest
            dx, dz, rest = stencil_parts(step * a, 0.0, 0.0)
            parts[3, v], parts[4, v], parts[5, v] = dx, dz, rest
        for i in range(8):
            cut = pl.ds(i * CHUNK, CHUNK)
            dx = [parts[0, v, :, cut] for v in range(NV)]
            dz = [parts[1, v, :, cut] for v in range(NV)]
            px = [parts[3, v, :, cut] for v in range(NV)]
            pz = [parts[4, v, :, cut] for v in range(NV)]
            for u in range(NV):
                a = a_ref[t, u, :, cut]
                space = convect(jx_ref, jz_ref, dx, dz, parts[2, u, :, cut], u)
                source = s_ref[t, u, :, cut] + space
                inner = a + ps_ref[:, cut] * source
                b.buffer[t, u, :, cut] = inner
                q.buffer[t, u, :, cut] = a + inner + convect(jx_ref, jz_ref, px, pz, parts[5, u, :, cut], u)
        b.put(pl.ds(t, 1))
        q.put(pl.ds(t, 1))
    for copy in copies:
        copy.wait()


def edge_terms(up_ref, down_ref, half, t, v):
    tile, slot = (t, v) if v < 4 else (6 + t // 4, t % 4)
    row = row_index(512)
    up, down = up_ref[2 * tile + half], down_ref[2 * tile + half]
    one = pltpu.roll(jnp.where(row == 2 * slot, down, up), (7 - 2 * slot) % 8, 0)
    one = jnp.where((row == 0) | (row == 7), one, 0.0)
    east_two = pltpu.roll(down, (6 - 2 * slot) % 8, 0)
    west_two = pltpu.roll(up, (8 - 2 * slot) % 8, 0)
    two = jnp.where(row >= 6, east_two, jnp.where(row < 2, west_two, 0.0))
    return one, two


def first_kernel(
    tab_ref, jx_ref, jz_ref, a_ref, bi_ref, qi_ref, e_ref, ps_ref, up_ref, down_ref, fc_ref, ff_ref, m_ref, cond_ref,
    q, b_out, bup, bdown, q4, m_out,
):
    first = lax.axis_index("inst") * 6
    step = ps_ref[...]
    q_ref, b_ref = q.buffer, b_out.buffer
    sign = jnp.where(row_index(512) == 0, 0.5, -0.5)
    step_edges = []
    for half in range(2):
        tile = 14 + half
        row = row_index(512)
        up, down = up_ref[tile], down_ref[tile]
        one = jnp.where(row == 7, pltpu.roll(down, 3, 0), pltpu.roll(up, 3, 0))
        two = jnp.where(row >= 6, pltpu.roll(down, 2, 0), pltpu.roll(up, 4, 0))
        step_edges.append((one, two))
    for t in range(6):
        for half in range(2):
            wide = pl.ds(half * 512, 512)
            here = ps_ref[:, wide]
            step_one, step_two = step_edges[half]
            edges = [edge_terms(up_ref, down_ref, half, t, v) for v in range(NV)]
            for u in range(NV):
                total = jx_ref[u, 0] * edges[0][0]
                for v in range(1, NV):
                    total += jx_ref[u, v] * edges[v][0]
                one = sign * total + (4.0 * damping_fourth) * edges[u][0]
                two = damping_fourth * edges[u][1]
                change = one - two
                if u == NV - 1:
                    change = change + e_ref[t, :, wide]
                change = here * change
                b_ref[t, u, :, wide] = bi_ref[t, u, :, wide] + change
                value = qi_ref[t, u, :, wide] + change + (step_one * one - step_two * two)
                for i in range(4):
                    q_ref[4 * half + i, t * NV + u] = value[:, i * CHUNK : (i + 1) * CHUNK]
                if u == NV - 1:
                    q4.buffer[t, :, wide] = value
        q.put((slice(None), pl.ds(t * NV, NV)))
        b_out.put(pl.ds(t, 1))
        pack_tile([b_ref[t, v] for v in range(4)], t, bup.buffer, bdown.buffer)
    pack_last(lambda t: b_ref[t, NV - 1], step, bup.buffer, bdown.buffer)
    q4.put(slice(None))
    bup.put(slice(None))
    bdown.put(slice(None))
    f_hot, f_row = fluid_hots(ff_ref)
    heat = []
    for ch in range(CH):
        h0 = h1 = jnp.zeros((ROWS, SPAN), F32)
        for t in range(6 if ch != NH else 0):
            at = (first + t) * CH + ch
            h0 += tab_ref[W0 + at] * b_ref[t, NV - 1]
            h1 += tab_ref[W1 + at] * a_ref[t, NV - 1]
        heat.append(h0 - step * h1)
    values = at_faces(jnp.stack(heat), f_hot, f_row) * fc_ref[...]
    for i in range(8):
        for k in range(4):
            q_ref[i, 30 + k] = values[:, k * CHUNK : (k + 1) * CHUNK]
    q.put((slice(None), pl.ds(30, 4)))
    before, after = metal_sides(up_ref.at[16], down_ref.at[16])
    m = metal_update(m_ref, before, after, cond_ref[...])
    for ch in range(CH):
        m_out.buffer[ch] = m[ch]
    m_out.put(slice(None))


def rotate_time(kron, x):
    high, low = split(x)
    return jnp.dot(kron, jnp.concatenate([high, low, high], axis=0), preferred_element_type=F32)


def local_step(ps_ref):
    start = pl.multiple_of(lax.axis_index("inst") * CHUNK, CHUNK)
    return ps_ref[:, pl.ds(start, CHUNK)]


def turned(get):
    return jnp.concatenate(
        [
            jnp.concatenate([get(j, t, v) for j in range(8) for t in range(6)], axis=0)
            for v in range(NV)
        ],
        axis=1,
    )


def derive_kernel(kron_ref, a_ref, ps_ref, g):
    wide = jnp.concatenate([local_step(ps_ref)] * NV, axis=1)
    x = turned(lambda j, t, v: a_ref[j, t, v])
    d = rotate_time(kron_ref[...], x)
    g.buffer[...] = (d.reshape(NT, ROWS, NV * CHUNK) * wide[None]).reshape(NT * ROWS, NV * CHUNK)
    g.put(slice(None))


def middle_kernel(
    tab_ref, jx_ref, jz_ref, b_in, s_in, ps_ref, up_ref, down_ref, a_ref, q4_ref, g_ref,
    c_out, hc,
    parts,
):
    first = lax.axis_index("inst") * 6
    c_ref = c_out.buffer
    for t in range(6):
        b_ref, s_ref = b_in.piece(t), s_in.piece(t)
        for v in range(NV):
            before, after = halo_pair(up_ref, down_ref, t, v)
            dx, dz, rest = stencil_parts(b_ref[t, v], before, after)
            parts[0, v], parts[1, v], parts[2, v] = dx, dz, rest
        for i in range(8):
            cut = pl.ds(i * CHUNK, CHUNK)
            dx = [parts[0, v, :, cut] for v in range(NV)]
            dz = [parts[1, v, :, cut] for v in range(NV)]
            for u in range(NV):
                space = convect(jx_ref, jz_ref, dx, dz, parts[2, u, :, cut], u)
                c_ref[t, u, :, cut] = b_ref[t, u, :, cut] + ps_ref[:, cut] * (s_ref[t, u, :, cut] + space)
        c_out.put(pl.ds(t, 1))
    step = ps_ref[...]
    for ch in range(CH):
        h0 = h2 = h3 = jnp.zeros((ROWS, SPAN), F32)
        for t in range(6 if ch != NH else 0):
            at = (first + t) * CH + ch
            h0 += tab_ref[W0 + at] * c_ref[t, NV - 1]
            h2 += tab_ref[W1 + at] * q4_ref[t]
            h3 += tab_ref[W2 + at] * a_ref[t, NV - 1]
        hc.buffer[ch] = h0 + step * (step * h3 - h2)
    hc.put(slice(None))


def metal_update(m, before, after, cond):
    row = row_index(MSPAN)
    out = []
    for ch in range(CH):
        a = m[ch]
        east = pltpu.roll(jnp.where(row == 0, after[ch], a), 7, 0)
        west = pltpu.roll(jnp.where(row == 7, before[ch], a), 1, 0)
        north, south = span_sides(a)
        laplace = east + west + north + south - 4.0 * a
        h = ch % NH
        turn = -heat_capacity * h * m[ch + NH] if ch < NH else heat_capacity * h * m[ch - NH]
        out.append(a + metal_step * (cond * laplace - sigma_metal * a - turn))
    return out


def metal_edges(m, up_ref, down_ref):
    up_ref[...] = jnp.concatenate([m[ch][7:8] for ch in range(CH)], axis=0)
    down_ref[...] = jnp.concatenate([m[ch][0:1] for ch in range(CH)], axis=0)


def metal_sides(up_ref, down_ref):
    before = [jnp.broadcast_to(up_ref[ch : ch + 1], (ROWS, MSPAN)) for ch in range(CH)]
    after = [jnp.broadcast_to(down_ref[ch : ch + 1], (ROWS, MSPAN)) for ch in range(CH)]
    return before, after


def heat_sum(get):
    tiles = []
    for k in range(4):
        total = get(0, k)
        for j in range(1, 8):
            total += get(j, k)
        tiles.append(total)
    return jnp.concatenate(tiles, axis=1)


def second_kernel(
    tab_ref, q_ref, g_ref, kron_ref, ps_ref, m_ref, fc_ref, ff_ref, mf_ref, hc_ref,
    v, m_out, mup, mdown, e,
):
    first = lax.axis_index("inst") * 6
    v_ref = v.buffer
    near = local_step(ps_ref)
    x = turned(lambda j, t, u: q_ref[j, t * NV + u]) - g_ref[...]

    def send(half):
        d = rotate_time(kron_ref[pl.ds(half * 192, 192), :], x)
        for j in range(4):
            for t in range(6):
                at = (j * 6 + t) * ROWS
                for u in range(NV):
                    v_ref[half * 4 + j, t * NV + u] = -near * d[at : at + ROWS, u * CHUNK : (u + 1) * CHUNK]
        v.put((pl.ds(half * 4, 4), pl.ds(0, 30)))

    step = ps_ref[...]
    coeff = fc_ref[...]
    m_hot, m_row = metal_hots(mf_ref)
    source = onto_cells(heat_sum(lambda j, k: q_ref[j, 30 + k]), m_hot, m_row)
    m = [m_ref[ch] + metal_step * source[ch] for ch in range(CH)]
    send(0)
    values = at_faces(jnp.stack(m), m_hot, m_row) * coeff
    f_hot, f_row = fluid_hots(ff_ref)
    cells = onto_cells(values, f_hot, f_row)
    send(1)
    for ch in range(CH):
        m_out.buffer[ch] = m[ch]
    metal_edges(m, mup.buffer, mdown.buffer)
    for result in (m_out, mup, mdown):
        result.put(slice(None))
    for t in range(6):
        e.buffer[t] = step * combine(tab_ref, SYNTH, first + t, cells)
    e.put(slice(None))
    heat = []
    for ch in range(CH):
        total = hc_ref[ch]
        for t in range(6 if ch != NH else 0):
            total += tab_ref[W0 + (first + t) * CH + ch] * e.buffer[t]
        heat.append(total)
    values = at_faces(jnp.stack(heat), f_hot, f_row) * coeff
    for i in range(8):
        for k in range(4):
            v_ref[i, 30 + k] = values[:, k * CHUNK : (k + 1) * CHUNK]
    v.put((slice(None), pl.ds(30, 4)))


def last_kernel(v, c, e, m_in, mup_ref, mdown_ref, cond_ref, mf_ref, out, m_out):
    for t in range(6):
        v_ref, c_ref, e_ref = v.piece(t), c.piece(t), e.whole()
        for i in range(8):
            cut = pl.ds(i * CHUNK, CHUNK)
            for u in range(NV):
                total = c_ref[t, u, :, cut] + v_ref[i, t * NV + u]
                if u == NV - 1:
                    total = total + e_ref[t, :, cut]
                out.buffer[t, u, :, cut] = total
        out.put(pl.ds(t, 1))
    m_hot, m_row = metal_hots(mf_ref)
    source = onto_cells(heat_sum(lambda j, k: v.buffer[j, 30 + k]), m_hot, m_row)
    before, after = metal_sides(mup_ref, mdown_ref)
    m = metal_update(m_in.whole(), before, after, cond_ref[...])
    for ch in range(CH):
        m_out.buffer[ch] = m[ch] + metal_step * source[ch]
    m_out.put(slice(None))


def exchange(up, down):
    n = lax.axis_size("space")
    forward = [(i, (i + 1) % n) for i in range(n)]
    back = [(j, i) for i, j in forward]
    return lax.ppermute(up, "space", forward), lax.ppermute(down, "space", back)


def turn(x):
    return lax.all_to_all(x, "inst", 0, 0, tiled=True)


SIX = by_piece(6)
EDGES = (17, ROWS, 512)
FLUID = (6, NV, ROWS, SPAN)
METAL = (CH, ROWS, MSPAN)
ONE = (6, ROWS, SPAN)
BLOCKS = (8, 34, ROWS, CHUNK)


LONG = 1 << 36


def plain(*arrays):
    return [(array, "vmem") for array in arrays]


def late(*arrays):
    return [(array, WHOLE) for array in arrays]


def held(*arrays):
    return [(array, "held") for array in arrays]


def local(a0, source, ps, jx, jz, metal, cond, coeff, ff, mf):
    kron = jnp.asarray(KRON)
    tab = jnp.asarray(FLAT)
    coeff, ff, mf = (x.reshape(1, NF) for x in (coeff, ff, mf))
    metal = metal.reshape(METAL)
    ends = tuple(
        (pl.ds(t, 1), slice(None), pl.ds(row, 2)) for t in range(6) for row in (0, ROWS - 2)
    )
    up, down = call(prepare_kernel, [(a0, ends)] + late(ps, metal), [(EDGES, 7), (EDGES, 7)])
    up, down = exchange(up, down)
    scalars = [(tab, "smem"), (jx, "smem"), (jz, "smem")]
    last_variable = (a0, ((slice(None), pl.ds(NV - 1, 1)),))
    b, q, blocks = call(
        inner_kernel,
        scalars[1:] + plain(a0, source, ps),
        [(FLUID, 6), (FLUID, 6), ((8, 6, NV, ROWS, CHUNK), -1)],
        scratch=[pltpu.VMEM((6, NV, ROWS, SPAN), F32), pltpu.SemaphoreType.DMA((8,))],
    )
    (e0,) = call(
        energy_kernel,
        scalars[:1] + plain(metal, coeff, ff, mf) + [(blocks, "idle")],
        [(ONE, 0)],
        flops=LONG,
    )
    a_turned = turn(blocks)
    q, b, bup, bdown, q4, metal = call(
        first_kernel,
        scalars + [last_variable] + plain(b, q, e0, ps, up, down, coeff, ff, metal, cond),
        [(BLOCKS, 7), (FLUID, 6), (EDGES, 1), (EDGES, 1), (ONE, 1), (METAL, 1)],
    )
    q_turned = turn(q)
    bup, bdown = exchange(bup, bdown)
    (g,) = call(derive_kernel, plain(kron, a_turned, ps), [((NT * ROWS, NV * CHUNK), 0)])
    c, hc = call(
        middle_kernel,
        scalars + [(b, SIX), (source, SIX)] + late(ps) + plain(bup, bdown) + [last_variable] + late(q4)
        + plain(g),
        [(FLUID, 0), ((CH, ROWS, SPAN), 0)],
        scratch=[pltpu.VMEM((3, NV, ROWS, SPAN), F32)],
        flops=LONG,
    )
    v, metal, mup, mdown, e1 = call(
        second_kernel,
        scalars[:1] + plain(q_turned, g, kron, ps, metal, coeff, ff, mf, hc),
        [(BLOCKS, 3), (METAL, 1), ((CH, MSPAN), 1), ((CH, MSPAN), 1), (ONE, 1)],
    )
    v = turn(v)
    mup, mdown = exchange(mup, mdown)
    out, metal = call(
        last_kernel, held(v, c, e1, metal) + plain(mup, mdown, cond, mf), [(FLUID, 6), (METAL, 1)]
    )
    return out, metal.reshape(2, NH, ROWS, MSPAN)


def solution(mesh):
    return jax.shard_map(
        local,
        mesh=mesh,
        in_specs=(
            P("inst", None, "space", None),
            P("inst", None, "space", None),
            P("space", None),
            P(),
            P(),
            P(None, None, "space", None),
            P("space", None),
            P("space"),
            P("space"),
            P("space"),
        ),
        out_specs=(P("inst", None, "space", None), P(None, None, "space", None)),
        check_vma=False,
    )
```

```python
import math

import jax
import jax.numpy as jnp
import ml_dtypes
import numpy as np
from jax import lax
from jax.experimental import pallas as pl
from jax.experimental.pallas import tpu as pltpu
from jax.sharding import PartitionSpec as P

NT, NV, NH = 48, 5, 4
ROWS, SPAN, MSPAN, NF = 8, 1024, 512, 512
CHUNK = 128
CH = 2 * NH
F32, BF16 = jnp.float32, jnp.bfloat16

damping_fourth = 1.0 / 32.0
viscous_coef = 0.1
sigma_fluid = 0.5
metal_step = 0.2
sigma_metal = 0.5
heat_capacity = 0.5
flux_scale = 4.0


def tables():
    t = np.arange(NT)
    offset = t[:, None] - t[None, :]
    angle = np.where(offset == 0, 0.5, math.pi * offset / NT)
    spectral = np.where(
        offset == 0, 0.0, 0.5 * (1.0 - 2.0 * (offset % 2)) * np.cos(angle) / np.sin(angle)
    )
    phase = 2.0 * math.pi * ((np.arange(NH)[:, None] * t[None, :]) % NT) / NT
    synth = np.concatenate([np.cos(phase), -np.sin(phase)])
    w0 = synth * (flux_scale / NT)
    w1 = w0 @ spectral
    w2 = w1 @ spectral
    high = spectral.astype(np.float32).astype(ml_dtypes.bfloat16)
    low = (spectral - high.astype(np.float64)).astype(np.float32).astype(ml_dtypes.bfloat16)
    eye = np.eye(ROWS, dtype=np.float32)
    kron_high = np.kron(high.astype(np.float32), eye)
    kron_low = np.kron(low.astype(np.float32), eye)
    kron = np.concatenate([kron_high, kron_high, kron_low], axis=1).astype(ml_dtypes.bfloat16)
    flat = np.concatenate([m.T.reshape(-1) for m in (synth, w0, w1, w2)]).astype(np.float32)
    return kron, flat


KRON, FLAT = tables()
SYNTH, W0, W1, W2 = (i * NT * CH for i in range(4))


class Loaded:
    def __init__(self, source, buffer, sems, cut):
        self.buffer, self.copies = buffer, []
        for i, index in enumerate(cut):
            self.copies.append(pltpu.make_async_copy(source.at[index], buffer.at[index], sems.at[i]))
        self.waiting = set(range(len(cut)))

    def start(self, i):
        self.copies[i].start()

    def piece(self, i):
        if i in self.waiting:
            self.waiting.remove(i)
            self.copies[i].wait()
        return self.buffer

    def whole(self):
        for i in range(len(self.copies)):
            self.piece(i)
        return self.buffer

    def __getitem__(self, index):
        return self.whole()[index]


class Held:
    def __init__(self, ref):
        self.buffer = ref

    def piece(self, i):
        return self.buffer

    def whole(self):
        return self.buffer

    def put(self, index):
        pass


class Stored:
    def __init__(self, target, buffer, sems):
        self.target, self.buffer, self.sems, self.copies = target, buffer, sems, []

    def put(self, index):
        copy = pltpu.make_async_copy(
            self.buffer.at[index], self.target.at[index], self.sems.at[len(self.copies)]
        )
        copy.start()
        self.copies.append(copy)

    def finish(self):
        for copy in self.copies:
            copy.wait()


class Into:
    def __init__(self, result, cut):
        self.result, self.cut = result, cut

    def __len__(self):
        return len(self.cut)


WHOLE = (slice(None),)


def by_piece(n):
    return tuple(pl.ds(i, 1) for i in range(n))


def call(body, operands, results, scratch=(), flops=1 << 20, moved=1 << 20):
    types = [r[2] if len(r) > 2 else F32 for r in results]
    results = [r[:2] for r in results]
    space = {"idle": pltpu.HBM, "smem": pltpu.SMEM, "vmem": pltpu.VMEM, "held": pltpu.VMEM}
    modes = [mode for _, mode in operands]
    here = [isinstance(mode, str) for mode in modes]
    in_specs = [
        pl.BlockSpec(memory_space=space[m] if h else pltpu.HBM) for m, h in zip(modes, here)
    ]
    out_specs = [pl.BlockSpec(memory_space=pltpu.HBM if n else pltpu.VMEM) for _, n in results]
    buffers = []
    kinds = {mode.result: array.dtype for array, mode in operands if isinstance(mode, Into)}
    for array, mode in operands:
        if isinstance(mode, tuple):
            buffers.append(pltpu.VMEM(array.shape, array.dtype))
        if not isinstance(mode, str):
            buffers.append(pltpu.SemaphoreType.DMA((len(mode),)))
    for dims, n in results:
        if n > 0:
            buffers += [pltpu.VMEM(dims, F32), pltpu.SemaphoreType.DMA((n,))]

    def kernel(*refs):
        ins, refs = refs[: len(modes)], refs[len(modes) :]
        outs, refs = refs[: len(results)], list(refs[len(results) :])
        args, loads = [], []
        for ref, mode, h in zip(ins, modes, here):
            if h:
                args.append(Held(ref) if mode == "held" else ref)
            else:
                into = isinstance(mode, Into)
                buffer = outs[mode.result] if into else refs.pop(0)
                args.append(Loaded(ref, buffer, refs.pop(0), mode.cut if into else mode))
                loads.append(args[-1])
        for i in range(max([len(x.copies) for x in loads], default=0)):
            for x in loads:
                if i < len(x.copies):
                    x.start(i)
        stores = []
        for ref, (_, n) in zip(outs, results):
            if n > 0:
                args.append(Stored(ref, refs.pop(0), refs.pop(0)))
                stores.append(args[-1])
            else:
                args.append(ref if n else Held(ref))
        body(*args, *refs)
        for x in loads:
            x.whole()
        for x in stores:
            x.finish()

    return pl.pallas_call(
        kernel,
        out_shape=[pltpu.HBM(dims, F32) if n else jax.ShapeDtypeStruct(dims, kinds.get(k, types[k])) for k, (dims, n) in enumerate(results)],
        in_specs=in_specs,
        out_specs=out_specs,
        scratch_shapes=buffers + list(scratch),
        compiler_params=pltpu.CompilerParams(vmem_limit_bytes=24 << 20),
        cost_estimate=pl.CostEstimate(flops=flops, bytes_accessed=moved, transcendentals=0),
    )(
        *[
            a if h and m != "idle" else pltpu.with_memory_space_constraint(a, pltpu.HBM)
            for (a, m), h in zip(operands, here)
        ]
    )


def shape(*dims):
    return jax.ShapeDtypeStruct(dims, F32)


def row_index(n=SPAN):
    return lax.broadcasted_iota(jnp.int32, (ROWS, n), 0)


def split(x):
    high = x.astype(BF16)
    return high, (x - high.astype(F32)).astype(BF16)


def one_hot(index, n):
    cell = lax.broadcasted_iota(jnp.int32, (n, NF), 0)
    return jnp.where(cell == index, 1.0, 0.0).astype(BF16)


def at_faces(field, span_hot, row_hot):
    n = field.shape[-1]
    both = jnp.concatenate(split(field.reshape(CH * ROWS, n)), axis=0)
    picked = jnp.dot(both, span_hot, preferred_element_type=F32)
    picked = (picked[: CH * ROWS] + picked[CH * ROWS :]).reshape(CH, ROWS, NF)
    return jnp.sum(picked * row_hot[None], axis=1)


def onto_cells(values, span_hot, row_hot):
    spread = (values[:, None, :] * row_hot[None]).reshape(CH * ROWS, NF)
    both = jnp.concatenate(split(spread), axis=0)
    out = lax.dot_general(both, span_hot, (((1,), (1,)), ((), ())), preferred_element_type=F32)
    return (out[: CH * ROWS] + out[CH * ROWS :]).reshape(CH, ROWS, span_hot.shape[0])


def rows_of(faces_ref, bits):
    return jnp.where(row_index(NF) == (faces_ref[...] >> bits), 1.0, 0.0)


def fluid_hots(ff_ref):
    cell = ff_ref[...]
    span = one_hot(cell & (SPAN - 1), SPAN)
    rows = jnp.where(row_index(NF) == (cell >> 10), 1.0, 0.0)
    return span, rows


def metal_hots(mf_ref):
    cell = mf_ref[...]
    span = one_hot(cell & (MSPAN - 1), MSPAN)
    rows = jnp.where(row_index(NF) == (cell >> 9), 1.0, 0.0)
    return span, rows


def span_sides(a):
    n = a.shape[-1]
    lane = lax.broadcasted_iota(jnp.int32, a.shape, a.ndim - 1)
    north = jnp.where(lane == n - 1, 0.0, pltpu.roll(a, n - 1, a.ndim - 1))
    south = jnp.where(lane == 0, 0.0, pltpu.roll(a, 1, a.ndim - 1))
    return north, south


def stencil_parts(a, before, after):
    row = row_index(a.shape[-1])
    east_one = pltpu.roll(jnp.where(row == 0, after, a), 7, 0)
    east_two = pltpu.roll(jnp.where(row < 2, after, a), 6, 0)
    west_one = pltpu.roll(jnp.where(row == 7, before, a), 1, 0)
    west_two = pltpu.roll(jnp.where(row >= 6, before, a), 2, 0)
    north, south = span_sides(a)
    rest = (
        (4.0 * damping_fourth) * (east_one + west_one)
        - damping_fourth * (east_two + west_two)
        + viscous_coef * (north + south)
        - (6.0 * damping_fourth + 2.0 * viscous_coef + sigma_fluid) * a
    )
    return east_one - west_one, north - south, rest


def edge_tile(ref, tile):
    return jnp.concatenate([ref[2 * tile], ref[2 * tile + 1]], axis=1)


def halo_pair(up_ref, down_ref, t, v):
    tile, slot = (t, v) if v < 4 else (6 + t // 4, t % 4)
    before = pltpu.roll(edge_tile(up_ref, tile), (6 - 2 * slot) % 8, 0)
    after = pltpu.roll(edge_tile(down_ref, tile), (8 - 2 * slot) % 8, 0)
    return before, after


def pack_tile(blocks, tile, up_ref, down_ref):
    row = row_index()
    up = down = None
    for slot, a in enumerate(blocks):
        u = pltpu.roll(a, (2 * slot + 2) % 8, 0) if (2 * slot + 2) % 8 else a
        d = pltpu.roll(a, 2 * slot, 0) if slot else a
        mine = (row >> 1) == slot
        up = u if up is None else jnp.where(mine, u, up)
        down = d if down is None else jnp.where(mine, d, down)
    for half in range(2):
        cut = slice(half * 512, half * 512 + 512)
        up_ref[2 * tile + half] = up[:, cut]
        down_ref[2 * tile + half] = down[:, cut]


def pack_last(get, extra, up_ref, down_ref):
    pack_tile([get(t) for t in range(4)], 6, up_ref, down_ref)
    pack_tile([get(4), get(5), extra, extra], 7, up_ref, down_ref)


def prepare_kernel(a, ps, m_in, up, down, a_copy, ps_copy):
    for t in range(6):
        ref = a.piece(t)
        pack_tile([ref[t, v] for v in range(4)], t, up.buffer, down.buffer)
        for x in (up, down):
            x.put(pl.ds(2 * t, 2))
    pack_last(lambda t: a.buffer[t, NV - 1], ps.whole()[...], up.buffer, down.buffer)
    metal_edges(m_in.whole(), up.buffer.at[16], down.buffer.at[16])
    for x in (up, down):
        x.put(pl.ds(12, 5))


def energy_kernel(tab_ref, m_ref, fc_ref, ff_ref, mf_ref, after, e):
    first = lax.axis_index("inst") * 6
    m_hot, m_row = metal_hots(mf_ref)
    f_hot, f_row = fluid_hots(ff_ref)
    values = at_faces(m_ref[...], m_hot, m_row) * fc_ref[...]
    cells = onto_cells(values, f_hot, f_row)
    for t in range(6):
        e.buffer[t] = combine(tab_ref, SYNTH, first + t, cells)
        e.put(pl.ds(t, 1))


def combine(tab_ref, base, t, fields):
    total = tab_ref[base + t * CH] * fields[0]
    for ch in range(1, CH):
        if ch != NH:
            total += tab_ref[base + t * CH + ch] * fields[ch]
    return total


def convect(jx_ref, jz_ref, dx, dz, rest, u):
    out = rest
    for v in range(NV):
        out = out - (0.5 * jx_ref[u, v]) * dx[v] - (0.5 * jz_ref[u, v]) * dz[v]
    return out


def inner_steps(instances, jx_ref, jz_ref, a_ref, s_ref, ps_ref, b, q, parts):
    step = ps_ref[...]
    for at, t in enumerate(instances):
        for v in range(NV):
            a = a_ref[t, v]
            dx, dz, rest = stencil_parts(a, 0.0, 0.0)
            parts[0, v], parts[1, v], parts[2, v] = dx, dz, rest
            dx, dz, rest = stencil_parts(step * a, 0.0, 0.0)
            parts[3, v], parts[4, v], parts[5, v] = dx, dz, rest
        for i in range(8):
            cut = pl.ds(i * CHUNK, CHUNK)
            dx = [parts[0, v, :, cut] for v in range(NV)]
            dz = [parts[1, v, :, cut] for v in range(NV)]
            px = [parts[3, v, :, cut] for v in range(NV)]
            pz = [parts[4, v, :, cut] for v in range(NV)]
            for u in range(NV):
                a = a_ref[t, u, :, cut]
                space = convect(jx_ref, jz_ref, dx, dz, parts[2, u, :, cut], u)
                source = s_ref[t, u, :, cut] + space
                inner = a + ps_ref[:, cut] * source
                b.buffer[at, u, :, cut] = inner
                q.buffer[at, u, :, cut] = a + inner + convect(jx_ref, jz_ref, px, pz, parts[5, u, :, cut], u)
        b.put(pl.ds(at, 1))
        q.put(pl.ds(at, 1))


EARLY = 4


def early_kernel(jx_ref, jz_ref, a_ref, s_ref, ps_ref, b, q, blocks, parts, sems):
    copies = [
        pltpu.make_async_copy(
            a_ref.at[:, :, :, pl.ds(i * CHUNK, CHUNK)], blocks.at[i], sems.at[i]
        )
        for i in range(8)
    ]
    for copy in copies:
        copy.start()
    inner_steps(range(EARLY), jx_ref, jz_ref, a_ref, s_ref, ps_ref, b, q, parts)
    for copy in copies:
        copy.wait()


def late_kernel(jx_ref, jz_ref, a_ref, s_ref, ps_ref, after, b, q, parts):
    inner_steps(range(EARLY, 6), jx_ref, jz_ref, a_ref, s_ref, ps_ref, b, q, parts)


def edge_terms(up_ref, down_ref, half, t, v):
    tile, slot = (t, v) if v < 4 else (6 + t // 4, t % 4)
    row = row_index(512)
    up, down = up_ref[2 * tile + half], down_ref[2 * tile + half]
    one = pltpu.roll(jnp.where(row == 2 * slot, down, up), (7 - 2 * slot) % 8, 0)
    one = jnp.where((row == 0) | (row == 7), one, 0.0)
    east_two = pltpu.roll(down, (6 - 2 * slot) % 8, 0)
    west_two = pltpu.roll(up, (8 - 2 * slot) % 8, 0)
    two = jnp.where(row >= 6, east_two, jnp.where(row < 2, west_two, 0.0))
    return one, two


def first_kernel(
    tab_ref, jx_ref, jz_ref, a_ref, b0_ref, q0_ref, b1_ref, q1_ref, e_ref, ps_ref, up_ref, down_ref, fc_ref, ff_ref, m_ref, cond_ref,
    q, b_out, bup, bdown, q4, m_out,
):
    first = lax.axis_index("inst") * 6
    step = ps_ref[...]
    q_ref, b_ref = q.buffer, b_out.buffer
    sign = jnp.where(row_index(512) == 0, 0.5, -0.5)
    step_edges = []
    for half in range(2):
        tile = 14 + half
        row = row_index(512)
        up, down = up_ref[tile], down_ref[tile]
        one = jnp.where(row == 7, pltpu.roll(down, 3, 0), pltpu.roll(up, 3, 0))
        two = jnp.where(row >= 6, pltpu.roll(down, 2, 0), pltpu.roll(up, 4, 0))
        step_edges.append((one, two))
    for t in range(6):
        for half in range(2):
            wide = pl.ds(half * 512, 512)
            here = ps_ref[:, wide]
            step_one, step_two = step_edges[half]
            edges = [edge_terms(up_ref, down_ref, half, t, v) for v in range(NV)]
            bi_ref, qi_ref = (b0_ref, q0_ref) if t < EARLY else (b1_ref, q1_ref)
            ti = t if t < EARLY else t - EARLY
            for u in range(NV):
                total = jx_ref[u, 0] * edges[0][0]
                for v in range(1, NV):
                    total += jx_ref[u, v] * edges[v][0]
                one = sign * total + (4.0 * damping_fourth) * edges[u][0]
                two = damping_fourth * edges[u][1]
                change = one - two
                if u == NV - 1:
                    change = change + e_ref[t, :, wide]
                change = here * change
                b_ref[t, u, :, wide] = bi_ref[ti, u, :, wide] + change
                value = qi_ref[ti, u, :, wide] + change + (step_one * one - step_two * two)
                for i in range(4):
                    q_ref[4 * half + i, t * NV + u] = value[:, i * CHUNK : (i + 1) * CHUNK]
                if u == NV - 1:
                    q4.buffer[t, :, wide] = value
        q.put((slice(None), pl.ds(t * NV, NV)))
        b_out.put(pl.ds(t, 1))
        pack_tile([b_ref[t, v] for v in range(4)], t, bup.buffer, bdown.buffer)
    pack_last(lambda t: b_ref[t, NV - 1], step, bup.buffer, bdown.buffer)
    q4.put(slice(None))
    bup.put(slice(None))
    bdown.put(slice(None))
    f_hot, f_row = fluid_hots(ff_ref)
    heat = []
    for ch in range(CH):
        h0 = h1 = jnp.zeros((ROWS, SPAN), F32)
        for t in range(6 if ch != NH else 0):
            at = (first + t) * CH + ch
            h0 += tab_ref[W0 + at] * b_ref[t, NV - 1]
            h1 += tab_ref[W1 + at] * a_ref[t, NV - 1]
        heat.append(h0 - step * h1)
    values = at_faces(jnp.stack(heat), f_hot, f_row) * fc_ref[...]
    for i in range(8):
        for k in range(4):
            q_ref[i, 30 + k] = values[:, k * CHUNK : (k + 1) * CHUNK]
    q.put((slice(None), pl.ds(30, 4)))
    before, after = metal_sides(up_ref.at[16], down_ref.at[16])
    m = metal_update(m_ref, before, after, cond_ref[...])
    for ch in range(CH):
        m_out.buffer[ch] = m[ch]
    m_out.put(slice(None))


def rotate_time(kron, x):
    high, low = split(x)
    return jnp.dot(kron, jnp.concatenate([high, low, high], axis=0), preferred_element_type=F32)


def local_step(ps_ref):
    start = pl.multiple_of(lax.axis_index("inst") * CHUNK, CHUNK)
    return ps_ref[:, pl.ds(start, CHUNK)]


def turned(get):
    return jnp.concatenate(
        [
            jnp.concatenate([get(j, t, v) for j in range(8) for t in range(6)], axis=0)
            for v in range(NV)
        ],
        axis=1,
    )


def derive_kernel(kron_ref, a_ref, ps_ref, g):
    wide = jnp.concatenate([local_step(ps_ref)] * NV, axis=1)
    x = turned(lambda j, t, v: a_ref[j, t, v])
    d = rotate_time(kron_ref[...], x)
    g.buffer[...] = (d.reshape(NT, ROWS, NV * CHUNK) * wide[None]).reshape(NT * ROWS, NV * CHUNK)
    g.put(slice(None))


def middle_kernel(
    tab_ref, jx_ref, jz_ref, b_in, s_in, ps_ref, up_ref, down_ref, a_ref, q4_ref, ff_ref, mf_ref, g_ref,
    c_out, hc, f_hot, m_hot,
    parts,
):
    first = lax.axis_index("inst") * 6
    c_ref = c_out.buffer
    for t in range(6):
        b_ref, s_ref = b_in.piece(t), s_in.piece(t)
        for v in range(NV):
            before, after = halo_pair(up_ref, down_ref, t, v)
            dx, dz, rest = stencil_parts(b_ref[t, v], before, after)
            parts[0, v], parts[1, v], parts[2, v] = dx, dz, rest
        for i in range(8):
            cut = pl.ds(i * CHUNK, CHUNK)
            dx = [parts[0, v, :, cut] for v in range(NV)]
            dz = [parts[1, v, :, cut] for v in range(NV)]
            for u in range(NV):
                space = convect(jx_ref, jz_ref, dx, dz, parts[2, u, :, cut], u)
                c_ref[t, u, :, cut] = b_ref[t, u, :, cut] + ps_ref[:, cut] * (s_ref[t, u, :, cut] + space)
        c_out.put(pl.ds(t, 1))
    step = ps_ref[...]
    for ch in range(CH):
        h0 = h2 = h3 = jnp.zeros((ROWS, SPAN), F32)
        for t in range(6 if ch != NH else 0):
            at = (first + t) * CH + ch
            h0 += tab_ref[W0 + at] * c_ref[t, NV - 1]
            h2 += tab_ref[W1 + at] * q4_ref[t]
            h3 += tab_ref[W2 + at] * a_ref[t, NV - 1]
        hc.buffer[ch] = h0 + step * (step * h3 - h2)
    hc.put(slice(None))
    f_hot.buffer[...] = fluid_hots(ff_ref)[0]
    m_hot.buffer[...] = metal_hots(mf_ref)[0]


def metal_update(m, before, after, cond):
    row = row_index(MSPAN)
    out = []
    for ch in range(CH):
        a = m[ch]
        east = pltpu.roll(jnp.where(row == 0, after[ch], a), 7, 0)
        west = pltpu.roll(jnp.where(row == 7, before[ch], a), 1, 0)
        north, south = span_sides(a)
        laplace = east + west + north + south - 4.0 * a
        h = ch % NH
        turn = -heat_capacity * h * m[ch + NH] if ch < NH else heat_capacity * h * m[ch - NH]
        out.append(a + metal_step * (cond * laplace - sigma_metal * a - turn))
    return out


def metal_edges(m, up_ref, down_ref):
    up_ref[...] = jnp.concatenate([m[ch][7:8] for ch in range(CH)], axis=0)
    down_ref[...] = jnp.concatenate([m[ch][0:1] for ch in range(CH)], axis=0)


def metal_sides(up_ref, down_ref):
    before = [jnp.broadcast_to(up_ref[ch : ch + 1], (ROWS, MSPAN)) for ch in range(CH)]
    after = [jnp.broadcast_to(down_ref[ch : ch + 1], (ROWS, MSPAN)) for ch in range(CH)]
    return before, after


def heat_sum(get):
    tiles = []
    for k in range(4):
        total = get(0, k)
        for j in range(1, 8):
            total += get(j, k)
        tiles.append(total)
    return jnp.concatenate(tiles, axis=1)


def second_kernel(
    tab_ref, q_ref, g_ref, kron_ref, ps_ref, m_ref, fc_ref, ff_ref, mf_ref, hc_ref, f_hot_ref, m_hot_ref,
    v, m_out, mup, mdown, e,
):
    first = lax.axis_index("inst") * 6
    v_ref = v.buffer
    near = local_step(ps_ref)
    x = turned(lambda j, t, u: q_ref[j, t * NV + u]) - g_ref[...]

    d = rotate_time(kron_ref[...], x)
    for half in range(2):
        for j in range(4 * half, 4 * half + 4):
            for t in range(6):
                at = (j * 6 + t) * ROWS
                for u in range(NV):
                    v_ref[j, t * NV + u] = -near * d[at : at + ROWS, u * CHUNK : (u + 1) * CHUNK]
        v.put((pl.ds(half * 4, 4), pl.ds(0, 30)))
    step = ps_ref[...]
    coeff = fc_ref[...]
    m_hot, m_row = m_hot_ref[...], rows_of(mf_ref, 9)
    source = onto_cells(heat_sum(lambda j, k: q_ref[j, 30 + k]), m_hot, m_row)
    m = [m_ref[ch] + metal_step * source[ch] for ch in range(CH)]
    values = at_faces(jnp.stack(m), m_hot, m_row) * coeff
    f_hot, f_row = f_hot_ref[...], rows_of(ff_ref, 10)
    cells = onto_cells(values, f_hot, f_row)
    for ch in range(CH):
        m_out.buffer[ch] = m[ch]
    metal_edges(m, mup.buffer, mdown.buffer)
    for result in (m_out, mup, mdown):
        result.put(slice(None))
    for t in range(6):
        e.buffer[t] = step * combine(tab_ref, SYNTH, first + t, cells)
    e.put(slice(None))
    heat = []
    for ch in range(CH):
        total = hc_ref[ch]
        for t in range(6 if ch != NH else 0):
            total += tab_ref[W0 + (first + t) * CH + ch] * e.buffer[t]
        heat.append(total)
    values = at_faces(jnp.stack(heat), f_hot, f_row) * coeff
    for i in range(8):
        for k in range(4):
            v_ref[i, 30 + k] = values[:, k * CHUNK : (k + 1) * CHUNK]
    v.put((slice(None), pl.ds(30, 4)))


def last_kernel(v, c, e, m_in, mup_ref, mdown_ref, cond_ref, mf_ref, out, m_out):
    for t in range(6):
        v_ref, c_ref, e_ref = v.piece(t), c.piece(t), e.whole()
        for i in range(8):
            cut = pl.ds(i * CHUNK, CHUNK)
            for u in range(NV):
                total = c_ref[t, u, :, cut] + v_ref[i, t * NV + u]
                if u == NV - 1:
                    total = total + e_ref[t, :, cut]
                out.buffer[t, u, :, cut] = total
        out.put(pl.ds(t, 1))
    m_hot, m_row = metal_hots(mf_ref)
    source = onto_cells(heat_sum(lambda j, k: v.buffer[j, 30 + k]), m_hot, m_row)
    before, after = metal_sides(mup_ref, mdown_ref)
    m = metal_update(m_in.whole(), before, after, cond_ref[...])
    for ch in range(CH):
        m_out.buffer[ch] = m[ch] + metal_step * source[ch]
    m_out.put(slice(None))


def exchange(up, down):
    n = lax.axis_size("space")
    forward = [(i, (i + 1) % n) for i in range(n)]
    back = [(j, i) for i, j in forward]
    return lax.ppermute(up, "space", forward), lax.ppermute(down, "space", back)


def turn(x):
    return lax.all_to_all(x, "inst", 0, 0, tiled=True)


SIX = by_piece(6)
EDGES = (17, ROWS, 512)
FLUID = (6, NV, ROWS, SPAN)
METAL = (CH, ROWS, MSPAN)
ONE = (6, ROWS, SPAN)
BLOCKS = (8, 34, ROWS, CHUNK)


LONG = 1 << 36


def plain(*arrays):
    return [(array, "vmem") for array in arrays]


def late(*arrays):
    return [(array, WHOLE) for array in arrays]


def held(*arrays):
    return [(array, "held") for array in arrays]


def local(a0, source, ps, jx, jz, metal, cond, coeff, ff, mf):
    kron = jnp.asarray(KRON)
    tab = jnp.asarray(FLAT)
    coeff, ff, mf = (x.reshape(1, NF) for x in (coeff, ff, mf))
    metal = metal.reshape(METAL)
    up, down, a_here, ps_here = call(
        prepare_kernel,
        [(a0, Into(2, SIX)), (ps, Into(3, WHOLE))] + late(metal),
        [(EDGES, 7), (EDGES, 7), (FLUID, 0), ((ROWS, SPAN), 0)],
    )
    up, down = exchange(up, down)
    scalars = [(tab, "smem"), (jx, "smem"), (jz, "smem")]
    last_variable = (a0, ((slice(None), pl.ds(NV - 1, 1)),))
    parts = pltpu.VMEM((6, NV, ROWS, SPAN), F32)
    b, q, blocks = call(
        early_kernel,
        scalars[1:] + plain(a_here, source, ps_here),
        [((EARLY,) + FLUID[1:], EARLY), ((EARLY,) + FLUID[1:], EARLY), ((8, 6, NV, ROWS, CHUNK), -1)],
        scratch=[parts, pltpu.SemaphoreType.DMA((8,))],
    )
    (e0,) = call(
        energy_kernel,
        scalars[:1] + plain(metal, coeff, ff, mf) + [(blocks, "idle")],
        [(ONE, 0)],
        flops=LONG,
    )
    b_late, q_late = call(
        late_kernel,
        scalars[1:] + plain(a0, source, ps) + [(blocks, "idle")],
        [((6 - EARLY,) + FLUID[1:], 0)] * 2,
        scratch=[parts],
        flops=LONG,
    )
    a_turned = turn(blocks)
    q, b, bup, bdown, q4, metal = call(
        first_kernel,
        scalars + [last_variable] + plain(b, q, b_late, q_late, e0, ps, up, down, coeff, ff, metal, cond),
        [(BLOCKS, 7), (FLUID, 6), (EDGES, 1), (EDGES, 1), (ONE, 1), (METAL, 1)],
    )
    q_turned = turn(q)
    bup, bdown = exchange(bup, bdown)
    (g,) = call(derive_kernel, plain(kron, a_turned, ps), [((NT * ROWS, NV * CHUNK), 0)])
    c, hc, f_hot, m_hot = call(
        middle_kernel,
        scalars + [(b, SIX), (source, SIX)] + late(ps) + plain(bup, bdown) + [last_variable] + late(q4, ff, mf)
        + plain(g),
        [(FLUID, 0), ((CH, ROWS, SPAN), 0), ((SPAN, NF), 0, BF16), ((MSPAN, NF), 0, BF16)],
        scratch=[pltpu.VMEM((3, NV, ROWS, SPAN), F32)],
        flops=LONG,
    )
    v, metal, mup, mdown, e1 = call(
        second_kernel,
        scalars[:1] + plain(q_turned, g, kron, ps, metal, coeff, ff, mf, hc, f_hot, m_hot),
        [(BLOCKS, 3), (METAL, 1), ((CH, MSPAN), 1), ((CH, MSPAN), 1), (ONE, 1)],
    )
    v = turn(v)
    mup, mdown = exchange(mup, mdown)
    out, metal = call(
        last_kernel, held(v, c, e1, metal) + plain(mup, mdown, cond, mf), [(FLUID, 6), (METAL, 1)]
    )
    return out, metal.reshape(2, NH, ROWS, MSPAN)


def solution(mesh):
    return jax.shard_map(
        local,
        mesh=mesh,
        in_specs=(
            P("inst", None, "space", None),
            P("inst", None, "space", None),
            P("space", None),
            P(),
            P(),
            P(None, None, "space", None),
            P("space", None),
            P("space"),
            P("space"),
            P("space"),
        ),
        out_specs=(P("inst", None, "space", None), P(None, None, "space", None)),
        check_vma=False,
    )
```

```python
import math

import jax
import jax.numpy as jnp
import ml_dtypes
import numpy as np
from jax import lax
from jax.experimental import pallas as pl
from jax.experimental.pallas import tpu as pltpu
from jax.sharding import PartitionSpec as P

NT, NV, NH = 48, 5, 4
ROWS, SPAN, MSPAN, NF = 8, 1024, 512, 512
CHUNK = 128
CH = 2 * NH
F32, BF16 = jnp.float32, jnp.bfloat16

damping_fourth = 1.0 / 32.0
viscous_coef = 0.1
sigma_fluid = 0.5
metal_step = 0.2
sigma_metal = 0.5
heat_capacity = 0.5
flux_scale = 4.0


def tables():
    t = np.arange(NT)
    offset = t[:, None] - t[None, :]
    angle = np.where(offset == 0, 0.5, math.pi * offset / NT)
    spectral = np.where(
        offset == 0, 0.0, 0.5 * (1.0 - 2.0 * (offset % 2)) * np.cos(angle) / np.sin(angle)
    )
    phase = 2.0 * math.pi * ((np.arange(NH)[:, None] * t[None, :]) % NT) / NT
    synth = np.concatenate([np.cos(phase), -np.sin(phase)])
    w0 = synth * (flux_scale / NT)
    w1 = w0 @ spectral
    w2 = w1 @ spectral
    high = spectral.astype(np.float32).astype(ml_dtypes.bfloat16)
    low = (spectral - high.astype(np.float64)).astype(np.float32).astype(ml_dtypes.bfloat16)
    eye = np.eye(ROWS, dtype=np.float32)
    kron_high = np.kron(high.astype(np.float32), eye)
    kron_low = np.kron(low.astype(np.float32), eye)
    kron = np.concatenate([kron_high, kron_high, kron_low], axis=1).astype(ml_dtypes.bfloat16)
    flat = np.concatenate([m.T.reshape(-1) for m in (synth, w0, w1, w2)]).astype(np.float32)
    return kron, flat


KRON, FLAT = tables()
SYNTH, W0, W1, W2 = (i * NT * CH for i in range(4))


class Loaded:
    def __init__(self, source, buffer, sems, cut):
        self.buffer, self.copies = buffer, []
        for i, index in enumerate(cut):
            self.copies.append(pltpu.make_async_copy(source.at[index], buffer.at[index], sems.at[i]))
        self.waiting = set(range(len(cut)))

    def start(self, i):
        self.copies[i].start()

    def piece(self, i):
        if i in self.waiting:
            self.waiting.remove(i)
            self.copies[i].wait()
        return self.buffer

    def whole(self):
        for i in range(len(self.copies)):
            self.piece(i)
        return self.buffer

    def __getitem__(self, index):
        return self.whole()[index]


class Held:
    def __init__(self, ref):
        self.buffer = ref

    def piece(self, i):
        return self.buffer

    def whole(self):
        return self.buffer

    def put(self, index):
        pass


class Stored:
    def __init__(self, target, buffer, sems):
        self.target, self.buffer, self.sems, self.copies = target, buffer, sems, []

    def put(self, index):
        copy = pltpu.make_async_copy(
            self.buffer.at[index], self.target.at[index], self.sems.at[len(self.copies)]
        )
        copy.start()
        self.copies.append(copy)

    def finish(self):
        for copy in self.copies:
            copy.wait()


class Into:
    def __init__(self, result, cut):
        self.result, self.cut = result, cut

    def __len__(self):
        return len(self.cut)


WHOLE = (slice(None),)


def by_piece(n):
    return tuple(pl.ds(i, 1) for i in range(n))


def call(body, operands, results, scratch=(), flops=1 << 20, moved=1 << 20):
    types = [r[2] if len(r) > 2 else F32 for r in results]
    results = [r[:2] for r in results]
    space = {"idle": pltpu.HBM, "smem": pltpu.SMEM, "vmem": pltpu.VMEM, "held": pltpu.VMEM}
    modes = [mode for _, mode in operands]
    here = [isinstance(mode, str) for mode in modes]
    in_specs = [
        pl.BlockSpec(memory_space=space[m] if h else pltpu.HBM) for m, h in zip(modes, here)
    ]
    out_specs = [pl.BlockSpec(memory_space=pltpu.HBM if n else pltpu.VMEM) for _, n in results]
    buffers = []
    kinds = {mode.result: array.dtype for array, mode in operands if isinstance(mode, Into)}
    for array, mode in operands:
        if isinstance(mode, tuple):
            buffers.append(pltpu.VMEM(array.shape, array.dtype))
        if not isinstance(mode, str):
            buffers.append(pltpu.SemaphoreType.DMA((len(mode),)))
    for dims, n in results:
        if n > 0:
            buffers += [pltpu.VMEM(dims, F32), pltpu.SemaphoreType.DMA((n,))]

    def kernel(*refs):
        ins, refs = refs[: len(modes)], refs[len(modes) :]
        outs, refs = refs[: len(results)], list(refs[len(results) :])
        args, loads = [], []
        for ref, mode, h in zip(ins, modes, here):
            if h:
                args.append(Held(ref) if mode == "held" else ref)
            else:
                into = isinstance(mode, Into)
                buffer = outs[mode.result] if into else refs.pop(0)
                args.append(Loaded(ref, buffer, refs.pop(0), mode.cut if into else mode))
                loads.append(args[-1])
        for i in range(max([len(x.copies) for x in loads], default=0)):
            for x in loads:
                if i < len(x.copies):
                    x.start(i)
        stores = []
        for ref, (_, n) in zip(outs, results):
            if n > 0:
                args.append(Stored(ref, refs.pop(0), refs.pop(0)))
                stores.append(args[-1])
            else:
                args.append(ref if n else Held(ref))
        body(*args, *refs)
        for x in loads:
            x.whole()
        for x in stores:
            x.finish()

    return pl.pallas_call(
        kernel,
        out_shape=[pltpu.HBM(dims, F32) if n else jax.ShapeDtypeStruct(dims, kinds.get(k, types[k])) for k, (dims, n) in enumerate(results)],
        in_specs=in_specs,
        out_specs=out_specs,
        scratch_shapes=buffers + list(scratch),
        compiler_params=pltpu.CompilerParams(vmem_limit_bytes=24 << 20),
        cost_estimate=pl.CostEstimate(flops=flops, bytes_accessed=moved, transcendentals=0),
    )(
        *[
            a if h and m != "idle" else pltpu.with_memory_space_constraint(a, pltpu.HBM)
            for (a, m), h in zip(operands, here)
        ]
    )


def shape(*dims):
    return jax.ShapeDtypeStruct(dims, F32)


def row_index(n=SPAN):
    return lax.broadcasted_iota(jnp.int32, (ROWS, n), 0)


def split(x):
    high = x.astype(BF16)
    return high, (x - high.astype(F32)).astype(BF16)


def one_hot(index, n):
    cell = lax.broadcasted_iota(jnp.int32, (n, NF), 0)
    return jnp.where(cell == index, 1.0, 0.0).astype(BF16)


def at_faces(field, span_hot, row_hot):
    n = field.shape[-1]
    both = jnp.concatenate(split(field.reshape(CH * ROWS, n)), axis=0)
    picked = jnp.dot(both, span_hot, preferred_element_type=F32)
    picked = (picked[: CH * ROWS] + picked[CH * ROWS :]).reshape(CH, ROWS, NF)
    return jnp.sum(picked * row_hot[None], axis=1)


def onto_cells(values, span_hot, row_hot):
    spread = (values[:, None, :] * row_hot[None]).reshape(CH * ROWS, NF)
    both = jnp.concatenate(split(spread), axis=0)
    out = lax.dot_general(both, span_hot, (((1,), (1,)), ((), ())), preferred_element_type=F32)
    return (out[: CH * ROWS] + out[CH * ROWS :]).reshape(CH, ROWS, span_hot.shape[0])


def rows_of(faces_ref, bits):
    return jnp.where(row_index(NF) == (faces_ref[...] >> bits), 1.0, 0.0)


def fluid_hots(ff_ref):
    cell = ff_ref[...]
    span = one_hot(cell & (SPAN - 1), SPAN)
    rows = jnp.where(row_index(NF) == (cell >> 10), 1.0, 0.0)
    return span, rows


def metal_hots(mf_ref):
    cell = mf_ref[...]
    span = one_hot(cell & (MSPAN - 1), MSPAN)
    rows = jnp.where(row_index(NF) == (cell >> 9), 1.0, 0.0)
    return span, rows


def span_sides(a):
    n = a.shape[-1]
    lane = lax.broadcasted_iota(jnp.int32, a.shape, a.ndim - 1)
    north = jnp.where(lane == n - 1, 0.0, pltpu.roll(a, n - 1, a.ndim - 1))
    south = jnp.where(lane == 0, 0.0, pltpu.roll(a, 1, a.ndim - 1))
    return north, south


def stencil_parts(a, before, after):
    row = row_index(a.shape[-1])
    east_one = pltpu.roll(jnp.where(row == 0, after, a), 7, 0)
    east_two = pltpu.roll(jnp.where(row < 2, after, a), 6, 0)
    west_one = pltpu.roll(jnp.where(row == 7, before, a), 1, 0)
    west_two = pltpu.roll(jnp.where(row >= 6, before, a), 2, 0)
    north, south = span_sides(a)
    rest = (
        (4.0 * damping_fourth) * (east_one + west_one)
        - damping_fourth * (east_two + west_two)
        + viscous_coef * (north + south)
        - (6.0 * damping_fourth + 2.0 * viscous_coef + sigma_fluid) * a
    )
    return east_one - west_one, north - south, rest


def edge_tile(ref, tile):
    return jnp.concatenate([ref[2 * tile], ref[2 * tile + 1]], axis=1)


def halo_pair(up_ref, down_ref, t, v):
    tile, slot = (t, v) if v < 4 else (6 + t // 4, t % 4)
    before = pltpu.roll(edge_tile(up_ref, tile), (6 - 2 * slot) % 8, 0)
    after = pltpu.roll(edge_tile(down_ref, tile), (8 - 2 * slot) % 8, 0)
    return before, after


def pack_tile(blocks, tile, up_ref, down_ref):
    row = row_index()
    up = down = None
    for slot, a in enumerate(blocks):
        u = pltpu.roll(a, (2 * slot + 2) % 8, 0) if (2 * slot + 2) % 8 else a
        d = pltpu.roll(a, 2 * slot, 0) if slot else a
        mine = (row >> 1) == slot
        up = u if up is None else jnp.where(mine, u, up)
        down = d if down is None else jnp.where(mine, d, down)
    for half in range(2):
        cut = slice(half * 512, half * 512 + 512)
        up_ref[2 * tile + half] = up[:, cut]
        down_ref[2 * tile + half] = down[:, cut]


def pack_last(get, extra, up_ref, down_ref):
    pack_tile([get(t) for t in range(4)], 6, up_ref, down_ref)
    pack_tile([get(4), get(5), extra, extra], 7, up_ref, down_ref)


def prepare_kernel(a, ps, m_in, up, down, a_copy, ps_copy):
    for t in range(6):
        ref = a.piece(t)
        pack_tile([ref[t, v] for v in range(4)], t, up.buffer, down.buffer)
        for x in (up, down):
            x.put(pl.ds(2 * t, 2))
    pack_last(lambda t: a.buffer[t, NV - 1], ps.whole()[...], up.buffer, down.buffer)
    metal_edges(m_in.whole(), up.buffer.at[16], down.buffer.at[16])
    for x in (up, down):
        x.put(pl.ds(12, 5))


def energy_kernel(tab_ref, m_ref, fc_ref, ff_ref, mf_ref, after, e):
    first = lax.axis_index("inst") * 6
    m_hot, m_row = metal_hots(mf_ref)
    f_hot, f_row = fluid_hots(ff_ref)
    values = at_faces(m_ref[...], m_hot, m_row) * fc_ref[...]
    cells = onto_cells(values, f_hot, f_row)
    for t in range(6):
        e.buffer[t] = combine(tab_ref, SYNTH, first + t, cells)
        e.put(pl.ds(t, 1))


def combine(tab_ref, base, t, fields):
    total = tab_ref[base + t * CH] * fields[0]
    for ch in range(1, CH):
        if ch != NH:
            total += tab_ref[base + t * CH + ch] * fields[ch]
    return total


def convect(jx_ref, jz_ref, dx, dz, rest, u):
    out = rest
    for v in range(NV):
        out = out - (0.5 * jx_ref[u, v]) * dx[v] - (0.5 * jz_ref[u, v]) * dz[v]
    return out


def inner_steps(instances, jx_ref, jz_ref, a_ref, s_ref, ps_ref, b, q, parts):
    step = ps_ref[...]
    for at, t in enumerate(instances):
        for v in range(NV):
            a = a_ref[t, v]
            dx, dz, rest = stencil_parts(a, 0.0, 0.0)
            parts[0, v], parts[1, v], parts[2, v] = dx, dz, rest
            dx, dz, rest = stencil_parts(step * a, 0.0, 0.0)
            parts[3, v], parts[4, v], parts[5, v] = dx, dz, rest
        for i in range(8):
            cut = pl.ds(i * CHUNK, CHUNK)
            dx = [parts[0, v, :, cut] for v in range(NV)]
            dz = [parts[1, v, :, cut] for v in range(NV)]
            px = [parts[3, v, :, cut] for v in range(NV)]
            pz = [parts[4, v, :, cut] for v in range(NV)]
            for u in range(NV):
                a = a_ref[t, u, :, cut]
                space = convect(jx_ref, jz_ref, dx, dz, parts[2, u, :, cut], u)
                source = s_ref[t, u, :, cut] + space
                inner = a + ps_ref[:, cut] * source
                b.buffer[at, u, :, cut] = inner
                q.buffer[at, u, :, cut] = a + inner + convect(jx_ref, jz_ref, px, pz, parts[5, u, :, cut], u)
        b.put(pl.ds(at, 1))
        q.put(pl.ds(at, 1))


EARLY = 4


def early_kernel(jx_ref, jz_ref, a_ref, s_ref, ps_ref, b, q, blocks, parts, sems):
    copies = [
        pltpu.make_async_copy(
            a_ref.at[:, :, :, pl.ds(i * CHUNK, CHUNK)], blocks.at[i], sems.at[i]
        )
        for i in range(8)
    ]
    for copy in copies:
        copy.start()
    inner_steps(range(EARLY), jx_ref, jz_ref, a_ref, s_ref, ps_ref, b, q, parts)
    for copy in copies:
        copy.wait()


def late_kernel(jx_ref, jz_ref, a_ref, s_ref, ps_ref, after, b, q, parts):
    inner_steps(range(EARLY, 6), jx_ref, jz_ref, a_ref, s_ref, ps_ref, b, q, parts)


def edge_terms(up_ref, down_ref, half, t, v):
    tile, slot = (t, v) if v < 4 else (6 + t // 4, t % 4)
    row = row_index(512)
    up, down = up_ref[2 * tile + half], down_ref[2 * tile + half]
    one = pltpu.roll(jnp.where(row == 2 * slot, down, up), (7 - 2 * slot) % 8, 0)
    one = jnp.where((row == 0) | (row == 7), one, 0.0)
    east_two = pltpu.roll(down, (6 - 2 * slot) % 8, 0)
    west_two = pltpu.roll(up, (8 - 2 * slot) % 8, 0)
    two = jnp.where(row >= 6, east_two, jnp.where(row < 2, west_two, 0.0))
    return one, two


def first_kernel(
    tab_ref, jx_ref, jz_ref, a_ref, b0_ref, q0_ref, b1_ref, q1_ref, e_ref, ps_ref, up_ref, down_ref, fc_ref, ff_ref,
    q, b_out, bup, bdown, q4, mup, mdown,
):
    first = lax.axis_index("inst") * 6
    step = ps_ref[...]
    mup.buffer[...], mdown.buffer[...] = up_ref[16], down_ref[16]
    mup.put(slice(None))
    mdown.put(slice(None))
    q_ref, b_ref = q.buffer, b_out.buffer
    sign = jnp.where(row_index(512) == 0, 0.5, -0.5)
    step_edges = []
    for half in range(2):
        tile = 14 + half
        row = row_index(512)
        up, down = up_ref[tile], down_ref[tile]
        one = jnp.where(row == 7, pltpu.roll(down, 3, 0), pltpu.roll(up, 3, 0))
        two = jnp.where(row >= 6, pltpu.roll(down, 2, 0), pltpu.roll(up, 4, 0))
        step_edges.append((one, two))
    for t in range(6):
        for half in range(2):
            wide = pl.ds(half * 512, 512)
            here = ps_ref[:, wide]
            step_one, step_two = step_edges[half]
            edges = [edge_terms(up_ref, down_ref, half, t, v) for v in range(NV)]
            bi_ref, qi_ref = (b0_ref, q0_ref) if t < EARLY else (b1_ref, q1_ref)
            ti = t if t < EARLY else t - EARLY
            for u in range(NV):
                total = jx_ref[u, 0] * edges[0][0]
                for v in range(1, NV):
                    total += jx_ref[u, v] * edges[v][0]
                one = sign * total + (4.0 * damping_fourth) * edges[u][0]
                two = damping_fourth * edges[u][1]
                change = one - two
                if u == NV - 1:
                    change = change + e_ref[t, :, wide]
                change = here * change
                b_ref[t, u, :, wide] = bi_ref[ti, u, :, wide] + change
                value = qi_ref[ti, u, :, wide] + change + (step_one * one - step_two * two)
                for i in range(4):
                    q_ref[4 * half + i, t * NV + u] = value[:, i * CHUNK : (i + 1) * CHUNK]
                if u == NV - 1:
                    q4.buffer[t, :, wide] = value
        q.put((slice(None), pl.ds(t * NV, NV)))
        b_out.put(pl.ds(t, 1))
        pack_tile([b_ref[t, v] for v in range(4)], t, bup.buffer, bdown.buffer)
    pack_last(lambda t: b_ref[t, NV - 1], step, bup.buffer, bdown.buffer)
    q4.put(slice(None))
    bup.put(slice(None))
    bdown.put(slice(None))
    f_hot, f_row = fluid_hots(ff_ref)
    heat = []
    for ch in range(CH):
        h0 = h1 = jnp.zeros((ROWS, SPAN), F32)
        for t in range(6 if ch != NH else 0):
            at = (first + t) * CH + ch
            h0 += tab_ref[W0 + at] * b_ref[t, NV - 1]
            h1 += tab_ref[W1 + at] * a_ref[t, NV - 1]
        heat.append(h0 - step * h1)
    values = at_faces(jnp.stack(heat), f_hot, f_row) * fc_ref[...]
    for i in range(8):
        for k in range(4):
            q_ref[i, 30 + k] = values[:, k * CHUNK : (k + 1) * CHUNK]
    q.put((slice(None), pl.ds(30, 4)))


def rotate_time(kron, x):
    high, low = split(x)
    return jnp.dot(kron, jnp.concatenate([high, low, high], axis=0), preferred_element_type=F32)


def local_step(ps_ref):
    start = pl.multiple_of(lax.axis_index("inst") * CHUNK, CHUNK)
    return ps_ref[:, pl.ds(start, CHUNK)]


def turned(get):
    return jnp.concatenate(
        [
            jnp.concatenate([get(j, t, v) for j in range(8) for t in range(6)], axis=0)
            for v in range(NV)
        ],
        axis=1,
    )


def derive_kernel(kron_ref, a_ref, ps_ref, g):
    wide = jnp.concatenate([local_step(ps_ref)] * NV, axis=1)
    x = turned(lambda j, t, v: a_ref[j, t, v])
    d = rotate_time(kron_ref[...], x)
    g.buffer[...] = (d.reshape(NT, ROWS, NV * CHUNK) * wide[None]).reshape(NT * ROWS, NV * CHUNK)
    g.put(slice(None))


def middle_kernel(
    tab_ref, jx_ref, jz_ref, b_in, s_in, ps_ref, up_ref, down_ref, a_ref, q4_ref, m_ref, mup_ref, mdown_ref, cond_ref, g_ref,
    c_out, hc, m_out,
    parts,
):
    first = lax.axis_index("inst") * 6
    c_ref = c_out.buffer
    for t in range(6):
        b_ref, s_ref = b_in.piece(t), s_in.piece(t)
        for v in range(NV):
            before, after = halo_pair(up_ref, down_ref, t, v)
            dx, dz, rest = stencil_parts(b_ref[t, v], before, after)
            parts[0, v], parts[1, v], parts[2, v] = dx, dz, rest
        for i in range(8):
            cut = pl.ds(i * CHUNK, CHUNK)
            dx = [parts[0, v, :, cut] for v in range(NV)]
            dz = [parts[1, v, :, cut] for v in range(NV)]
            for u in range(NV):
                space = convect(jx_ref, jz_ref, dx, dz, parts[2, u, :, cut], u)
                c_ref[t, u, :, cut] = b_ref[t, u, :, cut] + ps_ref[:, cut] * (s_ref[t, u, :, cut] + space)
        c_out.put(pl.ds(t, 1))
    step = ps_ref[...]
    for ch in range(CH):
        h0 = h2 = h3 = jnp.zeros((ROWS, SPAN), F32)
        for t in range(6 if ch != NH else 0):
            at = (first + t) * CH + ch
            h0 += tab_ref[W0 + at] * c_ref[t, NV - 1]
            h2 += tab_ref[W1 + at] * q4_ref[t]
            h3 += tab_ref[W2 + at] * a_ref[t, NV - 1]
        hc.buffer[ch] = h0 + step * (step * h3 - h2)
    hc.put(slice(None))
    before, after = metal_sides(mup_ref, mdown_ref)
    m = metal_update(m_ref, before, after, cond_ref[...])
    for ch in range(CH):
        m_out.buffer[ch] = m[ch]


def metal_update(m, before, after, cond):
    row = row_index(MSPAN)
    out = []
    for ch in range(CH):
        a = m[ch]
        east = pltpu.roll(jnp.where(row == 0, after[ch], a), 7, 0)
        west = pltpu.roll(jnp.where(row == 7, before[ch], a), 1, 0)
        north, south = span_sides(a)
        laplace = east + west + north + south - 4.0 * a
        h = ch % NH
        turn = -heat_capacity * h * m[ch + NH] if ch < NH else heat_capacity * h * m[ch - NH]
        out.append(a + metal_step * (cond * laplace - sigma_metal * a - turn))
    return out


def metal_edges(m, up_ref, down_ref):
    up_ref[...] = jnp.concatenate([m[ch][7:8] for ch in range(CH)], axis=0)
    down_ref[...] = jnp.concatenate([m[ch][0:1] for ch in range(CH)], axis=0)


def metal_sides(up_ref, down_ref):
    before = [jnp.broadcast_to(up_ref[ch : ch + 1], (ROWS, MSPAN)) for ch in range(CH)]
    after = [jnp.broadcast_to(down_ref[ch : ch + 1], (ROWS, MSPAN)) for ch in range(CH)]
    return before, after


def heat_sum(get):
    tiles = []
    for k in range(4):
        total = get(0, k)
        for j in range(1, 8):
            total += get(j, k)
        tiles.append(total)
    return jnp.concatenate(tiles, axis=1)


def second_kernel(
    tab_ref, q_ref, g_ref, kron_ref, ps_ref, m_ref, fc_ref, ff_ref, mf_ref, hc_ref,
    v, m_out, mup, mdown, e,
):
    first = lax.axis_index("inst") * 6
    v_ref = v.buffer
    near = local_step(ps_ref)
    x = turned(lambda j, t, u: q_ref[j, t * NV + u]) - g_ref[...]

    d = rotate_time(kron_ref[...], x)
    for half in range(2):
        for j in range(4 * half, 4 * half + 4):
            for t in range(6):
                at = (j * 6 + t) * ROWS
                for u in range(NV):
                    v_ref[j, t * NV + u] = -near * d[at : at + ROWS, u * CHUNK : (u + 1) * CHUNK]
        v.put((pl.ds(half * 4, 4), pl.ds(0, 30)))
    step = ps_ref[...]
    coeff = fc_ref[...]
    m_hot, m_row = metal_hots(mf_ref)
    source = onto_cells(heat_sum(lambda j, k: q_ref[j, 30 + k]), m_hot, m_row)
    m = [m_ref[ch] + metal_step * source[ch] for ch in range(CH)]
    values = at_faces(jnp.stack(m), m_hot, m_row) * coeff
    f_hot, f_row = fluid_hots(ff_ref)
    cells = onto_cells(values, f_hot, f_row)
    for ch in range(CH):
        m_out.buffer[ch] = m[ch]
    metal_edges(m, mup.buffer, mdown.buffer)
    for result in (m_out, mup, mdown):
        result.put(slice(None))
    for t in range(6):
        e.buffer[t] = step * combine(tab_ref, SYNTH, first + t, cells)
    e.put(slice(None))
    heat = []
    for ch in range(CH):
        total = hc_ref[ch]
        for t in range(6 if ch != NH else 0):
            total += tab_ref[W0 + (first + t) * CH + ch] * e.buffer[t]
        heat.append(total)
    values = at_faces(jnp.stack(heat), f_hot, f_row) * coeff
    for i in range(8):
        for k in range(4):
            v_ref[i, 30 + k] = values[:, k * CHUNK : (k + 1) * CHUNK]
    v.put((slice(None), pl.ds(30, 4)))


def last_kernel(v, c, e, m_in, mup_ref, mdown_ref, cond_ref, mf_ref, out, m_out):
    for t in range(6):
        v_ref, c_ref, e_ref = v.piece(t), c.piece(t), e.whole()
        for i in range(8):
            cut = pl.ds(i * CHUNK, CHUNK)
            for u in range(NV):
                total = c_ref[t, u, :, cut] + v_ref[i, t * NV + u]
                if u == NV - 1:
                    total = total + e_ref[t, :, cut]
                out.buffer[t, u, :, cut] = total
        out.put(pl.ds(t, 1))
    m_hot, m_row = metal_hots(mf_ref)
    source = onto_cells(heat_sum(lambda j, k: v.buffer[j, 30 + k]), m_hot, m_row)
    before, after = metal_sides(mup_ref, mdown_ref)
    m = metal_update(m_in.whole(), before, after, cond_ref[...])
    for ch in range(CH):
        m_out.buffer[ch] = m[ch] + metal_step * source[ch]
    m_out.put(slice(None))


def exchange(up, down):
    n = lax.axis_size("space")
    forward = [(i, (i + 1) % n) for i in range(n)]
    back = [(j, i) for i, j in forward]
    return lax.ppermute(up, "space", forward), lax.ppermute(down, "space", back)


def turn(x):
    return lax.all_to_all(x, "inst", 0, 0, tiled=True)


SIX = by_piece(6)
EDGES = (17, ROWS, 512)
FLUID = (6, NV, ROWS, SPAN)
METAL = (CH, ROWS, MSPAN)
ONE = (6, ROWS, SPAN)
BLOCKS = (8, 34, ROWS, CHUNK)


LONG = 1 << 36


def plain(*arrays):
    return [(array, "vmem") for array in arrays]


def late(*arrays):
    return [(array, WHOLE) for array in arrays]


def held(*arrays):
    return [(array, "held") for array in arrays]


def local(a0, source, ps, jx, jz, metal, cond, coeff, ff, mf):
    kron = jnp.asarray(KRON)
    tab = jnp.asarray(FLAT)
    coeff, ff, mf = (x.reshape(1, NF) for x in (coeff, ff, mf))
    metal = metal.reshape(METAL)
    up, down, a_here, ps_here = call(
        prepare_kernel,
        [(a0, Into(2, SIX)), (ps, Into(3, WHOLE))] + late(metal),
        [(EDGES, 7), (EDGES, 7), (FLUID, 0), ((ROWS, SPAN), 0)],
    )
    up, down = exchange(up, down)
    scalars = [(tab, "smem"), (jx, "smem"), (jz, "smem")]
    last_variable = (a0, ((slice(None), pl.ds(NV - 1, 1)),))
    parts = pltpu.VMEM((6, NV, ROWS, SPAN), F32)
    b, q, blocks = call(
        early_kernel,
        scalars[1:] + plain(a_here, source, ps_here),
        [((EARLY,) + FLUID[1:], EARLY), ((EARLY,) + FLUID[1:], EARLY), ((8, 6, NV, ROWS, CHUNK), -1)],
        scratch=[parts, pltpu.SemaphoreType.DMA((8,))],
    )
    (e0,) = call(
        energy_kernel,
        scalars[:1] + plain(metal, coeff, ff, mf) + [(blocks, "idle")],
        [(ONE, 0)],
        flops=LONG,
    )
    b_late, q_late = call(
        late_kernel,
        scalars[1:] + plain(a0, source, ps) + [(blocks, "idle")],
        [((6 - EARLY,) + FLUID[1:], 0)] * 2,
        scratch=[parts],
        flops=LONG,
    )
    a_turned = turn(blocks)
    q, b, bup, bdown, q4, mup, mdown = call(
        first_kernel,
        scalars + [last_variable] + plain(b, q, b_late, q_late, e0, ps, up, down, coeff, ff),
        [(BLOCKS, 7), (FLUID, 6), (EDGES, 1), (EDGES, 1), (ONE, 1), ((CH, MSPAN), 1), ((CH, MSPAN), 1)],
    )
    q_turned = turn(q)
    bup, bdown = exchange(bup, bdown)
    (g,) = call(derive_kernel, plain(kron, a_turned, ps), [((NT * ROWS, NV * CHUNK), 0)])
    c, hc, metal = call(
        middle_kernel,
        scalars + [(b, SIX), (source, SIX)] + late(ps) + plain(bup, bdown) + [last_variable] + late(q4, metal, mup, mdown, cond)
        + plain(g),
        [(FLUID, 0), ((CH, ROWS, SPAN), 0), (METAL, 0)],
        scratch=[pltpu.VMEM((3, NV, ROWS, SPAN), F32)],
        flops=LONG,
    )
    v, metal, mup, mdown, e1 = call(
        second_kernel,
        scalars[:1] + plain(q_turned, g, kron, ps, metal, coeff, ff, mf, hc),
        [(BLOCKS, 3), (METAL, 1), ((CH, MSPAN), 1), ((CH, MSPAN), 1), (ONE, 1)],
    )
    v = turn(v)
    mup, mdown = exchange(mup, mdown)
    out, metal = call(
        last_kernel, held(v, c, e1, metal) + plain(mup, mdown, cond, mf), [(FLUID, 6), (METAL, 1)]
    )
    return out, metal.reshape(2, NH, ROWS, MSPAN)


def solution(mesh):
    return jax.shard_map(
        local,
        mesh=mesh,
        in_specs=(
            P("inst", None, "space", None),
            P("inst", None, "space", None),
            P("space", None),
            P(),
            P(),
            P(None, None, "space", None),
            P("space", None),
            P("space"),
            P("space"),
            P("space"),
        ),
        out_specs=(P("inst", None, "space", None), P(None, None, "space", None)),
        check_vma=False,
    )
```

```python
import math

import jax
import jax.numpy as jnp
import ml_dtypes
import numpy as np
from jax import lax
from jax.experimental import pallas as pl
from jax.experimental.pallas import tpu as pltpu
from jax.sharding import PartitionSpec as P

NT, NV, NH = 48, 5, 4
ROWS, SPAN, MSPAN, NF = 8, 1024, 512, 512
CHUNK = 128
CH = 2 * NH
F32, BF16 = jnp.float32, jnp.bfloat16

damping_fourth = 1.0 / 32.0
viscous_coef = 0.1
sigma_fluid = 0.5
metal_step = 0.2
sigma_metal = 0.5
heat_capacity = 0.5
flux_scale = 4.0


def tables():
    t = np.arange(NT)
    offset = t[:, None] - t[None, :]
    angle = np.where(offset == 0, 0.5, math.pi * offset / NT)
    spectral = np.where(
        offset == 0, 0.0, 0.5 * (1.0 - 2.0 * (offset % 2)) * np.cos(angle) / np.sin(angle)
    )
    phase = 2.0 * math.pi * ((np.arange(NH)[:, None] * t[None, :]) % NT) / NT
    synth = np.concatenate([np.cos(phase), -np.sin(phase)])
    w0 = synth * (flux_scale / NT)
    w1 = w0 @ spectral
    w2 = w1 @ spectral
    high = spectral.astype(np.float32).astype(ml_dtypes.bfloat16)
    low = (spectral - high.astype(np.float64)).astype(np.float32).astype(ml_dtypes.bfloat16)
    eye = np.eye(ROWS, dtype=np.float32)
    kron_high = np.kron(high.astype(np.float32), eye)
    kron_low = np.kron(low.astype(np.float32), eye)
    kron = np.concatenate([kron_high, kron_high, kron_low], axis=1).astype(ml_dtypes.bfloat16)
    flat = np.concatenate([m.T.reshape(-1) for m in (synth, w0, w1, w2)]).astype(np.float32)
    return kron, flat


KRON, FLAT = tables()
SYNTH, W0, W1, W2 = (i * NT * CH for i in range(4))


class Loaded:
    def __init__(self, source, buffer, sems, cut):
        self.buffer, self.copies = buffer, []
        for i, index in enumerate(cut):
            self.copies.append(pltpu.make_async_copy(source.at[index], buffer.at[index], sems.at[i]))
        self.waiting = set(range(len(cut)))

    def start(self, i):
        self.copies[i].start()

    def piece(self, i):
        if i in self.waiting:
            self.waiting.remove(i)
            self.copies[i].wait()
        return self.buffer

    def whole(self):
        for i in range(len(self.copies)):
            self.piece(i)
        return self.buffer

    def __getitem__(self, index):
        return self.whole()[index]


class Held:
    def __init__(self, ref):
        self.buffer = ref

    def piece(self, i):
        return self.buffer

    def whole(self):
        return self.buffer

    def put(self, index):
        pass


class Stored:
    def __init__(self, target, buffer, sems):
        self.target, self.buffer, self.sems, self.copies = target, buffer, sems, []

    def put(self, index):
        copy = pltpu.make_async_copy(
            self.buffer.at[index], self.target.at[index], self.sems.at[len(self.copies)]
        )
        copy.start()
        self.copies.append(copy)

    def finish(self):
        for copy in self.copies:
            copy.wait()


class Into:
    def __init__(self, result, cut):
        self.result, self.cut = result, cut

    def __len__(self):
        return len(self.cut)


WHOLE = (slice(None),)


def by_piece(n):
    return tuple(pl.ds(i, 1) for i in range(n))


def call(body, operands, results, scratch=(), flops=1 << 20, moved=1 << 20):
    types = [r[2] if len(r) > 2 else F32 for r in results]
    results = [r[:2] for r in results]
    space = {"idle": pltpu.HBM, "smem": pltpu.SMEM, "vmem": pltpu.VMEM, "held": pltpu.VMEM}
    modes = [mode for _, mode in operands]
    here = [isinstance(mode, str) for mode in modes]
    in_specs = [
        pl.BlockSpec(memory_space=space[m] if h else pltpu.HBM) for m, h in zip(modes, here)
    ]
    out_specs = [pl.BlockSpec(memory_space=pltpu.HBM if n else pltpu.VMEM) for _, n in results]
    buffers = []
    kinds = {mode.result: array.dtype for array, mode in operands if isinstance(mode, Into)}
    for array, mode in operands:
        if isinstance(mode, tuple):
            buffers.append(pltpu.VMEM(array.shape, array.dtype))
        if not isinstance(mode, str):
            buffers.append(pltpu.SemaphoreType.DMA((len(mode),)))
    for dims, n in results:
        if n > 0:
            buffers += [pltpu.VMEM(dims, F32), pltpu.SemaphoreType.DMA((n,))]

    def kernel(*refs):
        ins, refs = refs[: len(modes)], refs[len(modes) :]
        outs, refs = refs[: len(results)], list(refs[len(results) :])
        args, loads = [], []
        for ref, mode, h in zip(ins, modes, here):
            if h:
                args.append(Held(ref) if mode == "held" else ref)
            else:
                into = isinstance(mode, Into)
                buffer = outs[mode.result] if into else refs.pop(0)
                args.append(Loaded(ref, buffer, refs.pop(0), mode.cut if into else mode))
                loads.append(args[-1])
        for i in range(max([len(x.copies) for x in loads], default=0)):
            for x in loads:
                if i < len(x.copies):
                    x.start(i)
        stores = []
        for ref, (_, n) in zip(outs, results):
            if n > 0:
                args.append(Stored(ref, refs.pop(0), refs.pop(0)))
                stores.append(args[-1])
            else:
                args.append(ref if n else Held(ref))
        body(*args, *refs)
        for x in loads:
            x.whole()
        for x in stores:
            x.finish()

    return pl.pallas_call(
        kernel,
        out_shape=[pltpu.HBM(dims, F32) if n else jax.ShapeDtypeStruct(dims, kinds.get(k, types[k])) for k, (dims, n) in enumerate(results)],
        in_specs=in_specs,
        out_specs=out_specs,
        scratch_shapes=buffers + list(scratch),
        compiler_params=pltpu.CompilerParams(vmem_limit_bytes=24 << 20),
        cost_estimate=pl.CostEstimate(flops=flops, bytes_accessed=moved, transcendentals=0),
    )(
        *[
            a if h and m != "idle" else pltpu.with_memory_space_constraint(a, pltpu.HBM)
            for (a, m), h in zip(operands, here)
        ]
    )


def shape(*dims):
    return jax.ShapeDtypeStruct(dims, F32)


def row_index(n=SPAN):
    return lax.broadcasted_iota(jnp.int32, (ROWS, n), 0)


def split(x):
    high = x.astype(BF16)
    return high, (x - high.astype(F32)).astype(BF16)


def one_hot(index, n):
    cell = lax.broadcasted_iota(jnp.int32, (n, NF), 0)
    return jnp.where(cell == index, 1.0, 0.0).astype(BF16)


def at_faces(field, span_hot, row_hot):
    n = field.shape[-1]
    both = jnp.concatenate(split(field.reshape(CH * ROWS, n)), axis=0)
    picked = jnp.dot(both, span_hot, preferred_element_type=F32)
    picked = (picked[: CH * ROWS] + picked[CH * ROWS :]).reshape(CH, ROWS, NF)
    return jnp.sum(picked * row_hot[None], axis=1)


def onto_cells(values, span_hot, row_hot):
    spread = (values[:, None, :] * row_hot[None]).reshape(CH * ROWS, NF)
    both = jnp.concatenate(split(spread), axis=0)
    out = lax.dot_general(both, span_hot, (((1,), (1,)), ((), ())), preferred_element_type=F32)
    return (out[: CH * ROWS] + out[CH * ROWS :]).reshape(CH, ROWS, span_hot.shape[0])


def rows_of(faces_ref, bits):
    return jnp.where(row_index(NF) == (faces_ref[...] >> bits), 1.0, 0.0)


def fluid_hots(ff_ref):
    cell = ff_ref[...]
    span = one_hot(cell & (SPAN - 1), SPAN)
    rows = jnp.where(row_index(NF) == (cell >> 10), 1.0, 0.0)
    return span, rows


def metal_hots(mf_ref):
    cell = mf_ref[...]
    span = one_hot(cell & (MSPAN - 1), MSPAN)
    rows = jnp.where(row_index(NF) == (cell >> 9), 1.0, 0.0)
    return span, rows


def span_sides(a):
    n = a.shape[-1]
    lane = lax.broadcasted_iota(jnp.int32, a.shape, a.ndim - 1)
    north = jnp.where(lane == n - 1, 0.0, pltpu.roll(a, n - 1, a.ndim - 1))
    south = jnp.where(lane == 0, 0.0, pltpu.roll(a, 1, a.ndim - 1))
    return north, south


def stencil_parts(a, before, after):
    row = row_index(a.shape[-1])
    east_one = pltpu.roll(jnp.where(row == 0, after, a), 7, 0)
    east_two = pltpu.roll(jnp.where(row < 2, after, a), 6, 0)
    west_one = pltpu.roll(jnp.where(row == 7, before, a), 1, 0)
    west_two = pltpu.roll(jnp.where(row >= 6, before, a), 2, 0)
    north, south = span_sides(a)
    rest = (
        (4.0 * damping_fourth) * (east_one + west_one)
        - damping_fourth * (east_two + west_two)
        + viscous_coef * (north + south)
        - (6.0 * damping_fourth + 2.0 * viscous_coef + sigma_fluid) * a
    )
    return east_one - west_one, north - south, rest


def edge_tile(ref, tile):
    return jnp.concatenate([ref[2 * tile], ref[2 * tile + 1]], axis=1)


def halo_pair(up_ref, down_ref, t, v):
    tile, slot = (t, v) if v < 4 else (6 + t // 4, t % 4)
    before = pltpu.roll(edge_tile(up_ref, tile), (6 - 2 * slot) % 8, 0)
    after = pltpu.roll(edge_tile(down_ref, tile), (8 - 2 * slot) % 8, 0)
    return before, after


def pack_tile(blocks, tile, up_ref, down_ref):
    row = row_index()
    up = down = None
    for slot, a in enumerate(blocks):
        u = pltpu.roll(a, (2 * slot + 2) % 8, 0) if (2 * slot + 2) % 8 else a
        d = pltpu.roll(a, 2 * slot, 0) if slot else a
        mine = (row >> 1) == slot
        up = u if up is None else jnp.where(mine, u, up)
        down = d if down is None else jnp.where(mine, d, down)
    for half in range(2):
        cut = slice(half * 512, half * 512 + 512)
        up_ref[2 * tile + half] = up[:, cut]
        down_ref[2 * tile + half] = down[:, cut]


def pack_last(get, extra, up_ref, down_ref):
    pack_tile([get(t) for t in range(4)], 6, up_ref, down_ref)
    pack_tile([get(4), get(5), extra, extra], 7, up_ref, down_ref)


def prepare_kernel(a, ps, m_in, up, down, a_copy, ps_copy):
    for t in range(6):
        ref = a.piece(t)
        pack_tile([ref[t, v] for v in range(4)], t, up.buffer, down.buffer)
        for x in (up, down):
            x.put(pl.ds(2 * t, 2))
    pack_last(lambda t: a.buffer[t, NV - 1], ps.whole()[...], up.buffer, down.buffer)
    metal_edges(m_in.whole(), up.buffer.at[16], down.buffer.at[16])
    for x in (up, down):
        x.put(pl.ds(12, 5))


def energy_kernel(tab_ref, m_ref, fc_ref, ff_ref, mf_ref, after, e):
    first = lax.axis_index("inst") * 6
    m_hot, m_row = metal_hots(mf_ref)
    f_hot, f_row = fluid_hots(ff_ref)
    values = at_faces(m_ref[...], m_hot, m_row) * fc_ref[...]
    cells = onto_cells(values, f_hot, f_row)
    for t in range(6):
        e.buffer[t] = combine(tab_ref, SYNTH, first + t, cells)
        e.put(pl.ds(t, 1))


def combine(tab_ref, base, t, fields):
    total = tab_ref[base + t * CH] * fields[0]
    for ch in range(1, CH):
        if ch != NH:
            total += tab_ref[base + t * CH + ch] * fields[ch]
    return total


def convect(jx_ref, jz_ref, dx, dz, rest, u):
    out = rest
    for v in range(NV):
        out = out - (0.5 * jx_ref[u, v]) * dx[v] - (0.5 * jz_ref[u, v]) * dz[v]
    return out


def inner_steps(instances, jx_ref, jz_ref, a_ref, s_ref, ps_ref, b, q, parts):
    step = ps_ref[...]
    for at, t in enumerate(instances):
        for v in range(NV):
            a = a_ref[t, v]
            dx, dz, rest = stencil_parts(a, 0.0, 0.0)
            parts[0, v], parts[1, v], parts[2, v] = dx, dz, rest
            dx, dz, rest = stencil_parts(step * a, 0.0, 0.0)
            parts[3, v], parts[4, v], parts[5, v] = dx, dz, rest
        for i in range(8):
            cut = pl.ds(i * CHUNK, CHUNK)
            dx = [parts[0, v, :, cut] for v in range(NV)]
            dz = [parts[1, v, :, cut] for v in range(NV)]
            px = [parts[3, v, :, cut] for v in range(NV)]
            pz = [parts[4, v, :, cut] for v in range(NV)]
            for u in range(NV):
                a = a_ref[t, u, :, cut]
                space = convect(jx_ref, jz_ref, dx, dz, parts[2, u, :, cut], u)
                source = s_ref[t, u, :, cut] + space
                inner = a + ps_ref[:, cut] * source
                b.buffer[at, u, :, cut] = inner
                q.buffer[at, u, :, cut] = a + inner + convect(jx_ref, jz_ref, px, pz, parts[5, u, :, cut], u)
        b.put(pl.ds(at, 1))
        q.put(pl.ds(at, 1))


EARLY = 3


def early_kernel(jx_ref, jz_ref, a_ref, s_ref, ps_ref, b, q, blocks, parts, sems):
    copies = [
        pltpu.make_async_copy(
            a_ref.at[:, :, :, pl.ds(i * CHUNK, CHUNK)], blocks.at[i], sems.at[i]
        )
        for i in range(8)
    ]
    for copy in copies:
        copy.start()
    inner_steps(range(EARLY), jx_ref, jz_ref, a_ref, s_ref, ps_ref, b, q, parts)
    for copy in copies:
        copy.wait()


def late_kernel(jx_ref, jz_ref, a_ref, s_ref, ps_ref, after, b, q, parts):
    inner_steps(range(EARLY, 6), jx_ref, jz_ref, a_ref, s_ref, ps_ref, b, q, parts)


def edge_terms(up_ref, down_ref, half, t, v):
    tile, slot = (t, v) if v < 4 else (6 + t // 4, t % 4)
    row = row_index(512)
    up, down = up_ref[2 * tile + half], down_ref[2 * tile + half]
    one = pltpu.roll(jnp.where(row == 2 * slot, down, up), (7 - 2 * slot) % 8, 0)
    one = jnp.where((row == 0) | (row == 7), one, 0.0)
    east_two = pltpu.roll(down, (6 - 2 * slot) % 8, 0)
    west_two = pltpu.roll(up, (8 - 2 * slot) % 8, 0)
    two = jnp.where(row >= 6, east_two, jnp.where(row < 2, west_two, 0.0))
    return one, two


def first_kernel(
    tab_ref, jx_ref, jz_ref, a_ref, b0_ref, q0_ref, b1_ref, q1_ref, e_ref, ps_ref, up_ref, down_ref, fc_ref, ff_ref,
    q, b_out, bup, bdown, q4, mup, mdown,
):
    first = lax.axis_index("inst") * 6
    step = ps_ref[...]
    mup.buffer[...], mdown.buffer[...] = up_ref[16], down_ref[16]
    mup.put(slice(None))
    mdown.put(slice(None))
    q_ref, b_ref = q.buffer, b_out.buffer
    sign = jnp.where(row_index(512) == 0, 0.5, -0.5)
    step_edges = []
    for half in range(2):
        tile = 14 + half
        row = row_index(512)
        up, down = up_ref[tile], down_ref[tile]
        one = jnp.where(row == 7, pltpu.roll(down, 3, 0), pltpu.roll(up, 3, 0))
        two = jnp.where(row >= 6, pltpu.roll(down, 2, 0), pltpu.roll(up, 4, 0))
        step_edges.append((one, two))
    for t in range(6):
        for half in range(2):
            wide = pl.ds(half * 512, 512)
            here = ps_ref[:, wide]
            step_one, step_two = step_edges[half]
            edges = [edge_terms(up_ref, down_ref, half, t, v) for v in range(NV)]
            bi_ref, qi_ref = (b0_ref, q0_ref) if t < EARLY else (b1_ref, q1_ref)
            ti = t if t < EARLY else t - EARLY
            for u in range(NV):
                total = jx_ref[u, 0] * edges[0][0]
                for v in range(1, NV):
                    total += jx_ref[u, v] * edges[v][0]
                one = sign * total + (4.0 * damping_fourth) * edges[u][0]
                two = damping_fourth * edges[u][1]
                change = one - two
                if u == NV - 1:
                    change = change + e_ref[t, :, wide]
                change = here * change
                b_ref[t, u, :, wide] = bi_ref[ti, u, :, wide] + change
                value = qi_ref[ti, u, :, wide] + change + (step_one * one - step_two * two)
                for i in range(4):
                    q_ref[4 * half + i, t * NV + u] = value[:, i * CHUNK : (i + 1) * CHUNK]
                if u == NV - 1:
                    q4.buffer[t, :, wide] = value
        q.put((slice(None), pl.ds(t * NV, NV)))
        b_out.put(pl.ds(t, 1))
        pack_tile([b_ref[t, v] for v in range(4)], t, bup.buffer, bdown.buffer)
    pack_last(lambda t: b_ref[t, NV - 1], step, bup.buffer, bdown.buffer)
    q4.put(slice(None))
    bup.put(slice(None))
    bdown.put(slice(None))
    f_hot, f_row = fluid_hots(ff_ref)
    heat = []
    for ch in range(CH):
        h0 = h1 = jnp.zeros((ROWS, SPAN), F32)
        for t in range(6 if ch != NH else 0):
            at = (first + t) * CH + ch
            h0 += tab_ref[W0 + at] * b_ref[t, NV - 1]
            h1 += tab_ref[W1 + at] * a_ref[t, NV - 1]
        heat.append(h0 - step * h1)
    values = at_faces(jnp.stack(heat), f_hot, f_row) * fc_ref[...]
    for i in range(8):
        for k in range(4):
            q_ref[i, 30 + k] = values[:, k * CHUNK : (k + 1) * CHUNK]
    q.put((slice(None), pl.ds(30, 4)))


def rotate_time(kron, x):
    high, low = split(x)
    return jnp.dot(kron, jnp.concatenate([high, low, high], axis=0), preferred_element_type=F32)


def local_step(ps_ref):
    start = pl.multiple_of(lax.axis_index("inst") * CHUNK, CHUNK)
    return ps_ref[:, pl.ds(start, CHUNK)]


def turned(get):
    return jnp.concatenate(
        [
            jnp.concatenate([get(j, t, v) for j in range(8) for t in range(6)], axis=0)
            for v in range(NV)
        ],
        axis=1,
    )


def derive_kernel(kron_ref, a_ref, ps_ref, g):
    wide = jnp.concatenate([local_step(ps_ref)] * NV, axis=1)
    x = turned(lambda j, t, v: a_ref[j, t, v])
    d = rotate_time(kron_ref[...], x)
    g.buffer[...] = (d.reshape(NT, ROWS, NV * CHUNK) * wide[None]).reshape(NT * ROWS, NV * CHUNK)
    g.put(slice(None))


def middle_kernel(
    tab_ref, jx_ref, jz_ref, b_in, s_in, ps_ref, up_ref, down_ref, a_ref, q4_ref, m_ref, mup_ref, mdown_ref, cond_ref, g_ref,
    c_out, hc, m_out,
    parts,
):
    first = lax.axis_index("inst") * 6
    c_ref = c_out.buffer
    for t in range(6):
        b_ref, s_ref = b_in.piece(t), s_in.piece(t)
        for v in range(NV):
            before, after = halo_pair(up_ref, down_ref, t, v)
            dx, dz, rest = stencil_parts(b_ref[t, v], before, after)
            parts[0, v], parts[1, v], parts[2, v] = dx, dz, rest
        for i in range(8):
            cut = pl.ds(i * CHUNK, CHUNK)
            dx = [parts[0, v, :, cut] for v in range(NV)]
            dz = [parts[1, v, :, cut] for v in range(NV)]
            for u in range(NV):
                space = convect(jx_ref, jz_ref, dx, dz, parts[2, u, :, cut], u)
                c_ref[t, u, :, cut] = b_ref[t, u, :, cut] + ps_ref[:, cut] * (s_ref[t, u, :, cut] + space)
        c_out.put(pl.ds(t, 1))
    step = ps_ref[...]
    for ch in range(CH):
        h0 = h2 = h3 = jnp.zeros((ROWS, SPAN), F32)
        for t in range(6 if ch != NH else 0):
            at = (first + t) * CH + ch
            h0 += tab_ref[W0 + at] * c_ref[t, NV - 1]
            h2 += tab_ref[W1 + at] * q4_ref[t]
            h3 += tab_ref[W2 + at] * a_ref[t, NV - 1]
        hc.buffer[ch] = h0 + step * (step * h3 - h2)
    hc.put(slice(None))
    before, after = metal_sides(mup_ref, mdown_ref)
    m = metal_update(m_ref, before, after, cond_ref[...])
    for ch in range(CH):
        m_out.buffer[ch] = m[ch]


def metal_update(m, before, after, cond):
    row = row_index(MSPAN)
    out = []
    for ch in range(CH):
        a = m[ch]
        east = pltpu.roll(jnp.where(row == 0, after[ch], a), 7, 0)
        west = pltpu.roll(jnp.where(row == 7, before[ch], a), 1, 0)
        north, south = span_sides(a)
        laplace = east + west + north + south - 4.0 * a
        h = ch % NH
        turn = -heat_capacity * h * m[ch + NH] if ch < NH else heat_capacity * h * m[ch - NH]
        out.append(a + metal_step * (cond * laplace - sigma_metal * a - turn))
    return out


def metal_edges(m, up_ref, down_ref):
    up_ref[...] = jnp.concatenate([m[ch][7:8] for ch in range(CH)], axis=0)
    down_ref[...] = jnp.concatenate([m[ch][0:1] for ch in range(CH)], axis=0)


def metal_sides(up_ref, down_ref):
    before = [jnp.broadcast_to(up_ref[ch : ch + 1], (ROWS, MSPAN)) for ch in range(CH)]
    after = [jnp.broadcast_to(down_ref[ch : ch + 1], (ROWS, MSPAN)) for ch in range(CH)]
    return before, after


def heat_sum(get):
    tiles = []
    for k in range(4):
        total = get(0, k)
        for j in range(1, 8):
            total += get(j, k)
        tiles.append(total)
    return jnp.concatenate(tiles, axis=1)


def second_kernel(
    tab_ref, q_ref, g_ref, kron_ref, ps_ref, m_ref, fc_ref, ff_ref, mf_ref, hc_ref,
    v, m_out, mup, mdown, e,
):
    first = lax.axis_index("inst") * 6
    v_ref = v.buffer
    near = local_step(ps_ref)
    x = turned(lambda j, t, u: q_ref[j, t * NV + u]) - g_ref[...]

    d = rotate_time(kron_ref[...], x)
    for half in range(2):
        for j in range(4 * half, 4 * half + 4):
            for t in range(6):
                at = (j * 6 + t) * ROWS
                for u in range(NV):
                    v_ref[j, t * NV + u] = -near * d[at : at + ROWS, u * CHUNK : (u + 1) * CHUNK]
        v.put((pl.ds(half * 4, 4), pl.ds(0, 30)))
    step = ps_ref[...]
    coeff = fc_ref[...]
    m_hot, m_row = metal_hots(mf_ref)
    source = onto_cells(heat_sum(lambda j, k: q_ref[j, 30 + k]), m_hot, m_row)
    m = [m_ref[ch] + metal_step * source[ch] for ch in range(CH)]
    values = at_faces(jnp.stack(m), m_hot, m_row) * coeff
    f_hot, f_row = fluid_hots(ff_ref)
    cells = onto_cells(values, f_hot, f_row)
    for ch in range(CH):
        m_out.buffer[ch] = m[ch]
    metal_edges(m, mup.buffer, mdown.buffer)
    for result in (m_out, mup, mdown):
        result.put(slice(None))
    for t in range(6):
        e.buffer[t] = step * combine(tab_ref, SYNTH, first + t, cells)
    e.put(slice(None))
    heat = []
    for ch in range(CH):
        total = hc_ref[ch]
        for t in range(6 if ch != NH else 0):
            total += tab_ref[W0 + (first + t) * CH + ch] * e.buffer[t]
        heat.append(total)
    values = at_faces(jnp.stack(heat), f_hot, f_row) * coeff
    for i in range(8):
        for k in range(4):
            v_ref[i, 30 + k] = values[:, k * CHUNK : (k + 1) * CHUNK]
    v.put((slice(None), pl.ds(30, 4)))


def last_kernel(v, c, e, m_in, mup_ref, mdown_ref, cond_ref, mf_ref, out, m_out):
    for t in range(6):
        v_ref, c_ref, e_ref = v.piece(t), c.piece(t), e.whole()
        for i in range(8):
            cut = pl.ds(i * CHUNK, CHUNK)
            for u in range(NV):
                total = c_ref[t, u, :, cut] + v_ref[i, t * NV + u]
                if u == NV - 1:
                    total = total + e_ref[t, :, cut]
                out.buffer[t, u, :, cut] = total
        out.put(pl.ds(t, 1))
    m_hot, m_row = metal_hots(mf_ref)
    source = onto_cells(heat_sum(lambda j, k: v.buffer[j, 30 + k]), m_hot, m_row)
    before, after = metal_sides(mup_ref, mdown_ref)
    m = metal_update(m_in.whole(), before, after, cond_ref[...])
    for ch in range(CH):
        m_out.buffer[ch] = m[ch] + metal_step * source[ch]
    m_out.put(slice(None))


def exchange(up, down):
    n = lax.axis_size("space")
    forward = [(i, (i + 1) % n) for i in range(n)]
    back = [(j, i) for i, j in forward]
    return lax.ppermute(up, "space", forward), lax.ppermute(down, "space", back)


def turn(x):
    return lax.all_to_all(x, "inst", 0, 0, tiled=True)


SIX = by_piece(6)
EDGES = (17, ROWS, 512)
FLUID = (6, NV, ROWS, SPAN)
METAL = (CH, ROWS, MSPAN)
ONE = (6, ROWS, SPAN)
BLOCKS = (8, 34, ROWS, CHUNK)


LONG = 1 << 36


def plain(*arrays):
    return [(array, "vmem") for array in arrays]


def late(*arrays):
    return [(array, WHOLE) for array in arrays]


def held(*arrays):
    return [(array, "held") for array in arrays]


def local(a0, source, ps, jx, jz, metal, cond, coeff, ff, mf):
    kron = jnp.asarray(KRON)
    tab = jnp.asarray(FLAT)
    coeff, ff, mf = (x.reshape(1, NF) for x in (coeff, ff, mf))
    metal = metal.reshape(METAL)
    up, down, a_here, ps_here = call(
        prepare_kernel,
        [(a0, Into(2, SIX)), (ps, Into(3, WHOLE))] + late(metal),
        [(EDGES, 7), (EDGES, 7), (FLUID, 0), ((ROWS, SPAN), 0)],
    )
    up, down = exchange(up, down)
    scalars = [(tab, "smem"), (jx, "smem"), (jz, "smem")]
    last_variable = (a0, ((slice(None), pl.ds(NV - 1, 1)),))
    parts = pltpu.VMEM((6, NV, ROWS, SPAN), F32)
    b, q, blocks = call(
        early_kernel,
        scalars[1:] + plain(a_here, source, ps_here),
        [((EARLY,) + FLUID[1:], EARLY), ((EARLY,) + FLUID[1:], EARLY), ((8, 6, NV, ROWS, CHUNK), -1)],
        scratch=[parts, pltpu.SemaphoreType.DMA((8,))],
    )
    (e0,) = call(
        energy_kernel,
        scalars[:1] + plain(metal, coeff, ff, mf) + [(blocks, "idle")],
        [(ONE, 0)],
        flops=LONG,
    )
    b_late, q_late = call(
        late_kernel,
        scalars[1:] + plain(a0, source, ps) + [(blocks, "idle")],
        [((6 - EARLY,) + FLUID[1:], 0)] * 2,
        scratch=[parts],
        flops=LONG,
    )
    a_turned = turn(blocks)
    q, b, bup, bdown, q4, mup, mdown = call(
        first_kernel,
        scalars + [last_variable] + plain(b, q, b_late, q_late, e0, ps, up, down, coeff, ff),
        [(BLOCKS, 7), (FLUID, 6), (EDGES, 1), (EDGES, 1), (ONE, 1), ((CH, MSPAN), 1), ((CH, MSPAN), 1)],
    )
    q_turned = turn(q)
    bup, bdown = exchange(bup, bdown)
    (g,) = call(derive_kernel, plain(kron, a_turned, ps), [((NT * ROWS, NV * CHUNK), 0)])
    c, hc, metal = call(
        middle_kernel,
        scalars + [(b, SIX), (source, SIX)] + late(ps) + plain(bup, bdown) + [last_variable] + late(q4, metal, mup, mdown, cond)
        + plain(g),
        [(FLUID, 0), ((CH, ROWS, SPAN), 0), (METAL, 0)],
        scratch=[pltpu.VMEM((3, NV, ROWS, SPAN), F32)],
        flops=LONG,
    )
    v, metal, mup, mdown, e1 = call(
        second_kernel,
        scalars[:1] + plain(q_turned, g, kron, ps, metal, coeff, ff, mf, hc),
        [(BLOCKS, 3), (METAL, 1), ((CH, MSPAN), 1), ((CH, MSPAN), 1), (ONE, 1)],
    )
    v = turn(v)
    mup, mdown = exchange(mup, mdown)
    out, metal = call(
        last_kernel, held(v, c, e1, metal) + plain(mup, mdown, cond, mf), [(FLUID, 6), (METAL, 1)]
    )
    return out, metal.reshape(2, NH, ROWS, MSPAN)


def solution(mesh):
    return jax.shard_map(
        local,
        mesh=mesh,
        in_specs=(
            P("inst", None, "space", None),
            P("inst", None, "space", None),
            P("space", None),
            P(),
            P(),
            P(None, None, "space", None),
            P("space", None),
            P("space"),
            P("space"),
            P("space"),
        ),
        out_specs=(P("inst", None, "space", None), P(None, None, "space", None)),
        check_vma=False,
    )
```
